512 devices in a mesh: wide: 128 (over z, y, core), narrow: 4 (over x).
Axes of the slice: x: 4, y: 4, z: 16, core: 2. Of those that a mesh axis runs over, the one named last changes fastest.
Arguments:
- pressure_head: float32 [64, 512, 1024], P('narrow', 'wide'), may hold values from -3 to 0.5
- texture: int32 [64, 512, 1024], P('narrow', 'wide'), may hold values from 0 to 11
- saturated_table: float32 [12], replicated, may hold values from 0.1 to 1
- shape_table: float32 [12], replicated, may hold values from 0.3 to 3
- capacity_table: float32 [12], replicated, may hold values from 0.5 to 2
- uptake: float32 [32768, 64], P('wide', 'narrow'), may hold values from 0.02 to 0.5
- root_tile: int32 [32768, 1], P('wide'), may hold values from 0 to 127; in each aligned block of 256 rows (0 to 255, 256 to 511, ...) at most 4 rows name the same one
- root_column: int32 [32768], P('wide'), may hold values from 0 to 4095
- aquifer_head: float32 [3, 512, 1024], P(None, 'wide'), may hold values from -4 to 4
- transmissivity: float32 [3, 512, 1024], P(None, 'wide'), may hold values from 0.5 to 5
Outputs:
- head_next: float32 [64, 512, 1024], P('narrow', 'wide')
- aquifer_next: float32 [3, 512, 1024], P(None, 'wide', 'narrow')
The draws below stay inside these ranges and needn't reach their ends.
Inputs may be any that keep to these rules, and one draw needn't show every extreme that they name: `root_tile`: within each aligned block of 256 rows no tile is named more than 4 times, a bound that some block reaches.
All inputs are finite; a program needn't handle non-finite values.
Results may differ from the reference program's by a relative error of at most 0.0003.
Values sent between devices are 32-bit elements; how exact they have to be, the bound alone decides.
A program may use at most 128 MiB of HBM per device.

```python
import math
import jax
import jax.numpy as jnp
import numpy as np
from jax import lax

CX = 4
NY = 1024
ROOTS_DEV = 256
CLASSES = 12
AQ_LAYERS = 3
SWEEPS = 8
NX = 512
NZ = 64
ROOTS = 32768
CAP = 4
N_WIDE = 128


def draw_aquifer_head(key, part):
    key = jax.random.fold_in(key, 11)
    return jnp.clip(jax.random.normal(key, (AQ_LAYERS, NX, NY), jnp.float32), -4.0, 4.0)


def place_ends(values, stream_key, smallest, high):
    longest = values.shape.index(max(values.shape))
    spots = []
    for shift in (0, 1):
        where = [jax.random.randint(jax.random.fold_in(stream_key, axis), (), 0, length) for axis, length in enumerate(values.shape)]
        where[longest] = (where[longest] + shift) % values.shape[longest]
        spots.append(tuple(where))
    return values.at[spots[0]].set(smallest).at[spots[1]].set(high)


def levels(rng, dims, cuts, low, largest):
    def one(dim, parts):
        draws = jax.random.uniform(jax.random.fold_in(jax.random.fold_in(rng, 6), dim), (parts,), jnp.float32, low / len(cuts), largest / len(cuts))
        return jnp.repeat(jnp.exp(draws), dims[dim] // parts).reshape((-1,) + (1,) * (len(dims) - dim - 1))

    loudness = one(*cuts[0])
    for cut in cuts[1:]:
        loudness = loudness * one(*cut)
    return loudness


def deal_out(stream_key, own, number, rows, amount, top, reach, lean):
    ranking = jax.random.permutation(stream_key, amount)
    packed, usual = shares(amount, rows * top, reach, lean, True), shares(amount, rows * top, reach, lean, False)
    places = jnp.arange(amount)

    def named(lengths, turn):
        used = int((lengths > 0).sum())
        fixed = max(1, used // 4)
        shifted = fixed + (places - fixed + turn * (used - fixed)) % max(1, amount - fixed)
        return jnp.zeros((amount,), jnp.int32).at[ranking[jnp.where(places < fixed, places, shifted)]].set(jnp.asarray(lengths, jnp.int32))

    lengths = jnp.where(number % 4 == 0, named(packed, number // 4), named(usual, number - number // 4 - 1))
    mixed = jax.random.permutation(jax.random.fold_in(own, 3), amount)
    giver, receiver = mixed[0:amount // 2 * 2:2], mixed[1:amount // 2 * 2:2]
    margin = jnp.minimum(lengths[giver] - 1, reach - lengths[receiver]) // 2
    margin = jnp.where((giver == ranking[0]) | (receiver == ranking[0]) | (lengths[receiver] == 0), 0, jnp.maximum(margin, 0))
    shifted = jax.random.randint(jax.random.fold_in(own, 4), (amount // 2,), 0, 1 << 20) % (margin + 1)
    lengths = lengths.at[giver].add(-shifted).at[receiver].add(shifted)
    items = jnp.searchsorted(jnp.cumsum(lengths), jnp.arange(rows * top), side="right").astype(jnp.int32)
    listing = items.reshape(top, rows).T
    listing = listing[jax.random.permutation(jax.random.fold_in(own, 1), rows)]
    turn = jax.random.randint(jax.random.fold_in(own, 2), (rows, 1), 0, top)
    return jnp.take_along_axis(listing, (jnp.arange(top)[None, :] + turn) % top, axis=1)


def shares(amount, total, limit, skew, full):
    loads = [(1 << 20) // math.isqrt(grade ** skew) + 1 for grade in range(1, amount + 1)]
    largest = limit if full else min(limit, max(-(-total // amount), total * loads[0] // sum(loads)))
    least = 1 if total - largest >= amount - 1 else 0
    given, rest = [largest] + [least] * (amount - 1), total - largest - least * (amount - 1)
    while rest > 0:
        free = [i for i in range(1, amount) if given[i] < largest] or [i for i in range(1, amount) if given[i] < limit]
        mass, budget = sum([loads[i] for i in free]), rest
        for i in free:
            addition = min(limit - given[i], max(1, budget * loads[i] // mass), rest)
            given[i] = given[i] + addition
            rest = rest - addition
    return np.array(given)


def setup_inputs(seed: int = 0) -> dict:
    keys = jax.random.split(jax.random.key(seed), 11)
    pressure_head = jnp.clip(-3.0 + 3.5 * jax.random.uniform(keys[0], (NZ, NX, NY), jnp.float32) ** levels(keys[0], (NZ, NX, NY), ((0, 4), (1, 128)), -0.2, 0.2), -3.0, 0.5)
    texture = place_ends(jax.random.randint(keys[1], (NZ, NX, NY), 0, CLASSES), jax.random.fold_in(keys[1], 1), 0, CLASSES - 1).astype(jnp.int32)
    saturated_table = jnp.clip(jnp.exp(jax.random.uniform(keys[2], (CLASSES,), jnp.float32, math.log(0.1), math.log(1.0))), 0.1, 1.0)
    shape_table = jnp.clip(jnp.exp(jax.random.uniform(keys[3], (CLASSES,), jnp.float32, math.log(0.3), math.log(3.0))), 0.3, 3.0)
    capacity_table = jnp.clip(jnp.exp(jax.random.uniform(keys[4], (CLASSES,), jnp.float32, math.log(0.5), math.log(2.0))), 0.5, 2.0)
    uptake = jnp.clip(jnp.exp(math.log(0.5) - 3.218876 * jax.random.uniform(keys[5], (ROOTS, NZ), jnp.float32) ** levels(keys[5], (ROOTS, NZ), ((0, 128), (1, 4)), -0.2, 0.2)), 0.02, 0.5)
    root_tile_keys = jax.random.split(jax.random.fold_in(keys[6], 1), ROOTS // ROOTS_DEV)
    root_tile_turns = jax.random.permutation(jax.random.fold_in(keys[6], 3), ROOTS // ROOTS_DEV)
    root_tile = jax.vmap(lambda own, number: deal_out(jax.random.fold_in(keys[6], 2), own, number, ROOTS_DEV, N_WIDE, 1, CAP, 2))(root_tile_keys, root_tile_turns).reshape((ROOTS, 1))
    root_column = place_ends(jax.random.randint(keys[7], (ROOTS,), 0, CX * NY), jax.random.fold_in(keys[7], 1), 0, (CX * NY) - 1).astype(jnp.int32)
    aquifer_head = draw_aquifer_head(jax.random.fold_in(keys[10], 71), 0)
    transmissivity = jnp.clip(jnp.exp(math.log(5.0) - 2.3025851 * jax.random.uniform(keys[9], (AQ_LAYERS, NX, NY), jnp.float32) ** levels(keys[9], (AQ_LAYERS, NX, NY), ((1, 128),), -0.2, 0.2)), 0.5, 5.0)
    return dict(pressure_head=pressure_head, texture=texture, saturated_table=saturated_table, shape_table=shape_table, capacity_table=capacity_table, uptake=uptake, root_tile=root_tile, root_column=root_column, aquifer_head=aquifer_head, transmissivity=transmissivity)


TIME_STEP = 0.25
STORAGE = 0.05
LEAKANCE = 0.5


def texture_values(texture, saturated_table, shape_table, capacity_table):
    tables = (saturated_table, shape_table, capacity_table)
    zero_field = jnp.zeros(texture.shape, saturated_table.dtype)

    def pick(class_index, carried):
        matched = texture == class_index
        return tuple(jnp.where(matched, table[class_index], current) for table, current in zip(tables, carried))

    return lax.fori_loop(0, saturated_table.shape[0], pick, (zero_field, zero_field, zero_field))


def relax(heads, fixed):
    previous = fixed[0:3, 1:-1, 1:-1]
    transmit = fixed[3:6]
    recharge = fixed[6, 1:-1, 1:-1]
    inside = fixed[7, 1:-1, 1:-1]
    centre_trans = transmit[:, 1:-1, 1:-1]
    north_face = 0.5 * (centre_trans + transmit[:, :-2, 1:-1])
    south_face = 0.5 * (centre_trans + transmit[:, 2:, 1:-1])
    west_face = 0.5 * (centre_trans + transmit[:, 1:-1, :-2])
    east_face = 0.5 * (centre_trans + transmit[:, 1:-1, 2:])
    inflow = north_face * heads[:, :-2, 1:-1] + south_face * heads[:, 2:, 1:-1] + west_face * heads[:, 1:-1, :-2] + east_face * heads[:, 1:-1, 2:]
    centre = heads[:, 1:-1, 1:-1]
    blank_layer = jnp.zeros_like(centre[:1])
    upward = jnp.concatenate([blank_layer, centre[:-1]], axis=0)
    downward = jnp.concatenate([centre[1:], blank_layer], axis=0)
    single = jnp.ones_like(blank_layer)
    link_count = jnp.concatenate([single, 2.0 * single, single], axis=0)
    top_source = jnp.concatenate([recharge[None], jnp.zeros_like(centre[1:])], axis=0)
    source = STORAGE * previous + inflow + LEAKANCE * (upward + downward) + top_source
    divisor = STORAGE + north_face + south_face + west_face + east_face + LEAKANCE * link_count
    return source / divisor * inside


def aquifer_sweeps(aquifer_head, transmissivity, drainage):
    fixed = jnp.concatenate([aquifer_head, transmissivity, drainage[None], jnp.ones_like(drainage)[None]], axis=0)
    fixed = jnp.pad(fixed, ((0, 0), (1, 1), (1, 1)))
    heads = aquifer_head
    for sweep_index in range(SWEEPS):
        heads = relax(jnp.pad(heads, ((0, 0), (1, 1), (1, 1))), fixed)
    return heads


def reference(pressure_head, texture, saturated_table, shape_table, capacity_table, uptake, root_tile, root_column, aquifer_head, transmissivity):
    head_pad = jnp.pad(pressure_head, ((0, 0), (1, 1), (0, 0)))
    texture_pad = jnp.pad(texture, ((0, 0), (1, 1), (0, 0)))

    def block(tile_index):
        first_row = (tile_index * CX).astype(jnp.int32)
        anchor = jnp.zeros((), jnp.int32)
        head_rows = lax.dynamic_slice(head_pad, (anchor, first_row, anchor), (NZ, CX + 2, NY))
        texture_rows = lax.dynamic_slice(texture_pad, (anchor, first_row, anchor), (NZ, CX + 2, NY))
        saturated, shape_rate, capacity = texture_values(texture_rows, saturated_table, shape_table, capacity_table)
        conduct = saturated * jnp.exp(shape_rate * jnp.minimum(head_rows, 0.0))
        heads = head_rows[:, 1:-1]
        cond_mid = conduct[:, 1:-1]
        capacity_mid = capacity[:, 1:-1]
        across = 0.5 * (conduct[:, :-1] + conduct[:, 1:]) * (head_rows[:, :-1] - head_rows[:, 1:])
        face_rows = first_row + jnp.arange(CX + 1, dtype=jnp.int32)
        open_face = (face_rows > 0) & (face_rows < NX)
        across = jnp.where(open_face[None, :, None], across, 0.0)
        along = 0.5 * (cond_mid[:, :, :-1] + cond_mid[:, :, 1:]) * (heads[:, :, :-1] - heads[:, :, 1:])
        edge_zeros = jnp.zeros_like(along[:, :, :1])
        along = jnp.concatenate([edge_zeros, along, edge_zeros], axis=2)
        aquifer_top = lax.dynamic_slice(aquifer_head[0], (first_row, anchor), (CX, NY))
        drainage = cond_mid[-1] * (heads[-1] - aquifer_top + 1.0)
        inner = 0.5 * (cond_mid[:-1] + cond_mid[1:]) * (heads[:-1] - heads[1:] + 1.0)
        vertical = jnp.concatenate([jnp.zeros_like(inner[:1]), inner, drainage[None]], axis=0)
        owned = jnp.where((root_tile[:, 0] == tile_index)[:, None], uptake, 0.0)
        uptake_sum = jnp.zeros((NZ, CX * NY), uptake.dtype).at[:, root_column].add(owned.T).reshape(NZ, CX, NY)
        balance = (vertical[:-1] - vertical[1:]) + (across[:, :-1] - across[:, 1:]) + (along[:, :, :-1] - along[:, :, 1:]) - uptake_sum
        return heads + TIME_STEP * balance / capacity_mid, drainage

    blocks, drains = lax.map(block, jnp.arange(N_WIDE, dtype=jnp.int32))
    head_next = jnp.transpose(blocks, (1, 0, 2, 3)).reshape(NZ, NX, NY)
    drainage = drains.reshape(NX, NY)
    aquifer_next = aquifer_sweeps(aquifer_head, transmissivity, drainage)
    return head_next, aquifer_next
```

```python
import functools

import jax
import jax.numpy as jnp
from jax import lax
from jax.experimental import pallas as pl
from jax.experimental.pallas import tpu as pltpu
from jax.sharding import PartitionSpec as P

SWEEPS = 8
TIME_STEP = 0.25
STORAGE = 0.05
LEAKANCE = 0.5
PEERS = 8
CAP = 4
F32, BF16, I32 = jnp.float32, jnp.bfloat16, jnp.int32
MESH = pl.DeviceIdType.MESH
NT = (((1,), (1,)), ((), ()))


def roll(x, shift, axis):
    return pltpu.roll(x, shift % x.shape[axis], axis)


def iota(shape, axis):
    return lax.broadcasted_iota(I32, shape, axis)


def send(src, dst, send_sem, recv_sem, wide, narrow):
    copy = pltpu.make_async_remote_copy(
        src_ref=src,
        dst_ref=dst,
        send_sem=send_sem,
        recv_sem=recv_sem,
        device_id=(wide, narrow),
        device_id_type=MESH,
    )
    copy.start()
    return copy


def root_slots(uptake, tile, column, order):
    place = order(tile)
    cell_row = ((column // 128) % 8) * 4 + column // 1024
    cell_lane = column % 128
    count = tile.shape[1]
    aimed = iota((128, count), 0) == place
    earlier = iota((count, count), 0) < iota((count, count), 1)
    rank = jnp.dot(
        aimed.astype(F32).astype(BF16),
        earlier.astype(F32).astype(BF16),
        preferred_element_type=F32,
    )
    picks = jnp.concatenate(
        [(aimed & (rank == float(k))).astype(F32).astype(BF16) for k in range(CAP)], axis=0
    )
    high = uptake.astype(BF16)
    low = (uptake - high.astype(F32)).astype(BF16)
    line = iota((16, count), 0)
    extra = jnp.where(
        line == 0,
        cell_row.astype(F32),
        jnp.where(line == 1, cell_lane.astype(F32), 0.0),
    ).astype(BF16)
    base = jnp.concatenate([high, extra, low, jnp.zeros_like(extra)], axis=0)
    spread = lax.dot_general(base, picks, NT, preferred_element_type=F32)
    rows = spread[:32] + spread[32:]
    slots = jnp.concatenate([rows[:, 128 * k : 128 * (k + 1)] for k in range(CAP)], axis=0)
    return slots.T


def ring_left(tiles, lane):
    moved = [roll(v, 1, 1) for v in tiles]
    return [jnp.where(lane == 0, moved[t - 1], moved[t]) for t in range(len(tiles))]


def ring_right(tiles, lane):
    moved = [roll(v, -1, 1) for v in tiles]
    return [
        jnp.where(lane == 127, moved[(t + 1) % len(tiles)], moved[t]) for t in range(len(tiles))
    ]


def kernel(
    wide_count,
    narrow_count,
    head_ref,
    texture_ref,
    saturated_ref,
    shape_ref,
    capacity_ref,
    uptake_ref,
    tile_ref,
    column_ref,
    aquifer_ref,
    trans_ref,
    out_ref,
    aquifer_out_ref,
    table,
    soil,
    rest,
    part,
    face_out,
    face_in,
    slots,
    stage_1,
    turned,
    stage_2,
    patch,
    patches,
    drain,
    drains,
    coef,
    spread,
    slot_lines,
    slots_sent,
    slots_got,
    turned_sent,
    turned_got,
    patch_sent,
    patch_got,
    drain_sent,
    drain_got,
    face_sent,
    face_got,
    slab_sent,
    slab_got,
):
    w = lax.axis_index("wide")
    n = lax.axis_index("narrow")
    depth = wide_count // PEERS
    my_z, my_peer = w // PEERS, w % PEERS
    bottom = n == narrow_count - 1
    around = (-2, -1, 1, 2)

    def wide_at(step):
        return (w + step + wide_count) % wide_count

    barrier = pltpu.get_barrier_semaphore()

    def greet(wide, narrow):
        pl.semaphore_signal(barrier, inc=1, device_id=(wide, narrow), device_id_type=MESH)

    for j in range(1, PEERS):
        greet(my_z * PEERS + (my_peer + j) % PEERS, n)
    for j in range(1, depth):
        greet(((my_z + j) % depth) * PEERS + my_peer, n)
    for step in around:
        greet(wide_at(step), n)
    greet(w, (n + 1) % narrow_count)
    greet(w, (n + narrow_count - 1) % narrow_count)

    @pl.when(jnp.logical_not(bottom))
    def _():
        for step in (-2, -1, 0, 1, 2):
            greet(wide_at(step), narrow_count - 1)

    made = root_slots(
        uptake_ref[...],
        tile_ref[...],
        column_ref[...],
        lambda tile: (tile % PEERS) * depth + tile // PEERS,
    )
    slots[...] = made.reshape(PEERS, depth, 128)

    lane4 = iota((4, 128), 1)
    for a in range(6):
        source = aquifer_ref if a < 3 else trans_ref
        first = (a % 3) * 32
        here = source[pl.ds(pl.multiple_of(first + 8 * n, 8), 8), :]
        after = source[pl.ds(pl.multiple_of(first + 8 * jnp.minimum(n + 1, 3), 8), 8), :]
        before = source[pl.ds(pl.multiple_of(first + 8 * jnp.maximum(n - 1, 0), 8), 8), :]
        after = jnp.where(n < narrow_count - 1, after[0:4], 0.0)
        before = jnp.where(n > 0, before[4:8], 0.0)
        patch[3 * a] = here[0:4]
        patch[3 * a + 1] = here[4:8]
        patch[3 * a + 2] = jnp.where(lane4 < 64, after, before)
    for a in range(18):
        patches[a, 2] = patch[a]
        patches[a, 5] = jnp.zeros((4, 128), F32)
    for t in range(3):
        drains[t, 5] = jnp.zeros((4, 128), F32)

    @pl.when(bottom)
    def _():
        pl.semaphore_wait(barrier, PEERS - 1 + depth - 1 + 6 + 5 * (narrow_count - 1))

    @pl.when(jnp.logical_not(bottom))
    def _():
        pl.semaphore_wait(barrier, PEERS - 1 + depth - 1 + 6)

    first_stage = []
    for j in range(1, PEERS):
        peer = (my_peer + j) % PEERS
        first_stage.append(
            send(
                slots.at[peer],
                stage_1.at[my_peer],
                slots_sent.at[j],
                slots_got.at[j],
                my_z * PEERS + peer,
                n,
            )
        )
    stage_1[my_peer] = slots[my_peer]

    patch_copies = []
    for i, step in enumerate(around):
        patch_copies.append(
            send(
                patch,
                patches.at[:, 2 - step],
                patch_sent.at[i],
                patch_got.at[i],
                wide_at(step),
                n,
            )
        )

    table[...] = jnp.zeros_like(table)
    table[0:1, 0:12] = saturated_ref[...]
    table[8:9, 0:12] = shape_ref[...]
    table[16:17, 0:12] = capacity_ref[...]

    def look_up(row, index):
        values = jnp.broadcast_to(table[row : row + 1, :], index.shape)
        return jnp.take_along_axis(values, index, axis=1, mode="promise_in_bounds")

    def conduct_layer(z, carry):
        here = pl.ds(pl.multiple_of(z * 32, 32), 32)
        there = pl.ds(pl.multiple_of(z * 32 + 32, 32), 32)
        head = head_ref[here, :]
        index = texture_ref[here, :]
        soil[0, there, :] = head
        soil[1, there, :] = look_up(0, index) * jnp.exp(look_up(8, index) * jnp.minimum(head, 0.0))
        rest[here, :] = TIME_STEP / look_up(16, index)
        return carry

    lax.fori_loop(0, 16, conduct_layer, 0)

    @pl.when(bottom)
    def _():
        flow = soil[1, 512:544, :] * (soil[0, 512:544, :] - aquifer_ref[0:32, :] + 1.0)
        for q in range(4):
            drain[q, 0] = flow[8 * q : 8 * q + 4]
            drain[q, 1] = flow[8 * q + 4 : 8 * q + 8]
            after = flow[8 * q + 8 : 8 * q + 12] if q < 3 else jnp.zeros((4, 128), F32)
            before = flow[8 * q - 4 : 8 * q] if q > 0 else jnp.zeros((4, 128), F32)
            drain[q, 2] = jnp.where(lane4 < 64, after, before)
        for step in (0, 1, -1, 2, -2):
            for q in range(4):
                if step == 0 and q == 3:
                    continue
                send(
                    drain.at[q],
                    drains.at[:, 2 - step],
                    drain_sent.at[step + 2, q],
                    drain_got.at[2 - step],
                    wide_at(step),
                    q,
                )
        drains[:, 2] = drain[3]

    for i, first in ((0, 35), (1, 32)):
        for v in range(2):
            face_out[i, v] = soil[v, pl.ds(first, 128, stride=4), :]
    face_copies = [
        send(
            face_out.at[i],
            face_in.at[i],
            face_sent.at[i],
            face_got.at[i],
            wide_at(1 if i == 0 else -1),
            n,
        )
        for i in range(2)
    ]
    slab_copies = [
        send(
            soil.at[:, pl.ds(512, 32)],
            soil.at[:, pl.ds(0, 32)],
            slab_sent.at[0],
            slab_got.at[0],
            w,
            (n + 1) % narrow_count,
        ),
        send(
            soil.at[:, pl.ds(32, 32)],
            soil.at[:, pl.ds(544, 32)],
            slab_sent.at[1],
            slab_got.at[1],
            w,
            (n + narrow_count - 1) % narrow_count,
        ),
    ]

    for j in range(1, PEERS):
        other = (my_peer + PEERS - j) % PEERS
        pltpu.make_async_remote_copy(
            src_ref=slots.at[other],
            dst_ref=stage_1.at[other],
            send_sem=slots_sent.at[j],
            recv_sem=slots_got.at[j],
            device_id=(w, n),
            device_id_type=MESH,
        ).wait_recv()
    for z in range(depth):
        for p in range(PEERS):
            turned[z, p : p + 1] = stage_1[p, z : z + 1]
    second_stage = []
    for j in range(1, depth):
        other = (my_z + j) % depth
        second_stage.append(
            send(
                turned.at[other],
                stage_2.at[my_z],
                turned_sent.at[j],
                turned_got.at[j],
                other * PEERS + my_peer,
                n,
            )
        )
    stage_2[my_z] = turned[my_z]

    for copy in slab_copies + face_copies:
        copy.wait_recv()

    @pl.when(n == 0)
    def _():
        soil[0, 0:32, :] = soil[0, 32:64, :]
        soil[1, 0:32, :] = -soil[1, 32:64, :]

    @pl.when(bottom)
    def _():
        soil[0, 544:576, :] = aquifer_ref[0:32, :]
        soil[1, 544:576, :] = soil[1, 512:544, :]

    row = iota((32, 128), 0)
    lane = iota((32, 128), 1)
    x = row % 4
    sub8 = iota((8, 128), 0)
    left_open = jnp.where((x == 0) & (w == 0), 0.0, 0.5)
    right_open = jnp.where(w == wide_count - 1, 0.0, 0.5)
    along_open = jnp.where((lane == 0) & (row < 4), 0.0, 0.5)

    def widened(side, v, z):
        pieces = []
        for j in range(4):
            one = face_in[side, v, pl.ds(z * 8 + 2 * j, 1), :]
            two = face_in[side, v, pl.ds(z * 8 + 2 * j + 1, 1), :]
            pieces.append(
                jnp.where(
                    sub8 < 4, jnp.broadcast_to(one, (8, 128)), jnp.broadcast_to(two, (8, 128))
                )
            )
        return jnp.concatenate(pieces, axis=0)

    def previous_column(v):
        moved = roll(v, 1, 1)
        return jnp.where(lane == 0, roll(moved, 4, 0), moved)

    def balance_layer(z, carry):
        over = pl.ds(pl.multiple_of(z * 32, 32), 32)
        here = pl.ds(pl.multiple_of(z * 32 + 32, 32), 32)
        under = pl.ds(pl.multiple_of(z * 32 + 64, 32), 32)
        head, cond = soil[0, here, :], soil[1, here, :]
        vertical_in = 0.5 * (soil[1, over, :] + cond) * (soil[0, over, :] - head + 1.0)
        vertical_out = 0.5 * (cond + soil[1, under, :]) * (head - soil[0, under, :] + 1.0)
        head_left = jnp.where(x == 0, widened(0, 0, z), roll(head, 1, 0))
        cond_left = jnp.where(x == 0, widened(0, 1, z), roll(cond, 1, 0))
        across_in = left_open * (cond_left + cond) * (head_left - head)
        last = right_open * (cond + widened(1, 1, z)) * (head - widened(1, 0, z))
        across_out = jnp.where(x == 3, last, roll(across_in, -1, 0))
        along_in = along_open * (previous_column(cond) + cond) * (previous_column(head) - head)
        moved = roll(along_in, -1, 1)
        along_out = jnp.where(lane == 127, roll(moved, -4, 0), moved)
        balance = (
            (vertical_in - vertical_out) + (across_in - across_out) + (along_in - along_out)
        )
        at = pl.ds(pl.multiple_of(z * 32, 32), 32)
        part[at, :] = head + balance * rest[at, :]
        return carry

    lax.fori_loop(0, 16, balance_layer, 0)

    for i, step in enumerate(around):
        pltpu.make_async_remote_copy(
            src_ref=patch,
            dst_ref=patches.at[:, 2 - step],
            send_sem=patch_sent.at[i],
            recv_sem=patch_got.at[i],
            device_id=(w, n),
            device_id_type=MESH,
        ).wait_recv()
    for step in (-2, -1, 0, 1, 2):

        def wait_drain(step=step):
            pltpu.make_async_remote_copy(
                src_ref=drain.at[0],
                dst_ref=drains.at[:, 2 - step],
                send_sem=drain_sent.at[step + 2, 0],
                recv_sem=drain_got.at[2 - step],
                device_id=(w, n),
                device_id_type=MESH,
            ).wait_recv()

        if step == 0:
            pl.when(jnp.logical_not(bottom))(wait_drain)
        else:
            wait_drain()

    lane24 = iota((24, 128), 1)
    line = iota((24, 128), 0) + 4 * w - 8
    inside = jnp.where((line >= 0) & (line < 4 * wide_count), 1.0, 0.0)
    after_open = jnp.where(n < narrow_count - 1, 1.0, 0.0)
    before_open = jnp.where(n > 0, 1.0, 0.0)
    inside_halo = inside * jnp.where(lane24 < 64, after_open, before_open)

    def stacked(ref, a):
        return jnp.concatenate([ref[a, s] for s in range(6)], axis=0)

    heads = [[stacked(patches, 3 * l + t) * inside for t in range(3)] for l in range(3)]
    flows = [stacked(drains, t) for t in range(3)]
    for l in range(3):
        trans = [stacked(patches, 9 + 3 * l + t) * inside for t in range(3)]
        wests, easts = ring_left(trans, lane24), ring_right(trans, lane24)
        for t in range(3):
            centre = trans[t]
            north = 0.5 * (centre + roll(centre, 1, 0))
            south = 0.5 * (centre + roll(centre, -1, 0))
            west = 0.5 * (centre + wests[t])
            east = 0.5 * (centre + easts[t])
            links = 2.0 if l == 1 else 1.0
            divisor = STORAGE + north + south + west + east + LEAKANCE * links
            inverse = (inside_halo if t == 2 else inside) / divisor
            source = STORAGE * heads[l][t]
            if l == 0:
                source = source + flows[t]
            k = 3 * l + t
            coef[0, k] = north * inverse
            coef[1, k] = south * inverse
            coef[2, k] = west * inverse
            coef[3, k] = east * inverse
            coef[4, k] = LEAKANCE * inverse
            coef[5, k] = source * inverse

    def sweep(_, flat):
        now = [flat[3 * l : 3 * l + 3] for l in range(3)]
        later = []
        for l in range(3):
            wests, easts = ring_left(now[l], lane24), ring_right(now[l], lane24)
            for t in range(3):
                k = 3 * l + t
                centre = now[l][t]
                if l == 1:
                    vertical = now[0][t] + now[2][t]
                else:
                    vertical = now[1][t]
                later.append(
                    coef[5, k]
                    + coef[0, k] * roll(centre, 1, 0)
                    + coef[1, k] * roll(centre, -1, 0)
                    + coef[2, k] * wests[t]
                    + coef[3, k] * easts[t]
                    + coef[4, k] * vertical
                )
        return tuple(later)

    flat = lax.fori_loop(0, SWEEPS, sweep, tuple(v for layer in heads for v in layer))
    for l in range(3):
        aquifer_out_ref[8 * l : 8 * l + 8, :] = jnp.concatenate(
            [flat[3 * l][8:12], flat[3 * l + 1][8:12]], axis=0
        )

    for j in range(1, depth):
        other = (my_z + depth - j) % depth
        pltpu.make_async_remote_copy(
            src_ref=turned.at[other],
            dst_ref=stage_2.at[other],
            send_sem=turned_sent.at[j],
            recv_sem=turned_got.at[j],
            device_id=(w, n),
            device_id_type=MESH,
        ).wait_recv()
    slot_lines[...] = stage_2[...].reshape(128, 128).T
    lanes = iota((128, 128), 0).astype(F32)
    rows = iota((32, 128), 0).astype(F32)
    target = jnp.concatenate(
        [
            (lanes == slot_lines[32 * k + 17 : 32 * k + 18, :]).astype(F32).astype(BF16)
            for k in range(CAP)
        ],
        axis=1,
    )
    for k in range(CAP):
        hit = rows == slot_lines[32 * k + 16 : 32 * k + 17, :]

        def place(z, carry, k=k, hit=hit):
            value = slot_lines[pl.ds(32 * k + z, 1), :]
            value = jnp.where(hit, jnp.broadcast_to(value, (32, 128)), 0.0)
            high = value.astype(BF16)
            low = (value - high.astype(F32)).astype(BF16)
            spread[pl.ds(pl.multiple_of(z * 32, 32), 32), 128 * k : 128 * k + 128] = high
            spread[pl.ds(pl.multiple_of(z * 32 + 512, 32), 32), 128 * k : 128 * k + 128] = low
            return carry

        lax.fori_loop(0, 16, place, 0)
    taken = lax.dot_general(spread[...], target, NT, preferred_element_type=F32)
    out_ref[...] = part[...] - (taken[:512] + taken[512:]) * rest[...]

    for copy in first_stage + patch_copies + face_copies + slab_copies + second_stage:
        copy.wait_send()

    @pl.when(bottom)
    def _():
        for step in (0, 1, -1, 2, -2):
            for q in range(4):
                if step == 0 and q == 3:
                    continue
                pltpu.make_async_remote_copy(
                    src_ref=drain.at[q],
                    dst_ref=drains.at[:, 2 - step],
                    send_sem=drain_sent.at[step + 2, q],
                    recv_sem=drain_got.at[2 - step],
                    device_id=(w, n),
                    device_id_type=MESH,
                ).wait_send()


def rows_of(a):
    k = a.shape[0]
    return a.reshape(k, 4, 8, 128).transpose(0, 2, 1, 3).reshape(k * 32, 128)


def grid_of(a, k, columns):
    return a.reshape(k, columns // 128, 4, 128).transpose(0, 2, 1, 3).reshape(k, 4, columns)


def body(
    pressure_head,
    texture,
    saturated_table,
    shape_table,
    capacity_table,
    uptake,
    root_tile,
    root_column,
    aquifer_head,
    transmissivity,
):
    wide_count = lax.axis_size("wide")
    narrow_count = lax.axis_size("narrow")
    depth = wide_count // PEERS
    dma = pltpu.SemaphoreType.DMA
    out, aquifer_out = pl.pallas_call(
        functools.partial(kernel, wide_count, narrow_count),
        out_shape=(
            jax.ShapeDtypeStruct((512, 128), F32),
            jax.ShapeDtypeStruct((24, 128), F32),
        ),
        in_specs=[pl.BlockSpec(memory_space=pltpu.VMEM)] * 10,
        out_specs=[pl.BlockSpec(memory_space=pltpu.VMEM)] * 2,
        scratch_shapes=[
            pltpu.VMEM((24, 128), F32),
            pltpu.VMEM((2, 576, 128), F32),
            pltpu.VMEM((512, 128), F32),
            pltpu.VMEM((512, 128), F32),
            pltpu.VMEM((2, 2, 128, 128), F32),
            pltpu.VMEM((2, 2, 128, 128), F32),
            pltpu.VMEM((PEERS, depth, 128), F32),
            pltpu.VMEM((PEERS, depth, 128), F32),
            pltpu.VMEM((depth, PEERS, 128), F32),
            pltpu.VMEM((depth, PEERS, 128), F32),
            pltpu.VMEM((18, 4, 128), F32),
            pltpu.VMEM((18, 6, 4, 128), F32),
            pltpu.VMEM((4, 3, 4, 128), F32),
            pltpu.VMEM((3, 6, 4, 128), F32),
            pltpu.VMEM((6, 9, 24, 128), F32),
            pltpu.VMEM((1024, 512), BF16),
            pltpu.VMEM((128, 128), F32),
            dma((PEERS,)),
            dma((PEERS,)),
            dma((depth,)),
            dma((depth,)),
            dma((4,)),
            dma((4,)),
            dma((5, 4)),
            dma((5,)),
            dma((2,)),
            dma((2,)),
            dma((2,)),
            dma((2,)),
        ],
        compiler_params=pltpu.CompilerParams(
            collective_id=0, has_side_effects=True, vmem_limit_bytes=32 * 1024 * 1024
        ),
        name="coupled_step",
    )(
        rows_of(pressure_head),
        rows_of(texture),
        saturated_table.reshape(1, -1),
        shape_table.reshape(1, -1),
        capacity_table.reshape(1, -1),
        uptake.T,
        root_tile.reshape(1, -1),
        root_column.reshape(1, -1),
        rows_of(aquifer_head),
        rows_of(transmissivity),
    )
    return grid_of(out, 16, 1024), grid_of(aquifer_out, 3, 256)


def solution(mesh):
    in_specs = (
        P("narrow", "wide", None),
        P("narrow", "wide", None),
        P(),
        P(),
        P(),
        P("wide", "narrow"),
        P("wide", None),
        P("wide"),
        P(None, "wide", None),
        P(None, "wide", None),
    )
    out_specs = (P("narrow", "wide", None), P(None, "wide", "narrow"))
    return jax.shard_map(body, mesh=mesh, in_specs=in_specs, out_specs=out_specs, check_vma=False)
```

```python
import functools

import jax
import jax.numpy as jnp
from jax import lax
from jax.experimental import pallas as pl
from jax.experimental.pallas import tpu as pltpu
from jax.sharding import PartitionSpec as P

SWEEPS = 8
TIME_STEP = 0.25
STORAGE = 0.05
LEAKANCE = 0.5
PEERS = 8
CAP = 4
F32, BF16, I32 = jnp.float32, jnp.bfloat16, jnp.int32
MESH = pl.DeviceIdType.MESH
NT = (((1,), (1,)), ((), ()))


def roll(x, shift, axis):
    return pltpu.roll(x, shift % x.shape[axis], axis)


def iota(shape, axis):
    return lax.broadcasted_iota(I32, shape, axis)


def send(src, dst, send_sem, recv_sem, wide, narrow):
    copy = pltpu.make_async_remote_copy(
        src_ref=src,
        dst_ref=dst,
        send_sem=send_sem,
        recv_sem=recv_sem,
        device_id=(wide, narrow),
        device_id_type=MESH,
    )
    copy.start()
    return copy


def root_slots(uptake, tile, column, order):
    place = order(tile)
    cell_row = ((column // 128) % 8) * 4 + column // 1024
    cell_lane = column % 128
    count = tile.shape[1]
    aimed = iota((128, count), 0) == place
    earlier = iota((count, count), 0) < iota((count, count), 1)
    rank = jnp.dot(
        aimed.astype(F32).astype(BF16),
        earlier.astype(F32).astype(BF16),
        preferred_element_type=F32,
    )
    picks = jnp.concatenate(
        [(aimed & (rank == float(k))).astype(F32).astype(BF16) for k in range(CAP)], axis=0
    )
    high = uptake.astype(BF16)
    low = (uptake - high.astype(F32)).astype(BF16)
    line = iota((16, count), 0)
    extra = jnp.where(
        line == 0,
        cell_row.astype(F32),
        jnp.where(line == 1, cell_lane.astype(F32), 0.0),
    ).astype(BF16)
    base = jnp.concatenate([high, extra, low, jnp.zeros_like(extra)], axis=0)
    spread = lax.dot_general(base, picks, NT, preferred_element_type=F32)
    rows = spread[:32] + spread[32:]
    slots = jnp.concatenate([rows[:, 128 * k : 128 * (k + 1)] for k in range(CAP)], axis=0)
    return slots.T


def ring_left(tiles, lane):
    moved = [roll(v, 1, 1) for v in tiles]
    return [jnp.where(lane == 0, moved[t - 1], moved[t]) for t in range(len(tiles))]


def ring_right(tiles, lane):
    moved = [roll(v, -1, 1) for v in tiles]
    return [
        jnp.where(lane == 127, moved[(t + 1) % len(tiles)], moved[t]) for t in range(len(tiles))
    ]


def kernel(
    wide_count,
    narrow_count,
    head_hbm,
    texture_hbm,
    saturated_hbm,
    shape_hbm,
    capacity_hbm,
    uptake_hbm,
    tile_hbm,
    column_hbm,
    aquifer_hbm,
    trans_hbm,
    out_ref,
    aquifer_out_ref,
    head_ref,
    texture_ref,
    saturated_ref,
    shape_ref,
    capacity_ref,
    uptake_ref,
    tile_ref,
    column_ref,
    aquifer_ref,
    trans_ref,
    table,
    soil,
    rest,
    part,
    face_out,
    face_in,
    slots,
    stage_1,
    turned,
    stage_2,
    patch,
    patches,
    drain,
    drains,
    coef,
    spread,
    slot_lines,
    load_done,
    slots_sent,
    slots_got,
    turned_sent,
    turned_got,
    patch_sent,
    patch_got,
    drain_sent,
    drain_got,
    face_sent,
    face_got,
    slab_sent,
    slab_got,
):
    w = lax.axis_index("wide")
    n = lax.axis_index("narrow")
    depth = wide_count // PEERS
    my_z, my_peer = w // PEERS, w % PEERS
    bottom = n == narrow_count - 1
    around = (-2, -1, 1, 2)

    def wide_at(step):
        return (w + step + wide_count) % wide_count

    order = (6, 7, 5, 8, 9, 0, 1, 2, 3, 4)
    held = (head_ref, texture_ref, saturated_ref, shape_ref, capacity_ref, uptake_ref, tile_ref)
    held += (column_ref, aquifer_ref, trans_ref)
    far = (head_hbm, texture_hbm, saturated_hbm, shape_hbm, capacity_hbm, uptake_hbm, tile_hbm)
    far += (column_hbm, aquifer_hbm, trans_hbm)
    loads = [pltpu.make_async_copy(far[i], held[i], load_done.at[i]) for i in range(10)]
    for i in order:
        loads[i].start()

    barrier = pltpu.get_barrier_semaphore()

    def greet(wide, narrow):
        pl.semaphore_signal(barrier, inc=1, device_id=(wide, narrow), device_id_type=MESH)

    for j in range(1, PEERS):
        greet(my_z * PEERS + (my_peer + j) % PEERS, n)
    for j in range(1, depth):
        greet(((my_z + j) % depth) * PEERS + my_peer, n)
    for step in around:
        greet(wide_at(step), n)
    greet(w, (n + 1) % narrow_count)
    greet(w, (n + narrow_count - 1) % narrow_count)

    @pl.when(jnp.logical_not(bottom))
    def _():
        for step in (-2, -1, 0, 1, 2):
            greet(wide_at(step), narrow_count - 1)

    for i in (6, 7, 5):
        loads[i].wait()

    made = root_slots(
        uptake_ref[...],
        tile_ref[...],
        column_ref[...],
        lambda tile: (tile % PEERS) * depth + tile // PEERS,
    )
    slots[...] = made.reshape(PEERS, depth, 128)

    for i in (8, 9):
        loads[i].wait()
    lane4 = iota((4, 128), 1)
    for a in range(6):
        source = aquifer_ref if a < 3 else trans_ref
        first = (a % 3) * 32
        here = source[pl.ds(pl.multiple_of(first + 8 * n, 8), 8), :]
        after = source[pl.ds(pl.multiple_of(first + 8 * jnp.minimum(n + 1, 3), 8), 8), :]
        before = source[pl.ds(pl.multiple_of(first + 8 * jnp.maximum(n - 1, 0), 8), 8), :]
        after = jnp.where(n < narrow_count - 1, after[0:4], 0.0)
        before = jnp.where(n > 0, before[4:8], 0.0)
        patch[3 * a] = here[0:4]
        patch[3 * a + 1] = here[4:8]
        patch[3 * a + 2] = jnp.where(lane4 < 64, after, before)
    for a in range(18):
        patches[a, 2] = patch[a]
        patches[a, 5] = jnp.zeros((4, 128), F32)
    for t in range(3):
        drains[t, 5] = jnp.zeros((4, 128), F32)

    @pl.when(bottom)
    def _():
        pl.semaphore_wait(barrier, PEERS - 1 + depth - 1 + 6 + 5 * (narrow_count - 1))

    @pl.when(jnp.logical_not(bottom))
    def _():
        pl.semaphore_wait(barrier, PEERS - 1 + depth - 1 + 6)

    first_stage = []
    for j in range(1, PEERS):
        peer = (my_peer + j) % PEERS
        first_stage.append(
            send(
                slots.at[peer],
                stage_1.at[my_peer],
                slots_sent.at[j],
                slots_got.at[j],
                my_z * PEERS + peer,
                n,
            )
        )
    stage_1[my_peer] = slots[my_peer]

    patch_copies = []
    for i, step in enumerate(around):
        patch_copies.append(
            send(
                patch,
                patches.at[:, 2 - step],
                patch_sent.at[i],
                patch_got.at[i],
                wide_at(step),
                n,
            )
        )

    for i in (0, 1, 2, 3, 4):
        loads[i].wait()
    table[...] = jnp.zeros_like(table)
    table[0:1, 0:12] = saturated_ref[...]
    table[8:9, 0:12] = shape_ref[...]
    table[16:17, 0:12] = capacity_ref[...]

    def look_up(row, index):
        values = jnp.broadcast_to(table[row : row + 1, :], index.shape)
        return jnp.take_along_axis(values, index, axis=1, mode="promise_in_bounds")

    def conduct_layer(z, carry):
        here = pl.ds(pl.multiple_of(z * 32, 32), 32)
        there = pl.ds(pl.multiple_of(z * 32 + 32, 32), 32)
        head = head_ref[here, :]
        index = texture_ref[here, :]
        soil[0, there, :] = head
        soil[1, there, :] = look_up(0, index) * jnp.exp(look_up(8, index) * jnp.minimum(head, 0.0))
        rest[here, :] = TIME_STEP / look_up(16, index)
        return carry

    lax.fori_loop(0, 16, conduct_layer, 0)

    @pl.when(bottom)
    def _():
        flow = soil[1, 512:544, :] * (soil[0, 512:544, :] - aquifer_ref[0:32, :] + 1.0)
        for q in range(4):
            drain[q, 0] = flow[8 * q : 8 * q + 4]
            drain[q, 1] = flow[8 * q + 4 : 8 * q + 8]
            after = flow[8 * q + 8 : 8 * q + 12] if q < 3 else jnp.zeros((4, 128), F32)
            before = flow[8 * q - 4 : 8 * q] if q > 0 else jnp.zeros((4, 128), F32)
            drain[q, 2] = jnp.where(lane4 < 64, after, before)
        for step in (0, 1, -1, 2, -2):
            for q in range(4):
                if step == 0 and q == 3:
                    continue
                send(
                    drain.at[q],
                    drains.at[:, 2 - step],
                    drain_sent.at[step + 2, q],
                    drain_got.at[2 - step],
                    wide_at(step),
                    q,
                )
        drains[:, 2] = drain[3]

    for i, first in ((0, 35), (1, 32)):
        for v in range(2):
            face_out[i, v] = soil[v, pl.ds(first, 128, stride=4), :]
    face_copies = [
        send(
            face_out.at[i],
            face_in.at[i],
            face_sent.at[i],
            face_got.at[i],
            wide_at(1 if i == 0 else -1),
            n,
        )
        for i in range(2)
    ]
    slab_copies = [
        send(
            soil.at[:, pl.ds(512, 32)],
            soil.at[:, pl.ds(0, 32)],
            slab_sent.at[0],
            slab_got.at[0],
            w,
            (n + 1) % narrow_count,
        ),
        send(
            soil.at[:, pl.ds(32, 32)],
            soil.at[:, pl.ds(544, 32)],
            slab_sent.at[1],
            slab_got.at[1],
            w,
            (n + narrow_count - 1) % narrow_count,
        ),
    ]

    for j in range(1, PEERS):
        other = (my_peer + PEERS - j) % PEERS
        pltpu.make_async_remote_copy(
            src_ref=slots.at[other],
            dst_ref=stage_1.at[other],
            send_sem=slots_sent.at[j],
            recv_sem=slots_got.at[j],
            device_id=(w, n),
            device_id_type=MESH,
        ).wait_recv()
    for z in range(depth):
        for p in range(PEERS):
            turned[z, p : p + 1] = stage_1[p, z : z + 1]
    second_stage = []
    for j in range(1, depth):
        other = (my_z + j) % depth
        second_stage.append(
            send(
                turned.at[other],
                stage_2.at[my_z],
                turned_sent.at[j],
                turned_got.at[j],
                other * PEERS + my_peer,
                n,
            )
        )
    stage_2[my_z] = turned[my_z]

    for copy in slab_copies + face_copies:
        copy.wait_recv()

    @pl.when(n == 0)
    def _():
        soil[0, 0:32, :] = soil[0, 32:64, :]
        soil[1, 0:32, :] = -soil[1, 32:64, :]

    @pl.when(bottom)
    def _():
        soil[0, 544:576, :] = aquifer_ref[0:32, :]
        soil[1, 544:576, :] = soil[1, 512:544, :]

    row = iota((32, 128), 0)
    lane = iota((32, 128), 1)
    x = row % 4
    sub8 = iota((8, 128), 0)
    left_open = jnp.where((x == 0) & (w == 0), 0.0, 0.5)
    right_open = jnp.where(w == wide_count - 1, 0.0, 0.5)
    along_open = jnp.where((lane == 0) & (row < 4), 0.0, 0.5)

    def widened(side, v, z):
        pieces = []
        for j in range(4):
            one = face_in[side, v, pl.ds(z * 8 + 2 * j, 1), :]
            two = face_in[side, v, pl.ds(z * 8 + 2 * j + 1, 1), :]
            pieces.append(
                jnp.where(
                    sub8 < 4, jnp.broadcast_to(one, (8, 128)), jnp.broadcast_to(two, (8, 128))
                )
            )
        return jnp.concatenate(pieces, axis=0)

    def previous_column(v):
        moved = roll(v, 1, 1)
        return jnp.where(lane == 0, roll(moved, 4, 0), moved)

    def balance_layer(z, carry):
        over = pl.ds(pl.multiple_of(z * 32, 32), 32)
        here = pl.ds(pl.multiple_of(z * 32 + 32, 32), 32)
        under = pl.ds(pl.multiple_of(z * 32 + 64, 32), 32)
        head, cond = soil[0, here, :], soil[1, here, :]
        vertical_in = 0.5 * (soil[1, over, :] + cond) * (soil[0, over, :] - head + 1.0)
        vertical_out = 0.5 * (cond + soil[1, under, :]) * (head - soil[0, under, :] + 1.0)
        head_left = jnp.where(x == 0, widened(0, 0, z), roll(head, 1, 0))
        cond_left = jnp.where(x == 0, widened(0, 1, z), roll(cond, 1, 0))
        across_in = left_open * (cond_left + cond) * (head_left - head)
        last = right_open * (cond + widened(1, 1, z)) * (head - widened(1, 0, z))
        across_out = jnp.where(x == 3, last, roll(across_in, -1, 0))
        along_in = along_open * (previous_column(cond) + cond) * (previous_column(head) - head)
        moved = roll(along_in, -1, 1)
        along_out = jnp.where(lane == 127, roll(moved, -4, 0), moved)
        balance = (
            (vertical_in - vertical_out) + (across_in - across_out) + (along_in - along_out)
        )
        at = pl.ds(pl.multiple_of(z * 32, 32), 32)
        part[at, :] = head + balance * rest[at, :]
        return carry

    lax.fori_loop(0, 16, balance_layer, 0)

    for i, step in enumerate(around):
        pltpu.make_async_remote_copy(
            src_ref=patch,
            dst_ref=patches.at[:, 2 - step],
            send_sem=patch_sent.at[i],
            recv_sem=patch_got.at[i],
            device_id=(w, n),
            device_id_type=MESH,
        ).wait_recv()
    for step in (-2, -1, 0, 1, 2):

        def wait_drain(step=step):
            pltpu.make_async_remote_copy(
                src_ref=drain.at[0],
                dst_ref=drains.at[:, 2 - step],
                send_sem=drain_sent.at[step + 2, 0],
                recv_sem=drain_got.at[2 - step],
                device_id=(w, n),
                device_id_type=MESH,
            ).wait_recv()

        if step == 0:
            pl.when(jnp.logical_not(bottom))(wait_drain)
        else:
            wait_drain()

    lane24 = iota((24, 128), 1)
    line = iota((24, 128), 0) + 4 * w - 8
    inside = jnp.where((line >= 0) & (line < 4 * wide_count), 1.0, 0.0)
    after_open = jnp.where(n < narrow_count - 1, 1.0, 0.0)
    before_open = jnp.where(n > 0, 1.0, 0.0)
    inside_halo = inside * jnp.where(lane24 < 64, after_open, before_open)

    def stacked(ref, a):
        return jnp.concatenate([ref[a, s] for s in range(6)], axis=0)

    heads = [[stacked(patches, 3 * l + t) * inside for t in range(3)] for l in range(3)]
    flows = [stacked(drains, t) for t in range(3)]
    for l in range(3):
        trans = [stacked(patches, 9 + 3 * l + t) * inside for t in range(3)]
        wests, easts = ring_left(trans, lane24), ring_right(trans, lane24)
        for t in range(3):
            centre = trans[t]
            north = 0.5 * (centre + roll(centre, 1, 0))
            south = 0.5 * (centre + roll(centre, -1, 0))
            west = 0.5 * (centre + wests[t])
            east = 0.5 * (centre + easts[t])
            links = 2.0 if l == 1 else 1.0
            divisor = STORAGE + north + south + west + east + LEAKANCE * links
            inverse = (inside_halo if t == 2 else inside) / divisor
            source = STORAGE * heads[l][t]
            if l == 0:
                source = source + flows[t]
            k = 3 * l + t
            coef[0, k] = north * inverse
            coef[1, k] = south * inverse
            coef[2, k] = west * inverse
            coef[3, k] = east * inverse
            coef[4, k] = LEAKANCE * inverse
            coef[5, k] = source * inverse

    def sweep(_, flat):
        now = [flat[3 * l : 3 * l + 3] for l in range(3)]
        later = []
        for l in range(3):
            wests, easts = ring_left(now[l], lane24), ring_right(now[l], lane24)
            for t in range(3):
                k = 3 * l + t
                centre = now[l][t]
                if l == 1:
                    vertical = now[0][t] + now[2][t]
                else:
                    vertical = now[1][t]
                later.append(
                    coef[5, k]
                    + coef[0, k] * roll(centre, 1, 0)
                    + coef[1, k] * roll(centre, -1, 0)
                    + coef[2, k] * wests[t]
                    + coef[3, k] * easts[t]
                    + coef[4, k] * vertical
                )
        return tuple(later)

    flat = lax.fori_loop(0, SWEEPS, sweep, tuple(v for layer in heads for v in layer))
    for l in range(3):
        aquifer_out_ref[8 * l : 8 * l + 8, :] = jnp.concatenate(
            [flat[3 * l][8:12], flat[3 * l + 1][8:12]], axis=0
        )

    for j in range(1, depth):
        other = (my_z + depth - j) % depth
        pltpu.make_async_remote_copy(
            src_ref=turned.at[other],
            dst_ref=stage_2.at[other],
            send_sem=turned_sent.at[j],
            recv_sem=turned_got.at[j],
            device_id=(w, n),
            device_id_type=MESH,
        ).wait_recv()
    slot_lines[...] = stage_2[...].reshape(128, 128).T
    lanes = iota((128, 128), 0).astype(F32)
    rows = iota((32, 128), 0).astype(F32)
    target = jnp.concatenate(
        [
            (lanes == slot_lines[32 * k + 17 : 32 * k + 18, :]).astype(F32).astype(BF16)
            for k in range(CAP)
        ],
        axis=1,
    )
    for k in range(CAP):
        hit = rows == slot_lines[32 * k + 16 : 32 * k + 17, :]

        def place(z, carry, k=k, hit=hit):
            value = slot_lines[pl.ds(32 * k + z, 1), :]
            value = jnp.where(hit, jnp.broadcast_to(value, (32, 128)), 0.0)
            high = value.astype(BF16)
            low = (value - high.astype(F32)).astype(BF16)
            spread[pl.ds(pl.multiple_of(z * 32, 32), 32), 128 * k : 128 * k + 128] = high
            spread[pl.ds(pl.multiple_of(z * 32 + 512, 32), 32), 128 * k : 128 * k + 128] = low
            return carry

        lax.fori_loop(0, 16, place, 0)
    taken = lax.dot_general(spread[...], target, NT, preferred_element_type=F32)
    out_ref[...] = part[...] - (taken[:512] + taken[512:]) * rest[...]

    for copy in first_stage + patch_copies + face_copies + slab_copies + second_stage:
        copy.wait_send()

    @pl.when(bottom)
    def _():
        for step in (0, 1, -1, 2, -2):
            for q in range(4):
                if step == 0 and q == 3:
                    continue
                pltpu.make_async_remote_copy(
                    src_ref=drain.at[q],
                    dst_ref=drains.at[:, 2 - step],
                    send_sem=drain_sent.at[step + 2, q],
                    recv_sem=drain_got.at[2 - step],
                    device_id=(w, n),
                    device_id_type=MESH,
                ).wait_send()


def rows_of(a):
    k = a.shape[0]
    return a.reshape(k, 4, 8, 128).transpose(0, 2, 1, 3).reshape(k * 32, 128)


def grid_of(a, k, columns):
    return a.reshape(k, columns // 128, 4, 128).transpose(0, 2, 1, 3).reshape(k, 4, columns)


def body(
    pressure_head,
    texture,
    saturated_table,
    shape_table,
    capacity_table,
    uptake,
    root_tile,
    root_column,
    aquifer_head,
    transmissivity,
):
    wide_count = lax.axis_size("wide")
    narrow_count = lax.axis_size("narrow")
    depth = wide_count // PEERS
    dma = pltpu.SemaphoreType.DMA
    out, aquifer_out = pl.pallas_call(
        functools.partial(kernel, wide_count, narrow_count),
        out_shape=(
            jax.ShapeDtypeStruct((512, 128), F32),
            jax.ShapeDtypeStruct((24, 128), F32),
        ),
        in_specs=[pl.BlockSpec(memory_space=pltpu.HBM)] * 10,
        out_specs=[pl.BlockSpec(memory_space=pltpu.VMEM)] * 2,
        scratch_shapes=[
            pltpu.VMEM((512, 128), F32),
            pltpu.VMEM((512, 128), I32),
            pltpu.VMEM((1, 12), F32),
            pltpu.VMEM((1, 12), F32),
            pltpu.VMEM((1, 12), F32),
            pltpu.VMEM((16, 256), F32),
            pltpu.VMEM((1, 256), I32),
            pltpu.VMEM((1, 256), I32),
            pltpu.VMEM((96, 128), F32),
            pltpu.VMEM((96, 128), F32),
            pltpu.VMEM((24, 128), F32),
            pltpu.VMEM((2, 576, 128), F32),
            pltpu.VMEM((512, 128), F32),
            pltpu.VMEM((512, 128), F32),
            pltpu.VMEM((2, 2, 128, 128), F32),
            pltpu.VMEM((2, 2, 128, 128), F32),
            pltpu.VMEM((PEERS, depth, 128), F32),
            pltpu.VMEM((PEERS, depth, 128), F32),
            pltpu.VMEM((depth, PEERS, 128), F32),
            pltpu.VMEM((depth, PEERS, 128), F32),
            pltpu.VMEM((18, 4, 128), F32),
            pltpu.VMEM((18, 6, 4, 128), F32),
            pltpu.VMEM((4, 3, 4, 128), F32),
            pltpu.VMEM((3, 6, 4, 128), F32),
            pltpu.VMEM((6, 9, 24, 128), F32),
            pltpu.VMEM((1024, 512), BF16),
            pltpu.VMEM((128, 128), F32),
            dma((10,)),
            dma((PEERS,)),
            dma((PEERS,)),
            dma((depth,)),
            dma((depth,)),
            dma((4,)),
            dma((4,)),
            dma((5, 4)),
            dma((5,)),
            dma((2,)),
            dma((2,)),
            dma((2,)),
            dma((2,)),
        ],
        compiler_params=pltpu.CompilerParams(
            collective_id=0, has_side_effects=True, vmem_limit_bytes=32 * 1024 * 1024
        ),
        name="coupled_step",
    )(
        rows_of(pressure_head),
        rows_of(texture),
        saturated_table.reshape(1, -1),
        shape_table.reshape(1, -1),
        capacity_table.reshape(1, -1),
        uptake.T,
        root_tile.reshape(1, -1),
        root_column.reshape(1, -1),
        rows_of(aquifer_head),
        rows_of(transmissivity),
    )
    return grid_of(out, 16, 1024), grid_of(aquifer_out, 3, 256)


def solution(mesh):
    in_specs = (
        P("narrow", "wide", None),
        P("narrow", "wide", None),
        P(),
        P(),
        P(),
        P("wide", "narrow"),
        P("wide", None),
        P("wide"),
        P(None, "wide", None),
        P(None, "wide", None),
    )
    out_specs = (P("narrow", "wide", None), P(None, "wide", "narrow"))
    return jax.shard_map(body, mesh=mesh, in_specs=in_specs, out_specs=out_specs, check_vma=False)
```

```python
import functools

import jax
import jax.numpy as jnp
from jax import lax
from jax.experimental import pallas as pl
from jax.experimental.pallas import tpu as pltpu
from jax.sharding import PartitionSpec as P

SWEEPS = 8
TIME_STEP = 0.25
STORAGE = 0.05
LEAKANCE = 0.5
PEERS = 8
CAP = 4
F32, BF16, I32 = jnp.float32, jnp.bfloat16, jnp.int32
MESH = pl.DeviceIdType.MESH
NT = (((1,), (1,)), ((), ()))


def roll(x, shift, axis):
    return pltpu.roll(x, shift % x.shape[axis], axis)


def iota(shape, axis):
    return lax.broadcasted_iota(I32, shape, axis)


def send(src, dst, send_sem, recv_sem, wide, narrow):
    copy = pltpu.make_async_remote_copy(
        src_ref=src,
        dst_ref=dst,
        send_sem=send_sem,
        recv_sem=recv_sem,
        device_id=(wide, narrow),
        device_id_type=MESH,
    )
    copy.start()
    return copy


def root_slots(uptake, tile, column, order):
    place = order(tile)
    cell_row = ((column // 128) % 8) * 4 + column // 1024
    cell_lane = column % 128
    count = tile.shape[1]
    aimed = iota((128, count), 0) == place
    earlier = iota((count, count), 0) < iota((count, count), 1)
    rank = jnp.dot(
        aimed.astype(F32).astype(BF16),
        earlier.astype(F32).astype(BF16),
        preferred_element_type=F32,
    )
    picks = jnp.concatenate(
        [(aimed & (rank == float(k))).astype(F32).astype(BF16) for k in range(CAP)], axis=0
    )
    high = uptake.astype(BF16)
    low = (uptake - high.astype(F32)).astype(BF16)
    line = iota((16, count), 0)
    extra = jnp.where(
        line == 0,
        cell_row.astype(F32),
        jnp.where(line == 1, cell_lane.astype(F32), 0.0),
    ).astype(BF16)
    base = jnp.concatenate([high, extra, low, jnp.zeros_like(extra)], axis=0)
    spread = lax.dot_general(base, picks, NT, preferred_element_type=F32)
    rows = spread[:32] + spread[32:]
    slots = jnp.concatenate([rows[:, 128 * k : 128 * (k + 1)] for k in range(CAP)], axis=0)
    return slots.T


def ring_left(tiles, lane):
    moved = [roll(v, 1, 1) for v in tiles]
    return [jnp.where(lane == 0, moved[t - 1], moved[t]) for t in range(len(tiles))]


def ring_right(tiles, lane):
    moved = [roll(v, -1, 1) for v in tiles]
    return [
        jnp.where(lane == 127, moved[(t + 1) % len(tiles)], moved[t]) for t in range(len(tiles))
    ]


def kernel(
    wide_count,
    narrow_count,
    head_hbm,
    texture_hbm,
    saturated_hbm,
    shape_hbm,
    capacity_hbm,
    uptake_hbm,
    tile_hbm,
    column_hbm,
    aquifer_hbm,
    trans_hbm,
    out_ref,
    aquifer_out_ref,
    head_ref,
    texture_ref,
    saturated_ref,
    shape_ref,
    capacity_ref,
    uptake_ref,
    tile_ref,
    column_ref,
    aquifer_ref,
    trans_ref,
    table,
    soil,
    rest,
    part,
    face_out,
    face_in,
    slots,
    stage_1,
    turned,
    stage_2,
    patch,
    patches,
    drain,
    drains,
    coef,
    spread,
    slot_lines,
    load_done,
    slots_sent,
    slots_got,
    turned_sent,
    turned_got,
    patch_sent,
    patch_got,
    drain_sent,
    drain_got,
    face_sent,
    face_got,
    slab_sent,
    slab_got,
):
    w = lax.axis_index("wide")
    n = lax.axis_index("narrow")
    depth = wide_count // PEERS
    my_z, my_peer = w // PEERS, w % PEERS
    bottom = n == narrow_count - 1
    around = (-2, -1, 1, 2)

    def wide_at(step):
        return (w + step + wide_count) % wide_count

    order = (6, 7, 5, 8, 9, 0, 1, 2, 3, 4)
    held = (head_ref, texture_ref, saturated_ref, shape_ref, capacity_ref, uptake_ref, tile_ref)
    held += (column_ref, aquifer_ref, trans_ref)
    far = (head_hbm, texture_hbm, saturated_hbm, shape_hbm, capacity_hbm, uptake_hbm, tile_hbm)
    far += (column_hbm, aquifer_hbm, trans_hbm)
    loads = [pltpu.make_async_copy(far[i], held[i], load_done.at[i]) for i in range(10)]
    for i in order:
        loads[i].start()

    barrier = pltpu.get_barrier_semaphore()

    def greet(wide, narrow):
        pl.semaphore_signal(barrier, inc=1, device_id=(wide, narrow), device_id_type=MESH)

    for j in range(1, PEERS):
        greet(my_z * PEERS + (my_peer + j) % PEERS, n)
    for j in range(1, depth):
        greet(((my_z + j) % depth) * PEERS + my_peer, n)
    for step in around:
        greet(wide_at(step), n)
    greet(w, (n + 1) % narrow_count)
    greet(w, (n + narrow_count - 1) % narrow_count)

    @pl.when(jnp.logical_not(bottom))
    def _():
        for step in (-2, -1, 0, 1, 2):
            greet(wide_at(step), narrow_count - 1)

    for i in (6, 7, 5):
        loads[i].wait()

    made = root_slots(
        uptake_ref[...],
        tile_ref[...],
        column_ref[...],
        lambda tile: (tile % PEERS) * depth + tile // PEERS,
    )
    slots[...] = made.reshape(PEERS, depth, 128)

    for i in (8, 9):
        loads[i].wait()
    lane4 = iota((4, 128), 1)
    for a in range(6):
        source = aquifer_ref if a < 3 else trans_ref
        first = (a % 3) * 32
        here = source[pl.ds(pl.multiple_of(first + 8 * n, 8), 8), :]
        after = source[pl.ds(pl.multiple_of(first + 8 * jnp.minimum(n + 1, 3), 8), 8), :]
        before = source[pl.ds(pl.multiple_of(first + 8 * jnp.maximum(n - 1, 0), 8), 8), :]
        after = jnp.where(n < narrow_count - 1, after[0:4], 0.0)
        before = jnp.where(n > 0, before[4:8], 0.0)
        patch[3 * a] = here[0:4]
        patch[3 * a + 1] = here[4:8]
        patch[3 * a + 2] = jnp.where(lane4 < 64, after, before)
    for a in range(18):
        patches[a, 2] = patch[a]
        patches[a, 5] = jnp.zeros((4, 128), F32)
    for t in range(3):
        drains[t, 5] = jnp.zeros((4, 128), F32)

    @pl.when(bottom)
    def _():
        pl.semaphore_wait(barrier, PEERS - 1 + depth - 1 + 6 + 5 * (narrow_count - 1))

    @pl.when(jnp.logical_not(bottom))
    def _():
        pl.semaphore_wait(barrier, PEERS - 1 + depth - 1 + 6)

    first_stage = []
    for j in range(1, PEERS):
        peer = (my_peer + j) % PEERS
        first_stage.append(
            send(
                slots.at[peer],
                stage_1.at[my_peer],
                slots_sent.at[j],
                slots_got.at[j],
                my_z * PEERS + peer,
                n,
            )
        )
    stage_1[my_peer] = slots[my_peer]

    patch_copies = []
    for i, step in enumerate(around):
        patch_copies.append(
            send(
                patch,
                patches.at[:, 2 - step],
                patch_sent.at[i],
                patch_got.at[i],
                wide_at(step),
                n,
            )
        )

    for i in (0, 1, 2, 3, 4):
        loads[i].wait()
    table[...] = jnp.zeros_like(table)
    table[0:1, 0:12] = saturated_ref[...]
    table[8:9, 0:12] = shape_ref[...]
    table[16:17, 0:12] = capacity_ref[...]

    def look_up(row, index):
        values = jnp.broadcast_to(table[row : row + 1, :], index.shape)
        return jnp.take_along_axis(values, index, axis=1, mode="promise_in_bounds")

    def conduct_layer(z, carry):
        here = pl.ds(pl.multiple_of(z * 32, 32), 32)
        there = pl.ds(pl.multiple_of(z * 32 + 32, 32), 32)
        head = head_ref[here, :]
        index = texture_ref[here, :]
        soil[0, there, :] = head
        soil[1, there, :] = look_up(0, index) * jnp.exp(look_up(8, index) * jnp.minimum(head, 0.0))
        rest[here, :] = TIME_STEP / look_up(16, index)
        return carry

    lax.fori_loop(0, 16, conduct_layer, 0)

    @pl.when(bottom)
    def _():
        flow = soil[1, 512:544, :] * (soil[0, 512:544, :] - aquifer_ref[0:32, :] + 1.0)
        for q in range(4):
            drain[q, 0] = flow[8 * q : 8 * q + 4]
            drain[q, 1] = flow[8 * q + 4 : 8 * q + 8]
            after = flow[8 * q + 8 : 8 * q + 12] if q < 3 else jnp.zeros((4, 128), F32)
            before = flow[8 * q - 4 : 8 * q] if q > 0 else jnp.zeros((4, 128), F32)
            drain[q, 2] = jnp.where(lane4 < 64, after, before)
        for step in (0, 1, -1, 2, -2):
            for q in range(4):
                if step == 0 and q == 3:
                    continue
                send(
                    drain.at[q],
                    drains.at[:, 2 - step],
                    drain_sent.at[step + 2, q],
                    drain_got.at[2 - step],
                    wide_at(step),
                    q,
                )
        drains[:, 2] = drain[3]

    for i, first in ((0, 35), (1, 32)):
        for v in range(2):
            face_out[i, v] = soil[v, pl.ds(first, 128, stride=4), :]
    face_copies = [
        send(
            face_out.at[i],
            face_in.at[i],
            face_sent.at[i],
            face_got.at[i],
            wide_at(1 if i == 0 else -1),
            n,
        )
        for i in range(2)
    ]
    slab_copies = [
        send(
            soil.at[:, pl.ds(512, 32)],
            soil.at[:, pl.ds(0, 32)],
            slab_sent.at[0],
            slab_got.at[0],
            w,
            (n + 1) % narrow_count,
        ),
        send(
            soil.at[:, pl.ds(32, 32)],
            soil.at[:, pl.ds(544, 32)],
            slab_sent.at[1],
            slab_got.at[1],
            w,
            (n + narrow_count - 1) % narrow_count,
        ),
    ]

    for j in range(1, PEERS):
        other = (my_peer + PEERS - j) % PEERS
        pltpu.make_async_remote_copy(
            src_ref=slots.at[other],
            dst_ref=stage_1.at[other],
            send_sem=slots_sent.at[j],
            recv_sem=slots_got.at[j],
            device_id=(w, n),
            device_id_type=MESH,
        ).wait_recv()
    for z in range(depth):
        for p in range(PEERS):
            turned[z, p : p + 1] = stage_1[p, z : z + 1]
    second_stage = []
    for j in range(1, depth):
        other = (my_z + j) % depth
        second_stage.append(
            send(
                turned.at[other],
                stage_2.at[my_z],
                turned_sent.at[j],
                turned_got.at[j],
                other * PEERS + my_peer,
                n,
            )
        )
    stage_2[my_z] = turned[my_z]

    for copy in slab_copies + face_copies:
        copy.wait_recv()

    @pl.when(n == 0)
    def _():
        soil[0, 0:32, :] = soil[0, 32:64, :]
        soil[1, 0:32, :] = -soil[1, 32:64, :]

    @pl.when(bottom)
    def _():
        soil[0, 544:576, :] = aquifer_ref[0:32, :]
        soil[1, 544:576, :] = soil[1, 512:544, :]

    row = iota((32, 128), 0)
    lane = iota((32, 128), 1)
    x = row % 4
    sub8 = iota((8, 128), 0)
    left_open = jnp.where((x == 0) & (w == 0), 0.0, 0.5)
    right_open = jnp.where(w == wide_count - 1, 0.0, 0.5)
    along_open = jnp.where((lane == 0) & (row < 4), 0.0, 0.5)

    def widened(side, v, z):
        pieces = []
        for j in range(4):
            one = face_in[side, v, pl.ds(z * 8 + 2 * j, 1), :]
            two = face_in[side, v, pl.ds(z * 8 + 2 * j + 1, 1), :]
            pieces.append(
                jnp.where(
                    sub8 < 4, jnp.broadcast_to(one, (8, 128)), jnp.broadcast_to(two, (8, 128))
                )
            )
        return jnp.concatenate(pieces, axis=0)

    def previous_column(v):
        moved = roll(v, 1, 1)
        return jnp.where(lane == 0, roll(moved, 4, 0), moved)

    def balance_layer(z, carry):
        over = pl.ds(pl.multiple_of(z * 32, 32), 32)
        here = pl.ds(pl.multiple_of(z * 32 + 32, 32), 32)
        under = pl.ds(pl.multiple_of(z * 32 + 64, 32), 32)
        head, cond = soil[0, here, :], soil[1, here, :]
        vertical_in = 0.5 * (soil[1, over, :] + cond) * (soil[0, over, :] - head + 1.0)
        vertical_out = 0.5 * (cond + soil[1, under, :]) * (head - soil[0, under, :] + 1.0)
        head_left = jnp.where(x == 0, widened(0, 0, z), roll(head, 1, 0))
        cond_left = jnp.where(x == 0, widened(0, 1, z), roll(cond, 1, 0))
        across_in = left_open * (cond_left + cond) * (head_left - head)
        last = right_open * (cond + widened(1, 1, z)) * (head - widened(1, 0, z))
        across_out = jnp.where(x == 3, last, roll(across_in, -1, 0))
        along_in = along_open * (previous_column(cond) + cond) * (previous_column(head) - head)
        moved = roll(along_in, -1, 1)
        along_out = jnp.where(lane == 127, roll(moved, -4, 0), moved)
        balance = (
            (vertical_in - vertical_out) + (across_in - across_out) + (along_in - along_out)
        )
        at = pl.ds(pl.multiple_of(z * 32, 32), 32)
        part[at, :] = head + balance * rest[at, :]
        return carry

    lax.fori_loop(0, 16, balance_layer, 0)

    for i, step in enumerate(around):
        pltpu.make_async_remote_copy(
            src_ref=patch,
            dst_ref=patches.at[:, 2 - step],
            send_sem=patch_sent.at[i],
            recv_sem=patch_got.at[i],
            device_id=(w, n),
            device_id_type=MESH,
        ).wait_recv()
    for step in (-2, -1, 0, 1, 2):

        def wait_drain(step=step):
            pltpu.make_async_remote_copy(
                src_ref=drain.at[0],
                dst_ref=drains.at[:, 2 - step],
                send_sem=drain_sent.at[step + 2, 0],
                recv_sem=drain_got.at[2 - step],
                device_id=(w, n),
                device_id_type=MESH,
            ).wait_recv()

        if step == 0:
            pl.when(jnp.logical_not(bottom))(wait_drain)
        else:
            wait_drain()

    lane24 = iota((24, 128), 1)
    line = iota((24, 128), 0) + 4 * w - 8
    inside = jnp.where((line >= 0) & (line < 4 * wide_count), 1.0, 0.0)
    after_open = jnp.where(n < narrow_count - 1, 1.0, 0.0)
    before_open = jnp.where(n > 0, 1.0, 0.0)
    inside_halo = inside * jnp.where(lane24 < 64, after_open, before_open)

    def stacked(ref, a):
        return jnp.concatenate([ref[a, s] for s in range(6)], axis=0)

    heads = [[stacked(patches, 3 * l + t) * inside for t in range(3)] for l in range(3)]
    flows = [stacked(drains, t) for t in range(3)]
    for l in range(3):
        trans = [stacked(patches, 9 + 3 * l + t) * inside for t in range(3)]
        wests, easts = ring_left(trans, lane24), ring_right(trans, lane24)
        for t in range(3):
            centre = trans[t]
            north = 0.5 * (centre + roll(centre, 1, 0))
            south = 0.5 * (centre + roll(centre, -1, 0))
            west = 0.5 * (centre + wests[t])
            east = 0.5 * (centre + easts[t])
            links = 2.0 if l == 1 else 1.0
            divisor = STORAGE + north + south + west + east + LEAKANCE * links
            inverse = (inside_halo if t == 2 else inside) / divisor
            source = STORAGE * heads[l][t]
            if l == 0:
                source = source + flows[t]
            k = 3 * l + t
            coef[0, k] = north * inverse
            coef[1, k] = south * inverse
            coef[2, k] = west * inverse
            coef[3, k] = east * inverse
            coef[4, k] = LEAKANCE * inverse
            coef[5, k] = source * inverse

    def sweep(_, flat):
        now = [flat[3 * l : 3 * l + 3] for l in range(3)]
        later = []
        for l in range(3):
            wests, easts = ring_left(now[l], lane24), ring_right(now[l], lane24)
            for t in range(3):
                k = 3 * l + t
                centre = now[l][t]
                if l == 1:
                    vertical = now[0][t] + now[2][t]
                else:
                    vertical = now[1][t]
                later.append(
                    coef[5, k]
                    + coef[0, k] * roll(centre, 1, 0)
                    + coef[1, k] * roll(centre, -1, 0)
                    + coef[2, k] * wests[t]
                    + coef[3, k] * easts[t]
                    + coef[4, k] * vertical
                )
        return tuple(later)

    flat = lax.fori_loop(0, SWEEPS, sweep, tuple(v for layer in heads for v in layer))
    for l in range(3):
        aquifer_out_ref[8 * l : 8 * l + 8, :] = jnp.concatenate(
            [flat[3 * l][8:12], flat[3 * l + 1][8:12]], axis=0
        )

    for j in range(1, depth):
        other = (my_z + depth - j) % depth
        pltpu.make_async_remote_copy(
            src_ref=turned.at[other],
            dst_ref=stage_2.at[other],
            send_sem=turned_sent.at[j],
            recv_sem=turned_got.at[j],
            device_id=(w, n),
            device_id_type=MESH,
        ).wait_recv()
    slot_lines[...] = stage_2[...].reshape(128, 128).T
    lanes = iota((128, 128), 0).astype(F32)
    rows = iota((32, 128), 0).astype(F32)
    target = jnp.concatenate(
        [
            (lanes == slot_lines[32 * k + 17 : 32 * k + 18, :]).astype(F32).astype(BF16)
            for k in range(CAP)
        ],
        axis=1,
    )
    for k in range(CAP):
        hit = rows == slot_lines[32 * k + 16 : 32 * k + 17, :]

        def place(z, carry, k=k, hit=hit):
            value = slot_lines[pl.ds(32 * k + z, 1), :]
            value = jnp.where(hit, jnp.broadcast_to(value, (32, 128)), 0.0)
            high = value.astype(BF16)
            low = (value - high.astype(F32)).astype(BF16)
            spread[pl.ds(pl.multiple_of(z * 32, 32), 32), 128 * k : 128 * k + 128] = high
            spread[pl.ds(pl.multiple_of(z * 32 + 512, 32), 32), 128 * k : 128 * k + 128] = low
            return carry

        lax.fori_loop(0, 16, place, 0)
    taken = lax.dot_general(spread[...], target, NT, preferred_element_type=F32)
    out_ref[...] = part[...] - (taken[:512] + taken[512:]) * rest[...]

    for copy in first_stage + patch_copies + face_copies + slab_copies + second_stage:
        copy.wait_send()

    @pl.when(bottom)
    def _():
        for step in (0, 1, -1, 2, -2):
            for q in range(4):
                if step == 0 and q == 3:
                    continue
                pltpu.make_async_remote_copy(
                    src_ref=drain.at[q],
                    dst_ref=drains.at[:, 2 - step],
                    send_sem=drain_sent.at[step + 2, q],
                    recv_sem=drain_got.at[2 - step],
                    device_id=(w, n),
                    device_id_type=MESH,
                ).wait_send()


def rows_of(a):
    k = a.shape[0]
    return a.reshape(k, 4, 8, 128).transpose(0, 2, 1, 3).reshape(k * 32, 128)


def grid_of(a, k, columns):
    return a.reshape(k, columns // 128, 4, 128).transpose(0, 2, 1, 3).reshape(k, 4, columns)


def body(
    pressure_head,
    texture,
    saturated_table,
    shape_table,
    capacity_table,
    uptake,
    root_tile,
    root_column,
    aquifer_head,
    transmissivity,
):
    wide_count = lax.axis_size("wide")
    narrow_count = lax.axis_size("narrow")
    depth = wide_count // PEERS
    dma = pltpu.SemaphoreType.DMA
    out, aquifer_out = pl.pallas_call(
        functools.partial(kernel, wide_count, narrow_count),
        out_shape=(
            jax.ShapeDtypeStruct((512, 128), F32),
            jax.ShapeDtypeStruct((24, 128), F32),
        ),
        in_specs=[pl.BlockSpec(memory_space=pltpu.HBM)] * 10,
        out_specs=[pl.BlockSpec(memory_space=pltpu.VMEM)] * 2,
        scratch_shapes=[
            pltpu.VMEM((512, 128), F32),
            pltpu.VMEM((512, 128), I32),
            pltpu.VMEM((1, 12), F32),
            pltpu.VMEM((1, 12), F32),
            pltpu.VMEM((1, 12), F32),
            pltpu.VMEM((16, 256), F32),
            pltpu.VMEM((1, 256), I32),
            pltpu.VMEM((1, 256), I32),
            pltpu.VMEM((96, 128), F32),
            pltpu.VMEM((96, 128), F32),
            pltpu.VMEM((24, 128), F32),
            pltpu.VMEM((2, 576, 128), F32),
            pltpu.VMEM((512, 128), F32),
            pltpu.VMEM((512, 128), F32),
            pltpu.VMEM((2, 2, 128, 128), F32),
            pltpu.VMEM((2, 2, 128, 128), F32),
            pltpu.VMEM((PEERS, depth, 128), F32),
            pltpu.VMEM((PEERS, depth, 128), F32),
            pltpu.VMEM((depth, PEERS, 128), F32),
            pltpu.VMEM((depth, PEERS, 128), F32),
            pltpu.VMEM((18, 4, 128), F32),
            pltpu.VMEM((18, 6, 4, 128), F32),
            pltpu.VMEM((4, 3, 4, 128), F32),
            pltpu.VMEM((3, 6, 4, 128), F32),
            pltpu.VMEM((6, 9, 24, 128), F32),
            pltpu.VMEM((1024, 512), BF16),
            pltpu.VMEM((128, 128), F32),
            dma((10,)),
            dma((PEERS,)),
            dma((PEERS,)),
            dma((depth,)),
            dma((depth,)),
            dma((4,)),
            dma((4,)),
            dma((5, 4)),
            dma((5,)),
            dma((2,)),
            dma((2,)),
            dma((2,)),
            dma((2,)),
        ],
        compiler_params=pltpu.CompilerParams(
            collective_id=0, has_side_effects=True, vmem_limit_bytes=60 * 1024 * 1024
        ),
        name="coupled_step",
    )(
        rows_of(pressure_head),
        rows_of(texture),
        saturated_table.reshape(1, -1),
        shape_table.reshape(1, -1),
        capacity_table.reshape(1, -1),
        uptake.T,
        root_tile.reshape(1, -1),
        root_column.reshape(1, -1),
        rows_of(aquifer_head),
        rows_of(transmissivity),
    )
    return grid_of(out, 16, 1024), grid_of(aquifer_out, 3, 256)


def solution(mesh):
    in_specs = (
        P("narrow", "wide", None),
        P("narrow", "wide", None),
        P(),
        P(),
        P(),
        P("wide", "narrow"),
        P("wide", None),
        P("wide"),
        P(None, "wide", None),
        P(None, "wide", None),
    )
    out_specs = (P("narrow", "wide", None), P(None, "wide", "narrow"))
    return jax.shard_map(body, mesh=mesh, in_specs=in_specs, out_specs=out_specs, check_vma=False)
```

```python
import functools

import jax
import jax.numpy as jnp
from jax import lax
from jax.experimental import pallas as pl
from jax.experimental.pallas import tpu as pltpu
from jax.sharding import PartitionSpec as P

SWEEPS = 8
TIME_STEP = 0.25
STORAGE = 0.05
LEAKANCE = 0.5
PEERS = 8
CAP = 4
F32, BF16, I32 = jnp.float32, jnp.bfloat16, jnp.int32
MESH = pl.DeviceIdType.MESH
NT = (((1,), (1,)), ((), ()))


def roll(x, shift, axis):
    return pltpu.roll(x, shift % x.shape[axis], axis)


def iota(shape, axis):
    return lax.broadcasted_iota(I32, shape, axis)


def send(src, dst, send_sem, recv_sem, wide, narrow):
    copy = pltpu.make_async_remote_copy(
        src_ref=src,
        dst_ref=dst,
        send_sem=send_sem,
        recv_sem=recv_sem,
        device_id=(wide, narrow),
        device_id_type=MESH,
    )
    copy.start()
    return copy


def root_slots(uptake, tile, column, order):
    place = order(tile)
    cell_row = ((column // 128) % 8) * 4 + column // 1024
    cell_lane = column % 128
    count = tile.shape[1]
    aimed = iota((128, count), 0) == place
    earlier = iota((count, count), 0) < iota((count, count), 1)
    rank = jnp.dot(
        aimed.astype(F32).astype(BF16),
        earlier.astype(F32).astype(BF16),
        preferred_element_type=F32,
    )
    picks = jnp.concatenate(
        [(aimed & (rank == float(k))).astype(F32).astype(BF16) for k in range(CAP)], axis=0
    )
    high = uptake.astype(BF16)
    low = (uptake - high.astype(F32)).astype(BF16)
    line = iota((16, count), 0)
    extra = jnp.where(
        line == 0,
        cell_row.astype(F32),
        jnp.where(line == 1, cell_lane.astype(F32), 0.0),
    ).astype(BF16)
    base = jnp.concatenate([high, extra, low, jnp.zeros_like(extra)], axis=0)
    spread = lax.dot_general(base, picks, NT, preferred_element_type=F32)
    rows = spread[:32] + spread[32:]
    slots = jnp.concatenate([rows[:, 128 * k : 128 * (k + 1)] for k in range(CAP)], axis=0)
    return slots.T


def ring_left(tiles, lane):
    moved = [roll(v, 1, 1) for v in tiles]
    return [jnp.where(lane == 0, moved[t - 1], moved[t]) for t in range(len(tiles))]


def ring_right(tiles, lane):
    moved = [roll(v, -1, 1) for v in tiles]
    return [
        jnp.where(lane == 127, moved[(t + 1) % len(tiles)], moved[t]) for t in range(len(tiles))
    ]


def kernel(
    wide_count,
    narrow_count,
    head_hbm,
    texture_hbm,
    saturated_hbm,
    shape_hbm,
    capacity_hbm,
    uptake_hbm,
    tile_hbm,
    column_hbm,
    aquifer_hbm,
    trans_hbm,
    stage_2,
    part_hbm,
    rest_hbm,
    aquifer_next,
    head_ref,
    texture_ref,
    saturated_ref,
    shape_ref,
    capacity_ref,
    uptake_ref,
    tile_ref,
    column_ref,
    aquifer_ref,
    trans_ref,
    table,
    soil,
    rest,
    part,
    face_out,
    face_in,
    slab_in,
    slots,
    stage_1,
    turned,
    patch,
    patches,
    drain,
    drains,
    coef,
    aquifer_part,
    store_done,
    load_done,
    slots_sent,
    slots_got,
    turned_sent,
    turned_got,
    patch_sent,
    patch_got,
    drain_sent,
    drain_got,
    face_sent,
    face_got,
    slab_sent,
    slab_got,
):
    w = lax.axis_index("wide")
    n = lax.axis_index("narrow")
    depth = wide_count // PEERS
    my_z, my_peer = w // PEERS, w % PEERS
    bottom = n == narrow_count - 1
    around = (-2, -1, 1, 2)

    def wide_at(step):
        return (w + step + wide_count) % wide_count

    order = (6, 7, 5, 8, 9, 0, 1, 2, 3, 4)
    held = (head_ref, texture_ref, saturated_ref, shape_ref, capacity_ref, uptake_ref, tile_ref)
    held += (column_ref, aquifer_ref, trans_ref)
    far = (head_hbm, texture_hbm, saturated_hbm, shape_hbm, capacity_hbm, uptake_hbm, tile_hbm)
    far += (column_hbm, aquifer_hbm, trans_hbm)
    loads = [pltpu.make_async_copy(far[i], held[i], load_done.at[i]) for i in range(10)]
    for i in order:
        loads[i].start()

    barrier = pltpu.get_barrier_semaphore()

    def greet(wide, narrow):
        pl.semaphore_signal(barrier, inc=1, device_id=(wide, narrow), device_id_type=MESH)

    for j in range(1, PEERS):
        greet(my_z * PEERS + (my_peer + j) % PEERS, n)
    for j in range(1, depth):
        greet(((my_z + j) % depth) * PEERS + my_peer, n)
    for step in around:
        greet(wide_at(step), n)
    greet(w, (n + 1) % narrow_count)
    greet(w, (n + narrow_count - 1) % narrow_count)

    @pl.when(jnp.logical_not(bottom))
    def _():
        for step in (-2, -1, 0, 1, 2):
            greet(wide_at(step), narrow_count - 1)

    for i in (6, 7, 5):
        loads[i].wait()

    made = root_slots(
        uptake_ref[...],
        tile_ref[...],
        column_ref[...],
        lambda tile: (tile % PEERS) * depth + tile // PEERS,
    )
    slots[...] = made.reshape(PEERS, depth, 128)

    for i in (8, 9):
        loads[i].wait()
    lane4 = iota((4, 128), 1)
    for a in range(6):
        source = aquifer_ref if a < 3 else trans_ref
        first = (a % 3) * 32
        here = source[pl.ds(pl.multiple_of(first + 8 * n, 8), 8), :]
        after = source[pl.ds(pl.multiple_of(first + 8 * jnp.minimum(n + 1, 3), 8), 8), :]
        before = source[pl.ds(pl.multiple_of(first + 8 * jnp.maximum(n - 1, 0), 8), 8), :]
        after = jnp.where(n < narrow_count - 1, after[0:4], 0.0)
        before = jnp.where(n > 0, before[4:8], 0.0)
        patch[3 * a] = here[0:4]
        patch[3 * a + 1] = here[4:8]
        patch[3 * a + 2] = jnp.where(lane4 < 64, after, before)
    for a in range(18):
        patches[a, 2] = patch[a]
        patches[a, 5] = jnp.zeros((4, 128), F32)
    for t in range(3):
        drains[t, 5] = jnp.zeros((4, 128), F32)

    @pl.when(bottom)
    def _():
        pl.semaphore_wait(barrier, PEERS - 1 + depth - 1 + 6 + 5 * (narrow_count - 1))

    @pl.when(jnp.logical_not(bottom))
    def _():
        pl.semaphore_wait(barrier, PEERS - 1 + depth - 1 + 6)

    first_stage = []
    for j in range(1, PEERS):
        peer = (my_peer + j) % PEERS
        first_stage.append(
            send(
                slots.at[peer],
                stage_1.at[my_peer],
                slots_sent.at[j],
                slots_got.at[j],
                my_z * PEERS + peer,
                n,
            )
        )
    stage_1[my_peer] = slots[my_peer]

    patch_copies = []
    for i, step in enumerate(around):
        patch_copies.append(
            send(
                patch,
                patches.at[:, 2 - step],
                patch_sent.at[i],
                patch_got.at[i],
                wide_at(step),
                n,
            )
        )

    for i in (0, 1, 2, 3, 4):
        loads[i].wait()
    table[...] = jnp.zeros_like(table)
    table[0:1, 0:12] = saturated_ref[...]
    table[8:9, 0:12] = shape_ref[...]
    table[16:17, 0:12] = capacity_ref[...]

    def look_up(row, index):
        values = jnp.broadcast_to(table[row : row + 1, :], index.shape)
        return jnp.take_along_axis(values, index, axis=1, mode="promise_in_bounds")

    def conduct_layer(z, carry):
        here = pl.ds(pl.multiple_of(z * 32, 32), 32)
        head = head_ref[here, :]
        index = texture_ref[here, :]
        soil[0, here, :] = head
        soil[1, here, :] = look_up(0, index) * jnp.exp(look_up(8, index) * jnp.minimum(head, 0.0))
        rest[here, :] = TIME_STEP / look_up(16, index)
        return carry

    lax.fori_loop(0, 16, conduct_layer, 0, unroll=4)
    rest_out = pltpu.make_async_copy(rest, rest_hbm, store_done.at[0])
    rest_out.start()

    for i, first in ((0, 3), (1, 0)):
        for v in range(2):
            face_out[i, v] = soil[v, pl.ds(first, 128, stride=4), :]
    face_copies = [
        send(
            face_out.at[i],
            face_in.at[i],
            face_sent.at[i],
            face_got.at[i],
            wide_at(1 if i == 0 else -1),
            n,
        )
        for i in range(2)
    ]
    slab_copies = [
        send(
            soil.at[:, pl.ds(480, 32)],
            slab_in.at[0],
            slab_sent.at[0],
            slab_got.at[0],
            w,
            (n + 1) % narrow_count,
        ),
        send(
            soil.at[:, pl.ds(0, 32)],
            slab_in.at[1],
            slab_sent.at[1],
            slab_got.at[1],
            w,
            (n + narrow_count - 1) % narrow_count,
        ),
    ]

    @pl.when(bottom)
    def _():
        flow = soil[1, 480:512, :] * (soil[0, 480:512, :] - aquifer_ref[0:32, :] + 1.0)
        for q in range(4):
            drain[q, 0] = flow[8 * q : 8 * q + 4]
            drain[q, 1] = flow[8 * q + 4 : 8 * q + 8]
            after = flow[8 * q + 8 : 8 * q + 12] if q < 3 else jnp.zeros((4, 128), F32)
            before = flow[8 * q - 4 : 8 * q] if q > 0 else jnp.zeros((4, 128), F32)
            drain[q, 2] = jnp.where(lane4 < 64, after, before)
        for step in (0, 1, -1, 2, -2):
            for q in range(4):
                if step == 0 and q == 3:
                    continue
                send(
                    drain.at[q],
                    drains.at[:, 2 - step],
                    drain_sent.at[step + 2, q],
                    drain_got.at[2 - step],
                    wide_at(step),
                    q,
                )
        drains[:, 2] = drain[3]

    for j in range(1, PEERS):
        other = (my_peer + PEERS - j) % PEERS
        pltpu.make_async_remote_copy(
            src_ref=slots.at[other],
            dst_ref=stage_1.at[other],
            send_sem=slots_sent.at[j],
            recv_sem=slots_got.at[j],
            device_id=(w, n),
            device_id_type=MESH,
        ).wait_recv()
    for z in range(depth):
        for p in range(PEERS):
            turned[z, p : p + 1] = stage_1[p, z : z + 1]
    second_stage = []
    for j in range(1, depth):
        other = (my_z + j) % depth
        second_stage.append(
            send(
                turned.at[other],
                stage_2.at[my_z],
                turned_sent.at[j],
                turned_got.at[j],
                other * PEERS + my_peer,
                n,
            )
        )
    own_rows = pltpu.make_async_copy(turned.at[my_z], stage_2.at[my_z], store_done.at[1])
    own_rows.start()

    row = iota((32, 128), 0)
    lane = iota((32, 128), 1)
    across_open = jnp.where(row % 4 == 0, 0.0, 0.5)
    along_open = jnp.where((lane == 0) & (row < 4), 0.0, 0.5)

    def previous_column(v):
        moved = roll(v, 1, 1)
        return jnp.where(lane == 0, roll(moved, 4, 0), moved)

    def layer(z):
        at = pl.ds(pl.multiple_of(z * 32, 32), 32)
        return soil[0, at, :], soil[1, at, :]

    def sides(head, cond):
        across = across_open * (roll(cond, 1, 0) + cond) * (roll(head, 1, 0) - head)
        along = along_open * (previous_column(cond) + cond) * (previous_column(head) - head)
        moved = roll(along, -1, 1)
        along_out = jnp.where(lane == 127, roll(moved, -4, 0), moved)
        return (across - roll(across, -1, 0)) + (along - along_out)

    def balance_layer(z, vertical_in):
        head, cond = layer(z)
        head_under, cond_under = layer(z + 1)
        vertical_out = 0.5 * (cond + cond_under) * (head - head_under + 1.0)
        at = pl.ds(pl.multiple_of(z * 32, 32), 32)
        balance = (vertical_in - vertical_out) + sides(head, cond)
        part[at, :] = head + balance * rest[at, :]
        return vertical_out

    vertical_in = lax.fori_loop(0, 15, balance_layer, jnp.zeros((32, 128), F32), unroll=5)
    head, cond = layer(15)
    part[480:512, :] = head + (vertical_in + sides(head, cond)) * rest[480:512, :]

    for copy in slab_copies + face_copies:
        copy.wait_recv()
    head_under = jnp.where(bottom, aquifer_ref[0:32, :], slab_in[1, 0])
    cond_under = jnp.where(bottom, cond, slab_in[1, 1])
    vertical_out = 0.5 * (cond + cond_under) * (head - head_under + 1.0)
    part[480:512, :] = part[480:512, :] - vertical_out * rest[480:512, :]
    head, cond = layer(0)
    top_open = jnp.where(n == 0, 0.0, 0.5)
    vertical_in = top_open * (slab_in[0, 1] + cond) * (slab_in[0, 0] - head + 1.0)
    part[0:32, :] = part[0:32, :] + vertical_in * rest[0:32, :]
    left_open = jnp.where(w == 0, 0.0, 0.5)
    right_open = jnp.where(w == wide_count - 1, 0.0, -0.5)
    for side, first, is_open in ((0, 0, left_open), (1, 3, right_open)):
        head, cond = face_out[1 - side, 0], face_out[1 - side, 1]
        other_head, other_cond = face_in[side, 0], face_in[side, 1]
        jump = other_head - head if side == 0 else head - other_head
        at = pl.ds(first, 128, stride=4)
        part[at, :] = part[at, :] + is_open * (cond + other_cond) * jump * rest[at, :]
    part_out = pltpu.make_async_copy(part, part_hbm, store_done.at[2])
    part_out.start()

    for i, step in enumerate(around):
        pltpu.make_async_remote_copy(
            src_ref=patch,
            dst_ref=patches.at[:, 2 - step],
            send_sem=patch_sent.at[i],
            recv_sem=patch_got.at[i],
            device_id=(w, n),
            device_id_type=MESH,
        ).wait_recv()
    for step in (-2, -1, 0, 1, 2):

        def wait_drain(step=step):
            pltpu.make_async_remote_copy(
                src_ref=drain.at[0],
                dst_ref=drains.at[:, 2 - step],
                send_sem=drain_sent.at[step + 2, 0],
                recv_sem=drain_got.at[2 - step],
                device_id=(w, n),
                device_id_type=MESH,
            ).wait_recv()

        if step == 0:
            pl.when(jnp.logical_not(bottom))(wait_drain)
        else:
            wait_drain()

    lane24 = iota((24, 128), 1)
    line = iota((24, 128), 0) + 4 * w - 8
    inside = jnp.where((line >= 0) & (line < 4 * wide_count), 1.0, 0.0)
    after_open = jnp.where(n < narrow_count - 1, 1.0, 0.0)
    before_open = jnp.where(n > 0, 1.0, 0.0)
    inside_halo = inside * jnp.where(lane24 < 64, after_open, before_open)

    def stacked(ref, a):
        return jnp.concatenate([ref[a, s] for s in range(6)], axis=0)

    heads = [[stacked(patches, 3 * l + t) * inside for t in range(3)] for l in range(3)]
    flows = [stacked(drains, t) for t in range(3)]
    for l in range(3):
        trans = [stacked(patches, 9 + 3 * l + t) * inside for t in range(3)]
        wests, easts = ring_left(trans, lane24), ring_right(trans, lane24)
        for t in range(3):
            centre = trans[t]
            north = 0.5 * (centre + roll(centre, 1, 0))
            south = 0.5 * (centre + roll(centre, -1, 0))
            west = 0.5 * (centre + wests[t])
            east = 0.5 * (centre + easts[t])
            links = 2.0 if l == 1 else 1.0
            divisor = STORAGE + north + south + west + east + LEAKANCE * links
            inverse = (inside_halo if t == 2 else inside) / divisor
            source = STORAGE * heads[l][t]
            if l == 0:
                source = source + flows[t]
            k = 3 * l + t
            coef[0, k] = north * inverse
            coef[1, k] = south * inverse
            coef[2, k] = west * inverse
            coef[3, k] = east * inverse
            coef[4, k] = LEAKANCE * inverse
            coef[5, k] = source * inverse

    def sweep(_, flat):
        now = [flat[3 * l : 3 * l + 3] for l in range(3)]
        later = []
        for l in range(3):
            wests, easts = ring_left(now[l], lane24), ring_right(now[l], lane24)
            for t in range(3):
                k = 3 * l + t
                centre = now[l][t]
                if l == 1:
                    vertical = now[0][t] + now[2][t]
                else:
                    vertical = now[1][t]
                later.append(
                    coef[5, k]
                    + coef[0, k] * roll(centre, 1, 0)
                    + coef[1, k] * roll(centre, -1, 0)
                    + coef[2, k] * wests[t]
                    + coef[3, k] * easts[t]
                    + coef[4, k] * vertical
                )
        return tuple(later)

    flat = lax.fori_loop(0, SWEEPS, sweep, tuple(v for layer in heads for v in layer))
    for l in range(3):
        aquifer_part[8 * l : 8 * l + 8, :] = jnp.concatenate(
            [flat[3 * l][8:12], flat[3 * l + 1][8:12]], axis=0
        )
    aquifer_out = pltpu.make_async_copy(aquifer_part, aquifer_next, store_done.at[3])
    aquifer_out.start()

    for j in range(1, depth):
        other = (my_z + depth - j) % depth
        pltpu.make_async_remote_copy(
            src_ref=turned.at[other],
            dst_ref=stage_2.at[other],
            send_sem=turned_sent.at[j],
            recv_sem=turned_got.at[j],
            device_id=(w, n),
            device_id_type=MESH,
        ).wait_recv()
    for copy in (rest_out, own_rows, part_out, aquifer_out):
        copy.wait()
    for copy in first_stage + patch_copies + face_copies + slab_copies + second_stage:
        copy.wait_send()

    @pl.when(bottom)
    def _():
        for step in (0, 1, -1, 2, -2):
            for q in range(4):
                if step == 0 and q == 3:
                    continue
                pltpu.make_async_remote_copy(
                    src_ref=drain.at[q],
                    dst_ref=drains.at[:, 2 - step],
                    send_sem=drain_sent.at[step + 2, q],
                    recv_sem=drain_got.at[2 - step],
                    device_id=(w, n),
                    device_id_type=MESH,
                ).wait_send()


def finish(
    rows_hbm,
    part_hbm,
    rest_hbm,
    aquifer_hbm,
    out_hbm,
    aquifer_out_hbm,
    rows_in,
    part,
    rest,
    out,
    spread,
    slot_lines,
    done,
):
    pairs = ((rows_hbm, rows_in), (part_hbm, part), (rest_hbm, rest), (aquifer_hbm, aquifer_out_hbm))
    loads = [pltpu.make_async_copy(a, b, done.at[i]) for i, (a, b) in enumerate(pairs)]
    for load in loads:
        load.start()
    loads[0].wait()
    slot_lines[...] = rows_in[...].T
    lanes = iota((128, 128), 0).astype(F32)
    rows = iota((32, 128), 0).astype(F32)
    target = jnp.concatenate(
        [
            (lanes == slot_lines[32 * k + 17 : 32 * k + 18, :]).astype(F32).astype(BF16)
            for k in range(CAP)
        ],
        axis=1,
    )
    for k in range(CAP):
        hit = rows == slot_lines[32 * k + 16 : 32 * k + 17, :]

        def place(z, carry, k=k, hit=hit):
            value = slot_lines[pl.ds(32 * k + z, 1), :]
            value = jnp.where(hit, jnp.broadcast_to(value, (32, 128)), 0.0)
            high = value.astype(BF16)
            low = (value - high.astype(F32)).astype(BF16)
            spread[pl.ds(pl.multiple_of(z * 32, 32), 32), 128 * k : 128 * k + 128] = high
            spread[pl.ds(pl.multiple_of(z * 32 + 512, 32), 32), 128 * k : 128 * k + 128] = low
            return carry

        lax.fori_loop(0, 16, place, 0, unroll=4)
    taken = lax.dot_general(spread[...], target, NT, preferred_element_type=F32)
    loads[1].wait()
    loads[2].wait()
    out[...] = part[...] - (taken[:512] + taken[512:]) * rest[...]
    stored = pltpu.make_async_copy(out, out_hbm, done.at[4])
    stored.start()
    loads[3].wait()
    stored.wait()


def rows_of(a):
    k = a.shape[0]
    return a.reshape(k, 4, 8, 128).transpose(0, 2, 1, 3).reshape(k * 32, 128)


def grid_of(a, k, columns):
    return a.reshape(k, columns // 128, 4, 128).transpose(0, 2, 1, 3).reshape(k, 4, columns)


def body(
    pressure_head,
    texture,
    saturated_table,
    shape_table,
    capacity_table,
    uptake,
    root_tile,
    root_column,
    aquifer_head,
    transmissivity,
):
    wide_count = lax.axis_size("wide")
    narrow_count = lax.axis_size("narrow")
    depth = wide_count // PEERS
    dma = pltpu.SemaphoreType.DMA
    hbm = pl.BlockSpec(memory_space=pl.ANY)
    rows_in, part, rest, aquifer_next = pl.pallas_call(
        functools.partial(kernel, wide_count, narrow_count),
        out_shape=(
            jax.ShapeDtypeStruct((depth, PEERS, 128), F32),
            jax.ShapeDtypeStruct((512, 128), F32),
            jax.ShapeDtypeStruct((512, 128), F32),
            jax.ShapeDtypeStruct((24, 128), F32),
        ),
        in_specs=[hbm] * 10,
        out_specs=[hbm] * 4,
        scratch_shapes=[
            pltpu.VMEM((512, 128), F32),
            pltpu.VMEM((512, 128), I32),
            pltpu.VMEM((1, 12), F32),
            pltpu.VMEM((1, 12), F32),
            pltpu.VMEM((1, 12), F32),
            pltpu.VMEM((16, 256), F32),
            pltpu.VMEM((1, 256), I32),
            pltpu.VMEM((1, 256), I32),
            pltpu.VMEM((96, 128), F32),
            pltpu.VMEM((96, 128), F32),
            pltpu.VMEM((24, 128), F32),
            pltpu.VMEM((2, 512, 128), F32),
            pltpu.VMEM((512, 128), F32),
            pltpu.VMEM((512, 128), F32),
            pltpu.VMEM((2, 2, 128, 128), F32),
            pltpu.VMEM((2, 2, 128, 128), F32),
            pltpu.VMEM((2, 2, 32, 128), F32),
            pltpu.VMEM((PEERS, depth, 128), F32),
            pltpu.VMEM((PEERS, depth, 128), F32),
            pltpu.VMEM((depth, PEERS, 128), F32),
            pltpu.VMEM((18, 4, 128), F32),
            pltpu.VMEM((18, 6, 4, 128), F32),
            pltpu.VMEM((4, 3, 4, 128), F32),
            pltpu.VMEM((3, 6, 4, 128), F32),
            pltpu.VMEM((6, 9, 24, 128), F32),
            pltpu.VMEM((24, 128), F32),
            dma((4,)),
            dma((10,)),
            dma((PEERS,)),
            dma((PEERS,)),
            dma((depth,)),
            dma((depth,)),
            dma((4,)),
            dma((4,)),
            dma((5, 4)),
            dma((5,)),
            dma((2,)),
            dma((2,)),
            dma((2,)),
            dma((2,)),
        ],
        compiler_params=pltpu.CompilerParams(
            collective_id=0, has_side_effects=True, vmem_limit_bytes=60 * 1024 * 1024
        ),
        name="coupled_step",
    )(
        rows_of(pressure_head),
        rows_of(texture),
        saturated_table.reshape(1, -1),
        shape_table.reshape(1, -1),
        capacity_table.reshape(1, -1),
        uptake.T,
        root_tile.reshape(1, -1),
        root_column.reshape(1, -1),
        rows_of(aquifer_head),
        rows_of(transmissivity),
    )
    out, aquifer_out = pl.pallas_call(
        finish,
        out_shape=(
            jax.ShapeDtypeStruct((512, 128), F32),
            jax.ShapeDtypeStruct((24, 128), F32),
        ),
        in_specs=[hbm] * 4,
        out_specs=[hbm] * 2,
        scratch_shapes=[
            pltpu.VMEM((128, 128), F32),
            pltpu.VMEM((512, 128), F32),
            pltpu.VMEM((512, 128), F32),
            pltpu.VMEM((512, 128), F32),
            pltpu.VMEM((1024, 512), BF16),
            pltpu.VMEM((128, 128), F32),
            dma((5,)),
        ],
        compiler_params=pltpu.CompilerParams(vmem_limit_bytes=60 * 1024 * 1024),
        name="finish_step",
    )(rows_in.reshape(128, 128), part, rest, aquifer_next)
    return grid_of(out, 16, 1024), grid_of(aquifer_out, 3, 256)


def solution(mesh):
    in_specs = (
        P("narrow", "wide", None),
        P("narrow", "wide", None),
        P(),
        P(),
        P(),
        P("wide", "narrow"),
        P("wide", None),
        P("wide"),
        P(None, "wide", None),
        P(None, "wide", None),
    )
    out_specs = (P("narrow", "wide", None), P(None, "wide", "narrow"))
    return jax.shard_map(body, mesh=mesh, in_specs=in_specs, out_specs=out_specs, check_vma=False)
```

```python
import functools

import jax
import jax.numpy as jnp
from jax import lax
from jax.experimental import pallas as pl
from jax.experimental.pallas import tpu as pltpu
from jax.sharding import PartitionSpec as P

SWEEPS = 8
TIME_STEP = 0.25
STORAGE = 0.05
LEAKANCE = 0.5
PEERS = 8
CAP = 4
F32, BF16, I32 = jnp.float32, jnp.bfloat16, jnp.int32
MESH = pl.DeviceIdType.MESH
NT = (((1,), (1,)), ((), ()))


def roll(x, shift, axis):
    return pltpu.roll(x, shift % x.shape[axis], axis)


def iota(shape, axis):
    return lax.broadcasted_iota(I32, shape, axis)


def send(src, dst, send_sem, recv_sem, wide, narrow):
    copy = pltpu.make_async_remote_copy(
        src_ref=src,
        dst_ref=dst,
        send_sem=send_sem,
        recv_sem=recv_sem,
        device_id=(wide, narrow),
        device_id_type=MESH,
    )
    copy.start()
    return copy


def root_slots(uptake, tile, column):
    cell_row = ((column // 128) % 8) * 4 + column // 1024
    cell_lane = column % 128
    count = tile.shape[1]
    aimed = iota((128, count), 0) == tile
    earlier = iota((count, count), 0) < iota((count, count), 1)
    rank = jnp.dot(
        aimed.astype(F32).astype(BF16),
        earlier.astype(F32).astype(BF16),
        preferred_element_type=F32,
    )
    picks = jnp.concatenate(
        [(aimed & (rank == float(k))).astype(F32).astype(BF16) for k in range(CAP)], axis=0
    )
    high = uptake.astype(BF16)
    low = (uptake - high.astype(F32)).astype(BF16)
    line = iota((16, count), 0)
    extra = jnp.where(
        line == 0,
        cell_row.astype(F32),
        jnp.where(line == 1, cell_lane.astype(F32), 0.0),
    ).astype(BF16)
    base = jnp.concatenate([high, extra, low, jnp.zeros_like(extra)], axis=0)
    spread = lax.dot_general(base, picks, NT, preferred_element_type=F32)
    rows = spread[:32] + spread[32:]
    slots = jnp.concatenate([rows[:, 128 * k : 128 * (k + 1)] for k in range(CAP)], axis=0)
    return slots.T


def ring_left(tiles, lane):
    moved = [roll(v, 1, 1) for v in tiles]
    return [jnp.where(lane == 0, moved[t - 1], moved[t]) for t in range(len(tiles))]


def ring_right(tiles, lane):
    moved = [roll(v, -1, 1) for v in tiles]
    return [
        jnp.where(lane == 127, moved[(t + 1) % len(tiles)], moved[t]) for t in range(len(tiles))
    ]


def kernel(
    wide_count,
    narrow_count,
    head_hbm,
    texture_hbm,
    saturated_hbm,
    shape_hbm,
    capacity_hbm,
    uptake_hbm,
    tile_hbm,
    column_hbm,
    aquifer_hbm,
    trans_hbm,
    rows,
    part_hbm,
    rest_hbm,
    aquifer_next,
    head_ref,
    texture_ref,
    saturated_ref,
    shape_ref,
    capacity_ref,
    uptake_ref,
    tile_ref,
    column_ref,
    aquifer_ref,
    trans_ref,
    table,
    soil,
    rest,
    part,
    face_out,
    face_in,
    slab_in,
    slots,
    patch,
    patches,
    drain,
    drains,
    coef,
    aquifer_part,
    store_done,
    load_done,
    rows_sent,
    rows_got,
    patch_sent,
    patch_got,
    drain_sent,
    drain_got,
    face_sent,
    face_got,
    slab_sent,
    slab_got,
):
    w = lax.axis_index("wide")
    n = lax.axis_index("narrow")
    depth = wide_count // PEERS
    my_z, my_peer = w // PEERS, w % PEERS
    bottom = n == narrow_count - 1
    around = (-2, -1, 1, 2)

    def wide_at(step):
        return (w + step + wide_count) % wide_count

    order = (6, 7, 5, 8, 9, 0, 1, 2, 3, 4)
    held = (head_ref, texture_ref, saturated_ref, shape_ref, capacity_ref, uptake_ref, tile_ref)
    held += (column_ref, aquifer_ref, trans_ref)
    far = (head_hbm, texture_hbm, saturated_hbm, shape_hbm, capacity_hbm, uptake_hbm, tile_hbm)
    far += (column_hbm, aquifer_hbm, trans_hbm)
    loads = [pltpu.make_async_copy(far[i], held[i], load_done.at[i]) for i in range(10)]
    for i in order:
        loads[i].start()

    barrier = pltpu.get_barrier_semaphore()

    def greet(wide, narrow):
        pl.semaphore_signal(barrier, inc=1, device_id=(wide, narrow), device_id_type=MESH)

    peers = [(my_peer + j) % PEERS for j in range(1, PEERS + 1)]

    def greet_plane(z, carry):
        for peer in peers:
            greet(z * PEERS + peer, n)
        return carry

    lax.fori_loop(my_z + 1, depth, greet_plane, 0)
    for peer in peers[:-1]:
        greet(my_z * PEERS + peer, n)
    later_around = 0
    for step in around:
        plane = wide_at(step) // PEERS
        later_around = later_around + jnp.where(plane > my_z, 1, 0)

        @pl.when(plane < my_z)
        def _(step=step):
            greet(wide_at(step), n)

    greet(w, (n + 1) % narrow_count)
    greet(w, (n + narrow_count - 1) % narrow_count)
    greeted = PEERS * my_z + PEERS - 1 + later_around + 2

    @pl.when(jnp.logical_not(bottom))
    def _():
        for step in (-2, -1, 0, 1, 2):
            greet(wide_at(step), narrow_count - 1)

    for i in (6, 7, 5):
        loads[i].wait()

    made = root_slots(
        uptake_ref[...],
        tile_ref[...],
        column_ref[...],
    )
    slots[...] = made

    for i in (8, 9):
        loads[i].wait()
    lane4 = iota((4, 128), 1)
    for a in range(6):
        source = aquifer_ref if a < 3 else trans_ref
        first = (a % 3) * 32
        here = source[pl.ds(pl.multiple_of(first + 8 * n, 8), 8), :]
        after = source[pl.ds(pl.multiple_of(first + 8 * jnp.minimum(n + 1, 3), 8), 8), :]
        before = source[pl.ds(pl.multiple_of(first + 8 * jnp.maximum(n - 1, 0), 8), 8), :]
        after = jnp.where(n < narrow_count - 1, after[0:4], 0.0)
        before = jnp.where(n > 0, before[4:8], 0.0)
        patch[3 * a] = here[0:4]
        patch[3 * a + 1] = here[4:8]
        patch[3 * a + 2] = jnp.where(lane4 < 64, after, before)
    for a in range(18):
        patches[a, 2] = patch[a]
        patches[a, 5] = jnp.zeros((4, 128), F32)
    for t in range(3):
        drains[t, 5] = jnp.zeros((4, 128), F32)

    @pl.when(bottom)
    def _():
        pl.semaphore_wait(barrier, greeted + 5 * (narrow_count - 1))

    @pl.when(jnp.logical_not(bottom))
    def _():
        pl.semaphore_wait(barrier, greeted)

    def send_rows(tile):
        pltpu.make_async_remote_copy(
            src_ref=slots.at[pl.ds(tile, 1)],
            dst_ref=rows.at[w],
            send_sem=rows_sent.at[0],
            recv_sem=rows_got.at[my_z],
            device_id=(tile, n),
            device_id_type=MESH,
        ).start()

    def rows_from(first, count, sent, got):
        at = pl.ds(first, count)
        return pltpu.make_async_remote_copy(
            src_ref=rows.at[at],
            dst_ref=rows.at[at],
            send_sem=sent,
            recv_sem=got,
            device_id=(w, n),
            device_id_type=MESH,
        )

    def send_plane(z, carry):
        for peer in peers:
            send_rows(z * PEERS + peer)
        return carry

    lax.fori_loop(0, my_z, send_plane, 0)
    for peer in peers[:-1]:
        send_rows(my_z * PEERS + peer)
    own_rows = pltpu.make_async_copy(slots.at[pl.ds(w, 1)], rows.at[w], store_done.at[1])
    own_rows.start()

    patch_copies = []
    for i, step in enumerate(around):
        patch_copies.append(
            send(
                patch,
                patches.at[:, 2 - step],
                patch_sent.at[i],
                patch_got.at[i],
                wide_at(step),
                n,
            )
        )

    for i in (0, 1, 2, 3, 4):
        loads[i].wait()
    table[...] = jnp.zeros_like(table)
    table[0:1, 0:12] = saturated_ref[...]
    table[8:9, 0:12] = shape_ref[...]
    table[16:17, 0:12] = capacity_ref[...]

    def look_up(row, index):
        values = jnp.broadcast_to(table[row : row + 1, :], index.shape)
        return jnp.take_along_axis(values, index, axis=1, mode="promise_in_bounds")

    def conduct_layer(z, carry):
        here = pl.ds(pl.multiple_of(z * 32, 32), 32)
        head = head_ref[here, :]
        index = texture_ref[here, :]
        soil[0, here, :] = head
        soil[1, here, :] = look_up(0, index) * jnp.exp(look_up(8, index) * jnp.minimum(head, 0.0))
        rest[here, :] = TIME_STEP / look_up(16, index)
        return carry

    lax.fori_loop(0, 16, conduct_layer, 0, unroll=4)
    rest_out = pltpu.make_async_copy(rest, rest_hbm, store_done.at[0])
    rest_out.start()

    for i, first in ((0, 3), (1, 0)):
        for v in range(2):
            face_out[i, v] = soil[v, pl.ds(first, 128, stride=4), :]
    face_copies = [
        send(
            face_out.at[i],
            face_in.at[i],
            face_sent.at[i],
            face_got.at[i],
            wide_at(1 if i == 0 else -1),
            n,
        )
        for i in range(2)
    ]
    slab_copies = [
        send(
            soil.at[:, pl.ds(480, 32)],
            slab_in.at[0],
            slab_sent.at[0],
            slab_got.at[0],
            w,
            (n + 1) % narrow_count,
        ),
        send(
            soil.at[:, pl.ds(0, 32)],
            slab_in.at[1],
            slab_sent.at[1],
            slab_got.at[1],
            w,
            (n + narrow_count - 1) % narrow_count,
        ),
    ]

    @pl.when(bottom)
    def _():
        flow = soil[1, 480:512, :] * (soil[0, 480:512, :] - aquifer_ref[0:32, :] + 1.0)
        for q in range(4):
            drain[q, 0] = flow[8 * q : 8 * q + 4]
            drain[q, 1] = flow[8 * q + 4 : 8 * q + 8]
            after = flow[8 * q + 8 : 8 * q + 12] if q < 3 else jnp.zeros((4, 128), F32)
            before = flow[8 * q - 4 : 8 * q] if q > 0 else jnp.zeros((4, 128), F32)
            drain[q, 2] = jnp.where(lane4 < 64, after, before)
        for step in (0, 1, -1, 2, -2):
            for q in range(4):
                if step == 0 and q == 3:
                    continue
                send(
                    drain.at[q],
                    drains.at[:, 2 - step],
                    drain_sent.at[step + 2, q],
                    drain_got.at[2 - step],
                    wide_at(step),
                    q,
                )
        drains[:, 2] = drain[3]

    row = iota((32, 128), 0)
    lane = iota((32, 128), 1)
    across_open = jnp.where(row % 4 == 0, 0.0, 0.5)
    along_open = jnp.where((lane == 0) & (row < 4), 0.0, 0.5)

    def previous_column(v):
        moved = roll(v, 1, 1)
        return jnp.where(lane == 0, roll(moved, 4, 0), moved)

    def layer(z):
        at = pl.ds(pl.multiple_of(z * 32, 32), 32)
        return soil[0, at, :], soil[1, at, :]

    def sides(head, cond):
        across = across_open * (roll(cond, 1, 0) + cond) * (roll(head, 1, 0) - head)
        along = along_open * (previous_column(cond) + cond) * (previous_column(head) - head)
        moved = roll(along, -1, 1)
        along_out = jnp.where(lane == 127, roll(moved, -4, 0), moved)
        return (across - roll(across, -1, 0)) + (along - along_out)

    def balance_layer(z, vertical_in):
        head, cond = layer(z)
        head_under, cond_under = layer(z + 1)
        vertical_out = 0.5 * (cond + cond_under) * (head - head_under + 1.0)
        at = pl.ds(pl.multiple_of(z * 32, 32), 32)
        balance = (vertical_in - vertical_out) + sides(head, cond)
        part[at, :] = head + balance * rest[at, :]
        return vertical_out

    vertical_in = lax.fori_loop(0, 15, balance_layer, jnp.zeros((32, 128), F32), unroll=5)
    head, cond = layer(15)
    part[480:512, :] = head + (vertical_in + sides(head, cond)) * rest[480:512, :]

    for copy in slab_copies + face_copies:
        copy.wait_recv()
    head_under = jnp.where(bottom, aquifer_ref[0:32, :], slab_in[1, 0])
    cond_under = jnp.where(bottom, cond, slab_in[1, 1])
    vertical_out = 0.5 * (cond + cond_under) * (head - head_under + 1.0)
    part[480:512, :] = part[480:512, :] - vertical_out * rest[480:512, :]
    head, cond = layer(0)
    top_open = jnp.where(n == 0, 0.0, 0.5)
    vertical_in = top_open * (slab_in[0, 1] + cond) * (slab_in[0, 0] - head + 1.0)
    part[0:32, :] = part[0:32, :] + vertical_in * rest[0:32, :]
    left_open = jnp.where(w == 0, 0.0, 0.5)
    right_open = jnp.where(w == wide_count - 1, 0.0, -0.5)
    for side, first, is_open in ((0, 0, left_open), (1, 3, right_open)):
        head, cond = face_out[1 - side, 0], face_out[1 - side, 1]
        other_head, other_cond = face_in[side, 0], face_in[side, 1]
        jump = other_head - head if side == 0 else head - other_head
        at = pl.ds(first, 128, stride=4)
        part[at, :] = part[at, :] + is_open * (cond + other_cond) * jump * rest[at, :]
    part_out = pltpu.make_async_copy(part, part_hbm, store_done.at[2])
    part_out.start()

    for i, step in enumerate(around):
        pltpu.make_async_remote_copy(
            src_ref=patch,
            dst_ref=patches.at[:, 2 - step],
            send_sem=patch_sent.at[i],
            recv_sem=patch_got.at[i],
            device_id=(w, n),
            device_id_type=MESH,
        ).wait_recv()
    for step in (-2, -1, 0, 1, 2):

        def wait_drain(step=step):
            pltpu.make_async_remote_copy(
                src_ref=drain.at[0],
                dst_ref=drains.at[:, 2 - step],
                send_sem=drain_sent.at[step + 2, 0],
                recv_sem=drain_got.at[2 - step],
                device_id=(w, n),
                device_id_type=MESH,
            ).wait_recv()

        if step == 0:
            pl.when(jnp.logical_not(bottom))(wait_drain)
        else:
            wait_drain()

    lane24 = iota((24, 128), 1)
    line = iota((24, 128), 0) + 4 * w - 8
    inside = jnp.where((line >= 0) & (line < 4 * wide_count), 1.0, 0.0)
    after_open = jnp.where(n < narrow_count - 1, 1.0, 0.0)
    before_open = jnp.where(n > 0, 1.0, 0.0)
    inside_halo = inside * jnp.where(lane24 < 64, after_open, before_open)

    def stacked(ref, a):
        return jnp.concatenate([ref[a, s] for s in range(6)], axis=0)

    heads = [[stacked(patches, 3 * l + t) * inside for t in range(3)] for l in range(3)]
    flows = [stacked(drains, t) for t in range(3)]
    for l in range(3):
        trans = [stacked(patches, 9 + 3 * l + t) * inside for t in range(3)]
        wests, easts = ring_left(trans, lane24), ring_right(trans, lane24)
        for t in range(3):
            centre = trans[t]
            north = 0.5 * (centre + roll(centre, 1, 0))
            south = 0.5 * (centre + roll(centre, -1, 0))
            west = 0.5 * (centre + wests[t])
            east = 0.5 * (centre + easts[t])
            links = 2.0 if l == 1 else 1.0
            divisor = STORAGE + north + south + west + east + LEAKANCE * links
            inverse = (inside_halo if t == 2 else inside) / divisor
            source = STORAGE * heads[l][t]
            if l == 0:
                source = source + flows[t]
            k = 3 * l + t
            coef[0, k] = north * inverse
            coef[1, k] = south * inverse
            coef[2, k] = west * inverse
            coef[3, k] = east * inverse
            coef[4, k] = LEAKANCE * inverse
            coef[5, k] = source * inverse

    def sweep(_, flat):
        now = [flat[3 * l : 3 * l + 3] for l in range(3)]
        later = []
        for l in range(3):
            wests, easts = ring_left(now[l], lane24), ring_right(now[l], lane24)
            for t in range(3):
                k = 3 * l + t
                centre = now[l][t]
                if l == 1:
                    vertical = now[0][t] + now[2][t]
                else:
                    vertical = now[1][t]
                later.append(
                    coef[5, k]
                    + coef[0, k] * roll(centre, 1, 0)
                    + coef[1, k] * roll(centre, -1, 0)
                    + coef[2, k] * wests[t]
                    + coef[3, k] * easts[t]
                    + coef[4, k] * vertical
                )
        return tuple(later)

    flat = lax.fori_loop(0, SWEEPS, sweep, tuple(v for layer in heads for v in layer))
    for l in range(3):
        aquifer_part[8 * l : 8 * l + 8, :] = jnp.concatenate(
            [flat[3 * l][8:12], flat[3 * l + 1][8:12]], axis=0
        )
    aquifer_out = pltpu.make_async_copy(aquifer_part, aquifer_next, store_done.at[3])
    aquifer_out.start()

    def answer_plane(z, carry):
        rows_from(0, PEERS, rows_sent.at[0], rows_got.at[z]).wait_recv()
        return send_plane(z, carry)

    def await_plane(z, carry):
        rows_from(0, PEERS, rows_sent.at[0], rows_got.at[z]).wait_recv()
        return carry

    lax.fori_loop(my_z + 1, depth, answer_plane, 0)
    rows_from(0, PEERS - 1, rows_sent.at[0], rows_got.at[my_z]).wait_recv()
    lax.fori_loop(0, my_z, await_plane, 0)

    for copy in (rest_out, own_rows, part_out, aquifer_out):
        copy.wait()
    for copy in patch_copies + face_copies + slab_copies:
        copy.wait_send()
    rows_from(0, wide_count - 1, rows_sent.at[0], rows_got.at[0]).wait_send()

    @pl.when(bottom)
    def _():
        for step in (0, 1, -1, 2, -2):
            for q in range(4):
                if step == 0 and q == 3:
                    continue
                pltpu.make_async_remote_copy(
                    src_ref=drain.at[q],
                    dst_ref=drains.at[:, 2 - step],
                    send_sem=drain_sent.at[step + 2, q],
                    recv_sem=drain_got.at[2 - step],
                    device_id=(w, n),
                    device_id_type=MESH,
                ).wait_send()


def finish(
    rows_hbm,
    part_hbm,
    rest_hbm,
    aquifer_hbm,
    out_hbm,
    aquifer_out_hbm,
    rows_in,
    part,
    rest,
    out,
    spread,
    slot_lines,
    done,
):
    pairs = ((rows_hbm, rows_in), (part_hbm, part), (rest_hbm, rest), (aquifer_hbm, aquifer_out_hbm))
    loads = [pltpu.make_async_copy(a, b, done.at[i]) for i, (a, b) in enumerate(pairs)]
    for load in loads:
        load.start()
    loads[0].wait()
    slot_lines[...] = rows_in[...].T
    lanes = iota((128, 128), 0).astype(F32)
    rows = iota((32, 128), 0).astype(F32)
    target = jnp.concatenate(
        [
            (lanes == slot_lines[32 * k + 17 : 32 * k + 18, :]).astype(F32).astype(BF16)
            for k in range(CAP)
        ],
        axis=1,
    )
    for k in range(CAP):
        hit = rows == slot_lines[32 * k + 16 : 32 * k + 17, :]

        def place(z, carry, k=k, hit=hit):
            value = slot_lines[pl.ds(32 * k + z, 1), :]
            value = jnp.where(hit, jnp.broadcast_to(value, (32, 128)), 0.0)
            high = value.astype(BF16)
            low = (value - high.astype(F32)).astype(BF16)
            spread[pl.ds(pl.multiple_of(z * 32, 32), 32), 128 * k : 128 * k + 128] = high
            spread[pl.ds(pl.multiple_of(z * 32 + 512, 32), 32), 128 * k : 128 * k + 128] = low
            return carry

        lax.fori_loop(0, 16, place, 0, unroll=4)
    taken = lax.dot_general(spread[...], target, NT, preferred_element_type=F32)
    loads[1].wait()
    loads[2].wait()
    out[...] = part[...] - (taken[:512] + taken[512:]) * rest[...]
    stored = pltpu.make_async_copy(out, out_hbm, done.at[4])
    stored.start()
    loads[3].wait()
    stored.wait()


def rows_of(a):
    k = a.shape[0]
    return a.reshape(k, 4, 8, 128).transpose(0, 2, 1, 3).reshape(k * 32, 128)


def grid_of(a, k, columns):
    return a.reshape(k, columns // 128, 4, 128).transpose(0, 2, 1, 3).reshape(k, 4, columns)


def body(
    pressure_head,
    texture,
    saturated_table,
    shape_table,
    capacity_table,
    uptake,
    root_tile,
    root_column,
    aquifer_head,
    transmissivity,
):
    wide_count = lax.axis_size("wide")
    narrow_count = lax.axis_size("narrow")
    depth = wide_count // PEERS
    dma = pltpu.SemaphoreType.DMA
    hbm = pl.BlockSpec(memory_space=pl.ANY)
    rows_in, part, rest, aquifer_next = pl.pallas_call(
        functools.partial(kernel, wide_count, narrow_count),
        out_shape=(
            jax.ShapeDtypeStruct((wide_count, 1, 128), F32),
            jax.ShapeDtypeStruct((512, 128), F32),
            jax.ShapeDtypeStruct((512, 128), F32),
            jax.ShapeDtypeStruct((24, 128), F32),
        ),
        in_specs=[hbm] * 10,
        out_specs=[hbm] * 4,
        scratch_shapes=[
            pltpu.VMEM((512, 128), F32),
            pltpu.VMEM((512, 128), I32),
            pltpu.VMEM((1, 12), F32),
            pltpu.VMEM((1, 12), F32),
            pltpu.VMEM((1, 12), F32),
            pltpu.VMEM((16, 256), F32),
            pltpu.VMEM((1, 256), I32),
            pltpu.VMEM((1, 256), I32),
            pltpu.VMEM((96, 128), F32),
            pltpu.VMEM((96, 128), F32),
            pltpu.VMEM((24, 128), F32),
            pltpu.VMEM((2, 512, 128), F32),
            pltpu.VMEM((512, 128), F32),
            pltpu.VMEM((512, 128), F32),
            pltpu.VMEM((2, 2, 128, 128), F32),
            pltpu.VMEM((2, 2, 128, 128), F32),
            pltpu.VMEM((2, 2, 32, 128), F32),
            pltpu.VMEM((wide_count, 128), F32),
            pltpu.VMEM((18, 4, 128), F32),
            pltpu.VMEM((18, 6, 4, 128), F32),
            pltpu.VMEM((4, 3, 4, 128), F32),
            pltpu.VMEM((3, 6, 4, 128), F32),
            pltpu.VMEM((6, 9, 24, 128), F32),
            pltpu.VMEM((24, 128), F32),
            dma((4,)),
            dma((10,)),
            dma((1,)),
            dma((depth,)),
            dma((4,)),
            dma((4,)),
            dma((5, 4)),
            dma((5,)),
            dma((2,)),
            dma((2,)),
            dma((2,)),
            dma((2,)),
        ],
        compiler_params=pltpu.CompilerParams(
            collective_id=0, has_side_effects=True, vmem_limit_bytes=60 * 1024 * 1024
        ),
        name="coupled_step",
    )(
        rows_of(pressure_head),
        rows_of(texture),
        saturated_table.reshape(1, -1),
        shape_table.reshape(1, -1),
        capacity_table.reshape(1, -1),
        uptake.T,
        root_tile.reshape(1, -1),
        root_column.reshape(1, -1),
        rows_of(aquifer_head),
        rows_of(transmissivity),
    )
    out, aquifer_out = pl.pallas_call(
        finish,
        out_shape=(
            jax.ShapeDtypeStruct((512, 128), F32),
            jax.ShapeDtypeStruct((24, 128), F32),
        ),
        in_specs=[hbm] * 4,
        out_specs=[hbm] * 2,
        scratch_shapes=[
            pltpu.VMEM((128, 128), F32),
            pltpu.VMEM((512, 128), F32),
            pltpu.VMEM((512, 128), F32),
            pltpu.VMEM((512, 128), F32),
            pltpu.VMEM((1024, 512), BF16),
            pltpu.VMEM((128, 128), F32),
            dma((5,)),
        ],
        compiler_params=pltpu.CompilerParams(vmem_limit_bytes=60 * 1024 * 1024),
        name="finish_step",
    )(rows_in.reshape(128, 128), part, rest, aquifer_next)
    return grid_of(out, 16, 1024), grid_of(aquifer_out, 3, 256)


def solution(mesh):
    in_specs = (
        P("narrow", "wide", None),
        P("narrow", "wide", None),
        P(),
        P(),
        P(),
        P("wide", "narrow"),
        P("wide", None),
        P("wide"),
        P(None, "wide", None),
        P(None, "wide", None),
    )
    out_specs = (P("narrow", "wide", None), P(None, "wide", "narrow"))
    return jax.shard_map(body, mesh=mesh, in_specs=in_specs, out_specs=out_specs, check_vma=False)
```

```python
import functools

import jax
import jax.numpy as jnp
from jax import lax
from jax.experimental import pallas as pl
from jax.experimental.pallas import tpu as pltpu
from jax.sharding import PartitionSpec as P

SWEEPS = 8
TIME_STEP = 0.25
STORAGE = 0.05
LEAKANCE = 0.5
PEERS = 8
CAP = 4
F32, BF16, I32 = jnp.float32, jnp.bfloat16, jnp.int32
MESH = pl.DeviceIdType.MESH
NT = (((1,), (1,)), ((), ()))


def roll(x, shift, axis):
    return pltpu.roll(x, shift % x.shape[axis], axis)


def iota(shape, axis):
    return lax.broadcasted_iota(I32, shape, axis)


def remote(src, dst, send_sem, recv_sem, wide, narrow):
    return pltpu.make_async_remote_copy(
        src_ref=src,
        dst_ref=dst,
        send_sem=send_sem,
        recv_sem=recv_sem,
        device_id=(wide, narrow),
        device_id_type=MESH,
    )


def root_slots(uptake, tile, column):
    cell_row = ((column // 128) % 8) * 4 + column // 1024
    cell_lane = column % 128
    count = tile.shape[1]
    aimed = iota((128, count), 0) == tile
    earlier = iota((count, count), 0) < iota((count, count), 1)
    rank = jnp.dot(
        aimed.astype(F32).astype(BF16),
        earlier.astype(F32).astype(BF16),
        preferred_element_type=F32,
    )
    picks = jnp.concatenate(
        [(aimed & (rank == float(k))).astype(F32).astype(BF16) for k in range(CAP)], axis=0
    )
    high = uptake.astype(BF16)
    low = (uptake - high.astype(F32)).astype(BF16)
    line = iota((16, count), 0)
    extra = jnp.where(
        line == 0,
        cell_row.astype(F32),
        jnp.where(line == 1, cell_lane.astype(F32), 0.0),
    ).astype(BF16)
    base = jnp.concatenate([high, extra, low, jnp.zeros_like(extra)], axis=0)
    spread = lax.dot_general(base, picks, NT, preferred_element_type=F32)
    rows = spread[:32] + spread[32:]
    slots = jnp.concatenate([rows[:, 128 * k : 128 * (k + 1)] for k in range(CAP)], axis=0)
    return slots.T


def ring_left(tiles, lane):
    moved = [roll(v, 1, 1) for v in tiles]
    return [jnp.where(lane == 0, moved[t - 1], moved[t]) for t in range(len(tiles))]


def ring_right(tiles, lane):
    moved = [roll(v, -1, 1) for v in tiles]
    return [
        jnp.where(lane == 127, moved[(t + 1) % len(tiles)], moved[t]) for t in range(len(tiles))
    ]


def kernel(
    wide_count,
    narrow_count,
    head_hbm,
    texture_hbm,
    saturated_hbm,
    shape_hbm,
    capacity_hbm,
    uptake_hbm,
    tile_hbm,
    column_hbm,
    aquifer_hbm,
    trans_hbm,
    rows,
    part_hbm,
    rest_hbm,
    aquifer_next,
    head_ref,
    texture_ref,
    saturated_ref,
    shape_ref,
    capacity_ref,
    uptake_ref,
    tile_ref,
    column_ref,
    aquifer_ref,
    trans_ref,
    table,
    soil,
    rest,
    part,
    face_out,
    face_in,
    slab_in,
    slots,
    patch,
    patches,
    drain,
    drains,
    coef,
    aquifer_part,
    store_done,
    load_done,
    rows_sent,
    rows_got,
    patch_sent,
    patch_got,
    drain_sent,
    drain_got,
    face_sent,
    face_got,
    slab_sent,
    slab_got,
):
    w = lax.axis_index("wide")
    n = lax.axis_index("narrow")
    depth = wide_count // PEERS
    my_z, my_peer = w // PEERS, w % PEERS
    bottom = n == narrow_count - 1
    around = (-2, -1, 1, 2)

    def exists(step):
        return (w + step >= 0) & (w + step < wide_count)

    barrier = pltpu.get_barrier_semaphore()

    def greet(wide, narrow):
        pl.semaphore_signal(barrier, inc=1, device_id=(wide, narrow), device_id_type=MESH)

    peers = [(my_peer + j) % PEERS for j in range(1, PEERS + 1)]

    def greet_plane(z, carry):
        for peer in peers:
            greet(z * PEERS + peer, n)
        return carry

    lax.fori_loop(my_z + 1, depth, greet_plane, 0)
    for peer in peers[:-1]:
        greet(my_z * PEERS + peer, n)
    greeted = PEERS * my_z + PEERS - 1 + 2
    for step in around:
        plane = (w + step + PEERS) // PEERS - 1
        greeted = greeted + jnp.where(exists(step) & (plane > my_z), 1, 0)

        @pl.when(exists(step) & (plane < my_z))
        def _(step=step):
            greet(w + step, n)

    greet(w, (n + 1) % narrow_count)
    greet(w, (n + narrow_count - 1) % narrow_count)

    for step in (-2, -1, 0, 1, 2):

        @pl.when(jnp.logical_not(bottom) & exists(step))
        def _(step=step):
            greet(w + step, narrow_count - 1)

    order = (6, 7, 5, 0, 1, 2, 3, 4, 8, 9)
    held = (head_ref, texture_ref, saturated_ref, shape_ref, capacity_ref, uptake_ref, tile_ref)
    held += (column_ref, aquifer_ref, trans_ref)
    far = (head_hbm, texture_hbm, saturated_hbm, shape_hbm, capacity_hbm, uptake_hbm, tile_hbm)
    far += (column_hbm, aquifer_hbm, trans_hbm)
    loads = [pltpu.make_async_copy(far[i], held[i], load_done.at[i]) for i in range(10)]
    for i in order:
        loads[i].start()
    for i in (6, 7, 5):
        loads[i].wait()

    made = root_slots(
        uptake_ref[...],
        tile_ref[...],
        column_ref[...],
    )
    slots[...] = made

    for i in (8, 9):
        loads[i].wait()
    lane4 = iota((4, 128), 1)
    for a in range(6):
        source = aquifer_ref if a < 3 else trans_ref
        first = (a % 3) * 32
        here = source[pl.ds(pl.multiple_of(first + 8 * n, 8), 8), :]
        after = source[pl.ds(pl.multiple_of(first + 8 * jnp.minimum(n + 1, 3), 8), 8), :]
        before = source[pl.ds(pl.multiple_of(first + 8 * jnp.maximum(n - 1, 0), 8), 8), :]
        after = jnp.where(n < narrow_count - 1, after[0:4], 0.0)
        before = jnp.where(n > 0, before[4:8], 0.0)
        patch[3 * a] = here[0:4]
        patch[3 * a + 1] = here[4:8]
        patch[3 * a + 2] = jnp.where(lane4 < 64, after, before)
    for a in range(18):
        patches[a, 2] = patch[a]
        patches[a, 5] = jnp.zeros((4, 128), F32)
    for t in range(3):
        drains[t, 5] = jnp.zeros((4, 128), F32)

    for i in (0, 1, 2, 3, 4):
        loads[i].wait()
    table[...] = jnp.zeros_like(table)
    table[0:1, 0:12] = saturated_ref[...]
    table[8:9, 0:12] = shape_ref[...]
    table[16:17, 0:12] = capacity_ref[...]

    def look_up(row, index):
        values = jnp.broadcast_to(table[row : row + 1, :], index.shape)
        return jnp.take_along_axis(values, index, axis=1, mode="promise_in_bounds")

    def conduct_layer(z, carry):
        here = pl.ds(pl.multiple_of(z * 32, 32), 32)
        head = head_ref[here, :]
        index = texture_ref[here, :]
        soil[0, here, :] = head
        soil[1, here, :] = look_up(0, index) * jnp.exp(look_up(8, index) * jnp.minimum(head, 0.0))
        rest[here, :] = TIME_STEP / look_up(16, index)
        return carry

    lax.fori_loop(0, 16, conduct_layer, 0, unroll=4)
    rest_out = pltpu.make_async_copy(rest, rest_hbm, store_done.at[0])
    rest_out.start()

    for i, first in ((0, 3), (1, 0)):
        for v in range(2):
            face_out[i, v] = soil[v, pl.ds(first, 128, stride=4), :]
    @pl.when(bottom)
    def _():
        flow = soil[1, 480:512, :] * (soil[0, 480:512, :] - aquifer_ref[0:32, :] + 1.0)
        for q in range(4):
            drain[q, 0] = flow[8 * q : 8 * q + 4]
            drain[q, 1] = flow[8 * q + 4 : 8 * q + 8]
            after = flow[8 * q + 8 : 8 * q + 12] if q < 3 else jnp.zeros((4, 128), F32)
            before = flow[8 * q - 4 : 8 * q] if q > 0 else jnp.zeros((4, 128), F32)
            drain[q, 2] = jnp.where(lane4 < 64, after, before)
        drains[:, 2] = drain[3]

    near_tiles = sum(jnp.where(exists(step), 1, 0) for step in (-2, -1, 0, 1, 2))
    greeted = greeted + jnp.where(bottom, (narrow_count - 1) * near_tiles, 0)
    pl.semaphore_wait(barrier, greeted)

    def send_rows(tile):
        remote(
            slots.at[pl.ds(tile, 1)], rows.at[w], rows_sent.at[0], rows_got.at[my_z], tile, n
        ).start()

    def rows_from(count, z):
        at = rows.at[pl.ds(0, count)]
        return remote(at, at, rows_sent.at[0], rows_got.at[z], w, n)

    def send_plane(z, carry):
        for peer in peers:
            send_rows(z * PEERS + peer)
        return carry

    lax.fori_loop(0, my_z, send_plane, 0)
    for peer in peers[:-1]:
        send_rows(my_z * PEERS + peer)
    own_rows = pltpu.make_async_copy(slots.at[pl.ds(w, 1)], rows.at[w], store_done.at[1])
    own_rows.start()

    def answer_plane(z, carry):
        rows_from(PEERS, z).wait_recv()
        return send_plane(z, carry)

    def await_plane(z, carry):
        rows_from(PEERS, z).wait_recv()
        return carry

    face_copies = [
        remote(face_out.at[i], face_in.at[i], face_sent.at[i], face_got.at[i], w + step, n)
        for i, step in ((0, 1), (1, -1))
    ]
    for copy, step in zip(face_copies, (1, -1)):
        pl.when(exists(step))(copy.start)
    slab_copies = [
        remote(
            soil.at[:, pl.ds(first, 32)],
            slab_in.at[i],
            slab_sent.at[i],
            slab_got.at[i],
            w,
            (n + step) % narrow_count,
        )
        for i, first, step in ((0, 480, 1), (1, 0, narrow_count - 1))
    ]
    for copy in slab_copies:
        copy.start()
    patch_copies = [
        remote(patch, patches.at[:, 2 - step], patch_sent.at[i], patch_got.at[i], w + step, n)
        for i, step in enumerate(around)
    ]
    for copy, step in zip(patch_copies, around):
        pl.when(exists(step))(copy.start)

    def drain_copy(step, q):
        return remote(
            drain.at[q],
            drains.at[:, 2 - step],
            drain_sent.at[step + 2, q],
            drain_got.at[2 - step],
            w + step,
            q,
        )

    def each_drain(act):
        for step in (0, 1, -1, 2, -2):

            @pl.when(bottom & exists(step))
            def _(step=step):
                for q in range(narrow_count - 1 if step == 0 else narrow_count):
                    act(drain_copy(step, q))

    each_drain(lambda copy: copy.start())

    def answer():
        lax.fori_loop(my_z + 1, depth, answer_plane, 0)

    row = iota((32, 128), 0)
    lane = iota((32, 128), 1)
    across_open = jnp.where(row % 4 == 0, 0.0, 0.5)
    along_open = jnp.where((lane == 0) & (row < 4), 0.0, 0.5)

    def previous_column(v):
        moved = roll(v, 1, 1)
        return jnp.where(lane == 0, roll(moved, 4, 0), moved)

    def layer(z):
        at = pl.ds(pl.multiple_of(z * 32, 32), 32)
        return soil[0, at, :], soil[1, at, :]

    def sides(head, cond):
        across = across_open * (roll(cond, 1, 0) + cond) * (roll(head, 1, 0) - head)
        along = along_open * (previous_column(cond) + cond) * (previous_column(head) - head)
        moved = roll(along, -1, 1)
        along_out = jnp.where(lane == 127, roll(moved, -4, 0), moved)
        return (across - roll(across, -1, 0)) + (along - along_out)

    def balance_layer(z, vertical_in):
        head, cond = layer(z)
        head_under, cond_under = layer(z + 1)
        vertical_out = 0.5 * (cond + cond_under) * (head - head_under + 1.0)
        at = pl.ds(pl.multiple_of(z * 32, 32), 32)
        balance = (vertical_in - vertical_out) + sides(head, cond)
        part[at, :] = head + balance * rest[at, :]
        return vertical_out

    vertical_in = lax.fori_loop(0, 15, balance_layer, jnp.zeros((32, 128), F32), unroll=5)
    head, cond = layer(15)
    part[480:512, :] = head + (vertical_in + sides(head, cond)) * rest[480:512, :]

    pl.when(my_z >= depth // 2)(answer)

    for copy in slab_copies:
        copy.wait_recv()
    for copy, step in zip(face_copies, (1, -1)):
        pl.when(exists(-step))(copy.wait_recv)
    head_under = jnp.where(bottom, aquifer_ref[0:32, :], slab_in[1, 0])
    cond_under = jnp.where(bottom, cond, slab_in[1, 1])
    vertical_out = 0.5 * (cond + cond_under) * (head - head_under + 1.0)
    part[480:512, :] = part[480:512, :] - vertical_out * rest[480:512, :]
    head, cond = layer(0)
    top_open = jnp.where(n == 0, 0.0, 0.5)
    vertical_in = top_open * (slab_in[0, 1] + cond) * (slab_in[0, 0] - head + 1.0)
    part[0:32, :] = part[0:32, :] + vertical_in * rest[0:32, :]
    for side, first, factor, is_open in ((0, 0, 0.5, exists(-1)), (1, 3, -0.5, exists(1))):
        head, cond = face_out[1 - side, 0], face_out[1 - side, 1]
        other_head, other_cond = face_in[side, 0], face_in[side, 1]
        jump = other_head - head if side == 0 else head - other_head
        at = pl.ds(first, 128, stride=4)
        flow = jnp.where(is_open, factor * (cond + other_cond) * jump, 0.0)
        part[at, :] = part[at, :] + flow * rest[at, :]
    part_out = pltpu.make_async_copy(part, part_hbm, store_done.at[2])
    part_out.start()

    for copy, step in zip(patch_copies, around):
        pl.when(exists(-step))(copy.wait_recv)
    for step in (-2, -1, 0, 1, 2):
        needed = exists(-step) & jnp.logical_not(bottom) if step == 0 else exists(-step)
        pl.when(needed)(drain_copy(step, 0).wait_recv)

    lane24 = iota((24, 128), 1)
    line = iota((24, 128), 0) + 4 * w - 8
    real = (line >= 0) & (line < 4 * wide_count)
    inside = jnp.where(real, 1.0, 0.0)
    after_open = jnp.where(n < narrow_count - 1, 1.0, 0.0)
    before_open = jnp.where(n > 0, 1.0, 0.0)
    inside_halo = inside * jnp.where(lane24 < 64, after_open, before_open)

    def stacked(ref, a):
        return jnp.where(real, jnp.concatenate([ref[a, s] for s in range(6)], axis=0), 0.0)

    heads = [[stacked(patches, 3 * l + t) for t in range(3)] for l in range(3)]
    flows = [stacked(drains, t) for t in range(3)]
    for l in range(3):
        trans = [stacked(patches, 9 + 3 * l + t) for t in range(3)]
        wests, easts = ring_left(trans, lane24), ring_right(trans, lane24)
        for t in range(3):
            centre = trans[t]
            north = 0.5 * (centre + roll(centre, 1, 0))
            south = 0.5 * (centre + roll(centre, -1, 0))
            west = 0.5 * (centre + wests[t])
            east = 0.5 * (centre + easts[t])
            links = 2.0 if l == 1 else 1.0
            divisor = STORAGE + north + south + west + east + LEAKANCE * links
            inverse = (inside_halo if t == 2 else inside) / divisor
            source = STORAGE * heads[l][t]
            if l == 0:
                source = source + flows[t]
            k = 3 * l + t
            coef[0, k] = north * inverse
            coef[1, k] = south * inverse
            coef[2, k] = west * inverse
            coef[3, k] = east * inverse
            coef[4, k] = LEAKANCE * inverse
            coef[5, k] = source * inverse

    def sweep(_, flat):
        now = [flat[3 * l : 3 * l + 3] for l in range(3)]
        later = []
        for l in range(3):
            wests, easts = ring_left(now[l], lane24), ring_right(now[l], lane24)
            for t in range(3):
                k = 3 * l + t
                centre = now[l][t]
                if l == 1:
                    vertical = now[0][t] + now[2][t]
                else:
                    vertical = now[1][t]
                later.append(
                    coef[5, k]
                    + coef[0, k] * roll(centre, 1, 0)
                    + coef[1, k] * roll(centre, -1, 0)
                    + coef[2, k] * wests[t]
                    + coef[3, k] * easts[t]
                    + coef[4, k] * vertical
                )
        return tuple(later)

    flat = lax.fori_loop(0, SWEEPS, sweep, tuple(v for layer in heads for v in layer))
    for l in range(3):
        aquifer_part[8 * l : 8 * l + 8, :] = jnp.concatenate(
            [flat[3 * l][8:12], flat[3 * l + 1][8:12]], axis=0
        )
    aquifer_out = pltpu.make_async_copy(aquifer_part, aquifer_next, store_done.at[3])
    aquifer_out.start()

    pl.when(my_z < depth // 2)(answer)
    rows_from(PEERS - 1, my_z).wait_recv()
    lax.fori_loop(0, my_z, await_plane, 0)

    for copy in (rest_out, own_rows, part_out, aquifer_out):
        copy.wait()
    for copy in slab_copies:
        copy.wait_send()
    for copy, step in zip(patch_copies + face_copies, around + (1, -1)):
        pl.when(exists(step))(copy.wait_send)
    each_drain(lambda copy: copy.wait_send())
    rows_from(wide_count - 1, 0).wait_send()


def finish(
    rows_hbm,
    part_hbm,
    rest_hbm,
    aquifer_hbm,
    out_hbm,
    aquifer_out_hbm,
    rows_in,
    part,
    rest,
    out,
    spread,
    slot_lines,
    done,
):
    pairs = ((rows_hbm, rows_in), (part_hbm, part), (rest_hbm, rest), (aquifer_hbm, aquifer_out_hbm))
    loads = [pltpu.make_async_copy(a, b, done.at[i]) for i, (a, b) in enumerate(pairs)]
    for load in loads:
        load.start()
    loads[0].wait()
    slot_lines[...] = rows_in[...].T
    lanes = iota((128, 128), 0).astype(F32)
    rows = iota((32, 128), 0).astype(F32)
    target = jnp.concatenate(
        [
            (lanes == slot_lines[32 * k + 17 : 32 * k + 18, :]).astype(F32).astype(BF16)
            for k in range(CAP)
        ],
        axis=1,
    )
    hits = [rows == slot_lines[32 * k + 16 : 32 * k + 17, :] for k in range(CAP)]
    loads[1].wait()
    loads[2].wait()
    stores = []
    for i in range(4):
        for layer in range(4):
            for k in range(CAP):
                line = 32 * k + 4 * i + layer
                value = jnp.broadcast_to(slot_lines[line : line + 1, :], (32, 128))
                value = jnp.where(hits[k], value, 0.0)
                high = value.astype(BF16)
                low = (value - high.astype(F32)).astype(BF16)
                spread[i, 32 * layer : 32 * layer + 32, 128 * k : 128 * k + 128] = high
                spread[i, 32 * layer + 128 : 32 * layer + 160, 128 * k : 128 * k + 128] = low
        taken = lax.dot_general(spread[i], target, NT, preferred_element_type=F32)
        at = pl.ds(128 * i, 128)
        out[at, :] = part[at, :] - (taken[:128] + taken[128:]) * rest[at, :]
        stores.append(pltpu.make_async_copy(out.at[at], out_hbm.at[at], done.at[4 + i]))
        stores[i].start()
    loads[3].wait()
    for store in stores:
        store.wait()


def rows_of(a):
    k = a.shape[0]
    return a.reshape(k, 4, 8, 128).transpose(0, 2, 1, 3).reshape(k * 32, 128)


def grid_of(a, k, columns):
    return a.reshape(k, columns // 128, 4, 128).transpose(0, 2, 1, 3).reshape(k, 4, columns)


def body(
    pressure_head,
    texture,
    saturated_table,
    shape_table,
    capacity_table,
    uptake,
    root_tile,
    root_column,
    aquifer_head,
    transmissivity,
):
    wide_count = lax.axis_size("wide")
    narrow_count = lax.axis_size("narrow")
    depth = wide_count // PEERS
    dma = pltpu.SemaphoreType.DMA
    hbm = pl.BlockSpec(memory_space=pl.ANY)
    rows_in, part, rest, aquifer_next = pl.pallas_call(
        functools.partial(kernel, wide_count, narrow_count),
        out_shape=(
            jax.ShapeDtypeStruct((wide_count, 1, 128), F32),
            jax.ShapeDtypeStruct((512, 128), F32),
            jax.ShapeDtypeStruct((512, 128), F32),
            jax.ShapeDtypeStruct((24, 128), F32),
        ),
        in_specs=[hbm] * 10,
        out_specs=[hbm] * 4,
        scratch_shapes=[
            pltpu.VMEM((512, 128), F32),
            pltpu.VMEM((512, 128), I32),
            pltpu.VMEM((1, 12), F32),
            pltpu.VMEM((1, 12), F32),
            pltpu.VMEM((1, 12), F32),
            pltpu.VMEM((16, 256), F32),
            pltpu.VMEM((1, 256), I32),
            pltpu.VMEM((1, 256), I32),
            pltpu.VMEM((96, 128), F32),
            pltpu.VMEM((96, 128), F32),
            pltpu.VMEM((24, 128), F32),
            pltpu.VMEM((2, 512, 128), F32),
            pltpu.VMEM((512, 128), F32),
            pltpu.VMEM((512, 128), F32),
            pltpu.VMEM((2, 2, 128, 128), F32),
            pltpu.VMEM((2, 2, 128, 128), F32),
            pltpu.VMEM((2, 2, 32, 128), F32),
            pltpu.VMEM((wide_count, 128), F32),
            pltpu.VMEM((18, 4, 128), F32),
            pltpu.VMEM((18, 6, 4, 128), F32),
            pltpu.VMEM((4, 3, 4, 128), F32),
            pltpu.VMEM((3, 6, 4, 128), F32),
            pltpu.VMEM((6, 9, 24, 128), F32),
            pltpu.VMEM((24, 128), F32),
            dma((4,)),
            dma((10,)),
            dma((1,)),
            dma((depth,)),
            dma((4,)),
            dma((4,)),
            dma((5, 4)),
            dma((5,)),
            dma((2,)),
            dma((2,)),
            dma((2,)),
            dma((2,)),
        ],
        compiler_params=pltpu.CompilerParams(
            collective_id=0, has_side_effects=True, vmem_limit_bytes=60 * 1024 * 1024
        ),
        name="coupled_step",
    )(
        rows_of(pressure_head),
        rows_of(texture),
        saturated_table.reshape(1, -1),
        shape_table.reshape(1, -1),
        capacity_table.reshape(1, -1),
        uptake.T,
        root_tile.reshape(1, -1),
        root_column.reshape(1, -1),
        rows_of(aquifer_head),
        rows_of(transmissivity),
    )
    out, aquifer_out = pl.pallas_call(
        finish,
        out_shape=(
            jax.ShapeDtypeStruct((512, 128), F32),
            jax.ShapeDtypeStruct((24, 128), F32),
        ),
        in_specs=[hbm] * 4,
        out_specs=[hbm] * 2,
        scratch_shapes=[
            pltpu.VMEM((128, 128), F32),
            pltpu.VMEM((512, 128), F32),
            pltpu.VMEM((512, 128), F32),
            pltpu.VMEM((512, 128), F32),
            pltpu.VMEM((4, 256, 512), BF16),
            pltpu.VMEM((128, 128), F32),
            dma((8,)),
        ],
        compiler_params=pltpu.CompilerParams(vmem_limit_bytes=60 * 1024 * 1024),
        name="finish_step",
    )(rows_in.reshape(128, 128), part, rest, aquifer_next)
    return grid_of(out, 16, 1024), grid_of(aquifer_out, 3, 256)


def solution(mesh):
    in_specs = (
        P("narrow", "wide", None),
        P("narrow", "wide", None),
        P(),
        P(),
        P(),
        P("wide", "narrow"),
        P("wide", None),
        P("wide"),
        P(None, "wide", None),
        P(None, "wide", None),
    )
    out_specs = (P("narrow", "wide", None), P(None, "wide", "narrow"))
    return jax.shard_map(body, mesh=mesh, in_specs=in_specs, out_specs=out_specs, check_vma=False)
```

```python
import functools

import jax
import jax.numpy as jnp
from jax import lax
from jax.experimental import pallas as pl
from jax.experimental.pallas import tpu as pltpu
from jax.sharding import PartitionSpec as P

SWEEPS = 8
TIME_STEP = 0.25
STORAGE = 0.05
LEAKANCE = 0.5
PEERS = 8
CAP = 4
F32, BF16, I32 = jnp.float32, jnp.bfloat16, jnp.int32
MESH = pl.DeviceIdType.MESH
NT = (((1,), (1,)), ((), ()))


def roll(x, shift, axis):
    return pltpu.roll(x, shift % x.shape[axis], axis)


def iota(shape, axis):
    return lax.broadcasted_iota(I32, shape, axis)


def remote(src, dst, send_sem, recv_sem, wide, narrow):
    return pltpu.make_async_remote_copy(
        src_ref=src,
        dst_ref=dst,
        send_sem=send_sem,
        recv_sem=recv_sem,
        device_id=(wide, narrow),
        device_id_type=MESH,
    )


def root_slots(uptake, tile, column):
    cell_row = ((column // 128) % 8) * 4 + column // 1024
    cell_lane = column % 128
    count = tile.shape[1]
    aimed = iota((128, count), 0) == tile
    earlier = iota((count, count), 0) < iota((count, count), 1)
    rank = jnp.dot(
        aimed.astype(F32).astype(BF16),
        earlier.astype(F32).astype(BF16),
        preferred_element_type=F32,
    )
    picks = jnp.concatenate(
        [(aimed & (rank == float(k))).astype(F32).astype(BF16) for k in range(CAP)], axis=0
    )
    high = uptake.astype(BF16)
    low = (uptake - high.astype(F32)).astype(BF16)
    line = iota((16, count), 0)
    extra = jnp.where(
        line == 0,
        cell_row.astype(F32),
        jnp.where(line == 1, cell_lane.astype(F32), 0.0),
    ).astype(BF16)
    base = jnp.concatenate([high, extra, low, jnp.zeros_like(extra)], axis=0)
    spread = lax.dot_general(base, picks, NT, preferred_element_type=F32)
    rows = spread[:32] + spread[32:]
    slots = jnp.concatenate([rows[:, 128 * k : 128 * (k + 1)] for k in range(CAP)], axis=0)
    return slots.T


def ring_left(tiles, lane):
    moved = [roll(v, 1, 1) for v in tiles]
    return [jnp.where(lane == 0, moved[t - 1], moved[t]) for t in range(len(tiles))]


def ring_right(tiles, lane):
    moved = [roll(v, -1, 1) for v in tiles]
    return [
        jnp.where(lane == 127, moved[(t + 1) % len(tiles)], moved[t]) for t in range(len(tiles))
    ]


def kernel(
    wide_count,
    narrow_count,
    head_hbm,
    texture_hbm,
    saturated_hbm,
    shape_hbm,
    capacity_hbm,
    uptake_hbm,
    tile_hbm,
    column_hbm,
    aquifer_hbm,
    trans_hbm,
    rows,
    part_hbm,
    rest_hbm,
    aquifer_next,
    head_ref,
    texture_ref,
    saturated_ref,
    shape_ref,
    capacity_ref,
    uptake_ref,
    tile_ref,
    column_ref,
    aquifer_ref,
    trans_ref,
    table,
    soil,
    rest,
    part,
    face_out,
    face_in,
    slab_in,
    slots,
    by_peer,
    plane_rows,
    by_plane,
    patch,
    patches,
    drain,
    drains,
    coef,
    aquifer_part,
    store_done,
    load_done,
    rows_sent,
    rows_got,
    answers_sent,
    plane_sent,
    plane_got,
    patch_sent,
    patch_got,
    drain_sent,
    drain_got,
    face_sent,
    face_got,
    slab_sent,
    slab_got,
):
    w = lax.axis_index("wide")
    n = lax.axis_index("narrow")
    depth = wide_count // PEERS
    my_z, my_peer = w // PEERS, w % PEERS
    bottom = n == narrow_count - 1
    around = (-2, -1, 1, 2)

    def exists(step):
        return (w + step >= 0) & (w + step < wide_count)

    barrier = pltpu.get_barrier_semaphore()

    def greet(wide, narrow):
        pl.semaphore_signal(barrier, inc=1, device_id=(wide, narrow), device_id_type=MESH)

    peers = [(my_peer + j) % PEERS for j in range(1, PEERS + 1)]

    def plane_at(k):
        return (my_z + depth // 2 + ((k + 1) // 2) * (1 - 2 * (k % 2)) + depth) % depth

    def greet_plane(k, carry):
        z = plane_at(k)

        @pl.when(z > my_z)
        def _():
            for peer in peers:
                greet(z * PEERS + peer, n)

        return carry

    lax.fori_loop(0, depth - 1, greet_plane, 0)
    for peer in peers[:-1]:
        greet(my_z * PEERS + peer, n)
    greeted = PEERS * my_z + PEERS - 1 + 2
    for step in around:
        plane = (w + step + PEERS) // PEERS - 1
        greeted = greeted + jnp.where(exists(step) & (plane > my_z), 1, 0)

        @pl.when(exists(step) & (plane < my_z))
        def _(step=step):
            greet(w + step, n)

    greet(w, (n + 1) % narrow_count)
    greet(w, (n + narrow_count - 1) % narrow_count)

    for step in (-2, -1, 0, 1, 2):

        @pl.when(jnp.logical_not(bottom) & exists(step))
        def _(step=step):
            greet(w + step, narrow_count - 1)

    order = (6, 7, 5, 0, 1, 2, 3, 4, 8, 9)
    held = (head_ref, texture_ref, saturated_ref, shape_ref, capacity_ref, uptake_ref, tile_ref)
    held += (column_ref, aquifer_ref, trans_ref)
    far = (head_hbm, texture_hbm, saturated_hbm, shape_hbm, capacity_hbm, uptake_hbm, tile_hbm)
    far += (column_hbm, aquifer_hbm, trans_hbm)
    loads = [pltpu.make_async_copy(far[i], held[i], load_done.at[i]) for i in range(10)]
    for i in order:
        loads[i].start()
    for i in (6, 7, 5):
        loads[i].wait()

    made = root_slots(
        uptake_ref[...],
        tile_ref[...],
        column_ref[...],
    )
    slots[...] = made
    for z in range(depth):
        for p in range(PEERS):
            by_peer[p, z : z + 1] = slots[z * PEERS + p : z * PEERS + p + 1]

    for i in (8, 9):
        loads[i].wait()
    lane4 = iota((4, 128), 1)
    for a in range(6):
        source = aquifer_ref if a < 3 else trans_ref
        first = (a % 3) * 32
        here = source[pl.ds(pl.multiple_of(first + 8 * n, 8), 8), :]
        after = source[pl.ds(pl.multiple_of(first + 8 * jnp.minimum(n + 1, 3), 8), 8), :]
        before = source[pl.ds(pl.multiple_of(first + 8 * jnp.maximum(n - 1, 0), 8), 8), :]
        after = jnp.where(n < narrow_count - 1, after[0:4], 0.0)
        before = jnp.where(n > 0, before[4:8], 0.0)
        patch[3 * a] = here[0:4]
        patch[3 * a + 1] = here[4:8]
        patch[3 * a + 2] = jnp.where(lane4 < 64, after, before)
    for a in range(18):
        patches[a, 2] = patch[a]
        patches[a, 5] = jnp.zeros((4, 128), F32)
    for t in range(3):
        drains[t, 5] = jnp.zeros((4, 128), F32)

    for i in (0, 1, 2, 3, 4):
        loads[i].wait()
    table[...] = jnp.zeros_like(table)
    table[0:1, 0:12] = saturated_ref[...]
    table[8:9, 0:12] = shape_ref[...]
    table[16:17, 0:12] = capacity_ref[...]

    def look_up(row, index):
        values = jnp.broadcast_to(table[row : row + 1, :], index.shape)
        return jnp.take_along_axis(values, index, axis=1, mode="promise_in_bounds")

    def conduct_layer(z, carry):
        here = pl.ds(pl.multiple_of(z * 32, 32), 32)
        head = head_ref[here, :]
        index = texture_ref[here, :]
        soil[0, here, :] = head
        soil[1, here, :] = look_up(0, index) * jnp.exp(look_up(8, index) * jnp.minimum(head, 0.0))
        rest[here, :] = TIME_STEP / look_up(16, index)
        return carry

    lax.fori_loop(0, 16, conduct_layer, 0, unroll=4)
    rest_out = pltpu.make_async_copy(rest, rest_hbm, store_done.at[0])
    rest_out.start()

    for i, first in ((0, 3), (1, 0)):
        for v in range(2):
            face_out[i, v] = soil[v, pl.ds(first, 128, stride=4), :]
    @pl.when(bottom)
    def _():
        flow = soil[1, 480:512, :] * (soil[0, 480:512, :] - aquifer_ref[0:32, :] + 1.0)
        for q in range(4):
            drain[q, 0] = flow[8 * q : 8 * q + 4]
            drain[q, 1] = flow[8 * q + 4 : 8 * q + 8]
            after = flow[8 * q + 8 : 8 * q + 12] if q < 3 else jnp.zeros((4, 128), F32)
            before = flow[8 * q - 4 : 8 * q] if q > 0 else jnp.zeros((4, 128), F32)
            drain[q, 2] = jnp.where(lane4 < 64, after, before)
        drains[:, 2] = drain[3]

    near_tiles = sum(jnp.where(exists(step), 1, 0) for step in (-2, -1, 0, 1, 2))
    greeted = greeted + jnp.where(bottom, (narrow_count - 1) * near_tiles, 0)
    pl.semaphore_wait(barrier, greeted)

    def send_rows(tile):
        remote(
            slots.at[pl.ds(tile, 1)], rows.at[pl.ds(w, 1)], rows_sent.at[0], rows_got.at[my_z], tile, n
        ).start()

    def rows_from(count, z):
        at = rows.at[pl.ds(0, count)]
        return remote(at, at, rows_sent.at[0], rows_got.at[z], w, n)

    def send_plane(k, carry):
        z = plane_at(k)

        @pl.when(z < my_z)
        def _():
            for peer in peers:
                send_rows(z * PEERS + peer)

        return carry

    lax.fori_loop(0, depth - 1, send_plane, 0)

    plane_copies = [
        remote(
            by_peer.at[peer],
            plane_rows.at[my_peer],
            plane_sent.at[j],
            plane_got.at[j],
            my_z * PEERS + peer,
            n,
        )
        for j, peer in enumerate(peers[:-1])
    ]
    for copy in plane_copies:
        copy.start()

    def rows_to(z):
        return (by_plane.at[z], rows.at[pl.ds(my_z * PEERS, PEERS)])

    def answer_plane(z, carry):
        rows_from(PEERS, z).wait_recv()
        to = z * PEERS + my_peer
        remote(*rows_to(z), answers_sent.at[0], rows_got.at[my_z], to, n).start()
        return carry

    def await_plane(z, carry):
        rows_from(PEERS, z).wait_recv()
        return carry

    face_copies = [
        remote(face_out.at[i], face_in.at[i], face_sent.at[i], face_got.at[i], w + step, n)
        for i, step in ((0, 1), (1, -1))
    ]
    for copy, step in zip(face_copies, (1, -1)):
        pl.when(exists(step))(copy.start)
    slab_copies = [
        remote(
            soil.at[:, pl.ds(first, 32)],
            slab_in.at[i],
            slab_sent.at[i],
            slab_got.at[i],
            w,
            (n + step) % narrow_count,
        )
        for i, first, step in ((0, 480, 1), (1, 0, narrow_count - 1))
    ]
    for copy in slab_copies:
        copy.start()
    patch_copies = [
        remote(patch, patches.at[:, 2 - step], patch_sent.at[i], patch_got.at[i], w + step, n)
        for i, step in enumerate(around)
    ]
    for copy, step in zip(patch_copies, around):
        pl.when(exists(step))(copy.start)

    def drain_copy(step, q):
        return remote(
            drain.at[q],
            drains.at[:, 2 - step],
            drain_sent.at[step + 2, q],
            drain_got.at[2 - step],
            w + step,
            q,
        )

    def each_drain(act):
        for step in (0, 1, -1, 2, -2):

            @pl.when(bottom & exists(step))
            def _(step=step):
                for q in range(narrow_count - 1 if step == 0 else narrow_count):
                    act(drain_copy(step, q))

    each_drain(lambda copy: copy.start())

    def answer():
        lax.fori_loop(my_z + 1, depth, answer_plane, 0)

    def regroup():
        for copy in plane_copies:
            copy.wait_recv()
        plane_rows[my_peer] = by_peer[my_peer]
        for z in range(depth):
            for p in range(PEERS):
                by_plane[z, p : p + 1] = plane_rows[p, z : z + 1]
        own = pltpu.make_async_copy(*rows_to(my_z), store_done.at[1])
        own.start()
        return own

    row = iota((32, 128), 0)
    lane = iota((32, 128), 1)
    across_open = jnp.where(row % 4 == 0, 0.0, 0.5)
    along_open = jnp.where((lane == 0) & (row < 4), 0.0, 0.5)

    def previous_column(v):
        moved = roll(v, 1, 1)
        return jnp.where(lane == 0, roll(moved, 4, 0), moved)

    def layer(z):
        at = pl.ds(pl.multiple_of(z * 32, 32), 32)
        return soil[0, at, :], soil[1, at, :]

    def sides(head, cond):
        across = across_open * (roll(cond, 1, 0) + cond) * (roll(head, 1, 0) - head)
        along = along_open * (previous_column(cond) + cond) * (previous_column(head) - head)
        moved = roll(along, -1, 1)
        along_out = jnp.where(lane == 127, roll(moved, -4, 0), moved)
        return (across - roll(across, -1, 0)) + (along - along_out)

    def balance_layer(z, vertical_in):
        head, cond = layer(z)
        head_under, cond_under = layer(z + 1)
        vertical_out = 0.5 * (cond + cond_under) * (head - head_under + 1.0)
        at = pl.ds(pl.multiple_of(z * 32, 32), 32)
        balance = (vertical_in - vertical_out) + sides(head, cond)
        part[at, :] = head + balance * rest[at, :]
        return vertical_out

    vertical_in = lax.fori_loop(0, 15, balance_layer, jnp.zeros((32, 128), F32), unroll=5)
    head, cond = layer(15)
    part[480:512, :] = head + (vertical_in + sides(head, cond)) * rest[480:512, :]

    own_rows = regroup()
    pl.when(my_z >= depth // 4)(answer)

    for copy in slab_copies:
        copy.wait_recv()
    for copy, step in zip(face_copies, (1, -1)):
        pl.when(exists(-step))(copy.wait_recv)
    head_under = jnp.where(bottom, aquifer_ref[0:32, :], slab_in[1, 0])
    cond_under = jnp.where(bottom, cond, slab_in[1, 1])
    vertical_out = 0.5 * (cond + cond_under) * (head - head_under + 1.0)
    part[480:512, :] = part[480:512, :] - vertical_out * rest[480:512, :]
    head, cond = layer(0)
    top_open = jnp.where(n == 0, 0.0, 0.5)
    vertical_in = top_open * (slab_in[0, 1] + cond) * (slab_in[0, 0] - head + 1.0)
    part[0:32, :] = part[0:32, :] + vertical_in * rest[0:32, :]
    for side, first, factor, is_open in ((0, 0, 0.5, exists(-1)), (1, 3, -0.5, exists(1))):
        head, cond = face_out[1 - side, 0], face_out[1 - side, 1]
        other_head, other_cond = face_in[side, 0], face_in[side, 1]
        jump = other_head - head if side == 0 else head - other_head
        at = pl.ds(first, 128, stride=4)
        flow = jnp.where(is_open, factor * (cond + other_cond) * jump, 0.0)
        part[at, :] = part[at, :] + flow * rest[at, :]
    part_out = pltpu.make_async_copy(part, part_hbm, store_done.at[2])
    part_out.start()

    for copy, step in zip(patch_copies, around):
        pl.when(exists(-step))(copy.wait_recv)
    for step in (-2, -1, 0, 1, 2):
        needed = exists(-step) & jnp.logical_not(bottom) if step == 0 else exists(-step)
        pl.when(needed)(drain_copy(step, 0).wait_recv)

    lane24 = iota((24, 128), 1)
    line = iota((24, 128), 0) + 4 * w - 8
    real = (line >= 0) & (line < 4 * wide_count)
    inside = jnp.where(real, 1.0, 0.0)
    after_open = jnp.where(n < narrow_count - 1, 1.0, 0.0)
    before_open = jnp.where(n > 0, 1.0, 0.0)
    inside_halo = inside * jnp.where(lane24 < 64, after_open, before_open)

    def stacked(ref, a):
        return jnp.where(real, jnp.concatenate([ref[a, s] for s in range(6)], axis=0), 0.0)

    heads = [[stacked(patches, 3 * l + t) for t in range(3)] for l in range(3)]
    flows = [stacked(drains, t) for t in range(3)]
    for l in range(3):
        trans = [stacked(patches, 9 + 3 * l + t) for t in range(3)]
        wests, easts = ring_left(trans, lane24), ring_right(trans, lane24)
        for t in range(3):
            centre = trans[t]
            north = 0.5 * (centre + roll(centre, 1, 0))
            south = 0.5 * (centre + roll(centre, -1, 0))
            west = 0.5 * (centre + wests[t])
            east = 0.5 * (centre + easts[t])
            links = 2.0 if l == 1 else 1.0
            divisor = STORAGE + north + south + west + east + LEAKANCE * links
            inverse = (inside_halo if t == 2 else inside) / divisor
            source = STORAGE * heads[l][t]
            if l == 0:
                source = source + flows[t]
            k = 3 * l + t
            coef[0, k] = north * inverse
            coef[1, k] = south * inverse
            coef[2, k] = west * inverse
            coef[3, k] = east * inverse
            coef[4, k] = LEAKANCE * inverse
            coef[5, k] = source * inverse

    def sweep(_, flat):
        now = [flat[3 * l : 3 * l + 3] for l in range(3)]
        later = []
        for l in range(3):
            wests, easts = ring_left(now[l], lane24), ring_right(now[l], lane24)
            for t in range(3):
                k = 3 * l + t
                centre = now[l][t]
                if l == 1:
                    vertical = now[0][t] + now[2][t]
                else:
                    vertical = now[1][t]
                later.append(
                    coef[5, k]
                    + coef[0, k] * roll(centre, 1, 0)
                    + coef[1, k] * roll(centre, -1, 0)
                    + coef[2, k] * wests[t]
                    + coef[3, k] * easts[t]
                    + coef[4, k] * vertical
                )
        return tuple(later)

    flat = lax.fori_loop(0, SWEEPS, sweep, tuple(v for layer in heads for v in layer))
    for l in range(3):
        aquifer_part[8 * l : 8 * l + 8, :] = jnp.concatenate(
            [flat[3 * l][8:12], flat[3 * l + 1][8:12]], axis=0
        )
    aquifer_out = pltpu.make_async_copy(aquifer_part, aquifer_next, store_done.at[3])
    aquifer_out.start()

    pl.when(my_z < depth // 4)(answer)
    lax.fori_loop(0, my_z, await_plane, 0)

    for copy in (rest_out, own_rows, part_out, aquifer_out):
        copy.wait()
    for copy in slab_copies:
        copy.wait_send()
    for copy, step in zip(patch_copies + face_copies, around + (1, -1)):
        pl.when(exists(step))(copy.wait_send)
    each_drain(lambda copy: copy.wait_send())
    for copy in plane_copies:
        copy.wait_send()

    def left_plane(z, carry):
        rows_from(PEERS, 0).wait_send()
        return carry

    def left_answer(z, carry):
        remote(*rows_to(0), answers_sent.at[0], rows_got.at[0], w, n).wait_send()
        return carry

    lax.fori_loop(0, my_z, left_plane, 0)
    lax.fori_loop(my_z + 1, depth, left_answer, 0)


def finish(
    rows_hbm,
    part_hbm,
    rest_hbm,
    aquifer_hbm,
    out_hbm,
    aquifer_out_hbm,
    rows_in,
    part,
    rest,
    out,
    spread,
    slot_lines,
    done,
):
    pairs = ((rows_hbm, rows_in), (part_hbm, part), (rest_hbm, rest), (aquifer_hbm, aquifer_out_hbm))
    loads = [pltpu.make_async_copy(a, b, done.at[i]) for i, (a, b) in enumerate(pairs)]
    for load in loads:
        load.start()
    loads[0].wait()
    slot_lines[...] = rows_in[...].T
    lanes = iota((128, 128), 0).astype(F32)
    rows = iota((32, 128), 0).astype(F32)
    target = jnp.concatenate(
        [
            (lanes == slot_lines[32 * k + 17 : 32 * k + 18, :]).astype(F32).astype(BF16)
            for k in range(CAP)
        ],
        axis=1,
    )
    hits = [rows == slot_lines[32 * k + 16 : 32 * k + 17, :] for k in range(CAP)]
    loads[1].wait()
    loads[2].wait()
    stores = []
    for i in range(4):
        for layer in range(4):
            for k in range(CAP):
                line = 32 * k + 4 * i + layer
                value = jnp.broadcast_to(slot_lines[line : line + 1, :], (32, 128))
                value = jnp.where(hits[k], value, 0.0)
                high = value.astype(BF16)
                low = (value - high.astype(F32)).astype(BF16)
                spread[i, 32 * layer : 32 * layer + 32, 128 * k : 128 * k + 128] = high
                spread[i, 32 * layer + 128 : 32 * layer + 160, 128 * k : 128 * k + 128] = low
        taken = lax.dot_general(spread[i], target, NT, preferred_element_type=F32)
        at = pl.ds(128 * i, 128)
        out[at, :] = part[at, :] - (taken[:128] + taken[128:]) * rest[at, :]
        stores.append(pltpu.make_async_copy(out.at[at], out_hbm.at[at], done.at[4 + i]))
        stores[i].start()
    loads[3].wait()
    for store in stores:
        store.wait()


def rows_of(a):
    k = a.shape[0]
    return a.reshape(k, 4, 8, 128).transpose(0, 2, 1, 3).reshape(k * 32, 128)


def grid_of(a, k, columns):
    return a.reshape(k, columns // 128, 4, 128).transpose(0, 2, 1, 3).reshape(k, 4, columns)


def body(
    pressure_head,
    texture,
    saturated_table,
    shape_table,
    capacity_table,
    uptake,
    root_tile,
    root_column,
    aquifer_head,
    transmissivity,
):
    wide_count = lax.axis_size("wide")
    narrow_count = lax.axis_size("narrow")
    depth = wide_count // PEERS
    dma = pltpu.SemaphoreType.DMA
    hbm = pl.BlockSpec(memory_space=pl.ANY)
    rows_in, part, rest, aquifer_next = pl.pallas_call(
        functools.partial(kernel, wide_count, narrow_count),
        out_shape=(
            jax.ShapeDtypeStruct((wide_count, 128), F32),
            jax.ShapeDtypeStruct((512, 128), F32),
            jax.ShapeDtypeStruct((512, 128), F32),
            jax.ShapeDtypeStruct((24, 128), F32),
        ),
        in_specs=[hbm] * 10,
        out_specs=[hbm] * 4,
        scratch_shapes=[
            pltpu.VMEM((512, 128), F32),
            pltpu.VMEM((512, 128), I32),
            pltpu.VMEM((1, 12), F32),
            pltpu.VMEM((1, 12), F32),
            pltpu.VMEM((1, 12), F32),
            pltpu.VMEM((16, 256), F32),
            pltpu.VMEM((1, 256), I32),
            pltpu.VMEM((1, 256), I32),
            pltpu.VMEM((96, 128), F32),
            pltpu.VMEM((96, 128), F32),
            pltpu.VMEM((24, 128), F32),
            pltpu.VMEM((2, 512, 128), F32),
            pltpu.VMEM((512, 128), F32),
            pltpu.VMEM((512, 128), F32),
            pltpu.VMEM((2, 2, 128, 128), F32),
            pltpu.VMEM((2, 2, 128, 128), F32),
            pltpu.VMEM((2, 2, 32, 128), F32),
            pltpu.VMEM((wide_count, 128), F32),
            pltpu.VMEM((PEERS, depth, 128), F32),
            pltpu.VMEM((PEERS, depth, 128), F32),
            pltpu.VMEM((depth, PEERS, 128), F32),
            pltpu.VMEM((18, 4, 128), F32),
            pltpu.VMEM((18, 6, 4, 128), F32),
            pltpu.VMEM((4, 3, 4, 128), F32),
            pltpu.VMEM((3, 6, 4, 128), F32),
            pltpu.VMEM((6, 9, 24, 128), F32),
            pltpu.VMEM((24, 128), F32),
            dma((4,)),
            dma((10,)),
            dma((1,)),
            dma((depth,)),
            dma((1,)),
            dma((PEERS - 1,)),
            dma((PEERS - 1,)),
            dma((4,)),
            dma((4,)),
            dma((5, 4)),
            dma((5,)),
            dma((2,)),
            dma((2,)),
            dma((2,)),
            dma((2,)),
        ],
        compiler_params=pltpu.CompilerParams(
            collective_id=0, has_side_effects=True, vmem_limit_bytes=60 * 1024 * 1024
        ),
        name="coupled_step",
    )(
        rows_of(pressure_head),
        rows_of(texture),
        saturated_table.reshape(1, -1),
        shape_table.reshape(1, -1),
        capacity_table.reshape(1, -1),
        uptake.T,
        root_tile.reshape(1, -1),
        root_column.reshape(1, -1),
        rows_of(aquifer_head),
        rows_of(transmissivity),
    )
    out, aquifer_out = pl.pallas_call(
        finish,
        out_shape=(
            jax.ShapeDtypeStruct((512, 128), F32),
            jax.ShapeDtypeStruct((24, 128), F32),
        ),
        in_specs=[hbm] * 4,
        out_specs=[hbm] * 2,
        scratch_shapes=[
            pltpu.VMEM((128, 128), F32),
            pltpu.VMEM((512, 128), F32),
            pltpu.VMEM((512, 128), F32),
            pltpu.VMEM((512, 128), F32),
            pltpu.VMEM((4, 256, 512), BF16),
            pltpu.VMEM((128, 128), F32),
            dma((8,)),
        ],
        compiler_params=pltpu.CompilerParams(vmem_limit_bytes=60 * 1024 * 1024),
        name="finish_step",
    )(rows_in, part, rest, aquifer_next)
    return grid_of(out, 16, 1024), grid_of(aquifer_out, 3, 256)


def solution(mesh):
    in_specs = (
        P("narrow", "wide", None),
        P("narrow", "wide", None),
        P(),
        P(),
        P(),
        P("wide", "narrow"),
        P("wide", None),
        P("wide"),
        P(None, "wide", None),
        P(None, "wide", None),
    )
    out_specs = (P("narrow", "wide", None), P(None, "wide", "narrow"))
    return jax.shard_map(body, mesh=mesh, in_specs=in_specs, out_specs=out_specs, check_vma=False)
```

```python
import functools

import jax
import jax.numpy as jnp
from jax import lax
from jax.experimental import pallas as pl
from jax.experimental.pallas import tpu as pltpu
from jax.sharding import PartitionSpec as P

SWEEPS = 8
TIME_STEP = 0.25
STORAGE = 0.05
LEAKANCE = 0.5
PEERS = 8
CAP = 4
VMEM_GRANT = 32 * 1024 * 1024
F32, BF16, I32 = jnp.float32, jnp.bfloat16, jnp.int32
MESH = pl.DeviceIdType.MESH
NT = (((1,), (1,)), ((), ()))


def roll(x, shift, axis):
    return pltpu.roll(x, shift % x.shape[axis], axis)


def iota(shape, axis):
    return lax.broadcasted_iota(I32, shape, axis)


def remote(src, dst, send_sem, recv_sem, wide, narrow):
    return pltpu.make_async_remote_copy(
        src_ref=src,
        dst_ref=dst,
        send_sem=send_sem,
        recv_sem=recv_sem,
        device_id=(wide, narrow),
        device_id_type=MESH,
    )


def root_slots(uptake, tile, column):
    cell_row = ((column // 128) % 8) * 4 + column // 1024
    cell_lane = column % 128
    count = tile.shape[1]
    aimed = iota((128, count), 0) == tile
    earlier = iota((count, count), 0) < iota((count, count), 1)
    rank = jnp.dot(
        aimed.astype(F32).astype(BF16),
        earlier.astype(F32).astype(BF16),
        preferred_element_type=F32,
    )
    picks = jnp.concatenate(
        [(aimed & (rank == float(k))).astype(F32).astype(BF16) for k in range(CAP)], axis=0
    )
    high = uptake.astype(BF16)
    low = (uptake - high.astype(F32)).astype(BF16)
    line = iota((16, count), 0)
    extra = jnp.where(
        line == 0,
        cell_row.astype(F32),
        jnp.where(line == 1, cell_lane.astype(F32), 0.0),
    ).astype(BF16)
    base = jnp.concatenate([high, extra, low, jnp.zeros_like(extra)], axis=0)
    spread = lax.dot_general(base, picks, NT, preferred_element_type=F32)
    rows = spread[:32] + spread[32:]
    slots = jnp.concatenate([rows[:, 128 * k : 128 * (k + 1)] for k in range(CAP)], axis=0)
    return slots.T


def ring_left(tiles, lane):
    moved = [roll(v, 1, 1) for v in tiles]
    return [jnp.where(lane == 0, moved[t - 1], moved[t]) for t in range(len(tiles))]


def ring_right(tiles, lane):
    moved = [roll(v, -1, 1) for v in tiles]
    return [
        jnp.where(lane == 127, moved[(t + 1) % len(tiles)], moved[t]) for t in range(len(tiles))
    ]


def kernel(
    wide_count,
    narrow_count,
    head_hbm,
    texture_hbm,
    saturated_hbm,
    shape_hbm,
    capacity_hbm,
    uptake_hbm,
    tile_hbm,
    column_hbm,
    aquifer_hbm,
    trans_hbm,
    rows,
    part,
    rest,
    aquifer_next,
    head_ref,
    texture_ref,
    saturated_ref,
    shape_ref,
    capacity_ref,
    uptake_ref,
    tile_ref,
    column_ref,
    aquifer_ref,
    trans_ref,
    table,
    soil,
    face_out,
    face_in,
    slab_in,
    slots,
    by_peer,
    plane_rows,
    by_plane,
    patch,
    patches,
    drain,
    drains,
    coef,
    load_done,
    rows_sent,
    rows_got,
    answers_sent,
    plane_sent,
    plane_got,
    patch_sent,
    patch_got,
    drain_sent,
    drain_got,
    face_sent,
    face_got,
    slab_sent,
    slab_got,
):
    w = lax.axis_index("wide")
    n = lax.axis_index("narrow")
    depth = wide_count // PEERS
    my_z, my_peer = w // PEERS, w % PEERS
    bottom = n == narrow_count - 1
    around = (-2, -1, 1, 2)

    def exists(step):
        return (w + step >= 0) & (w + step < wide_count)

    barrier = pltpu.get_barrier_semaphore()

    def greet(wide, narrow):
        pl.semaphore_signal(barrier, inc=1, device_id=(wide, narrow), device_id_type=MESH)

    peers = [(my_peer + j) % PEERS for j in range(1, PEERS + 1)]

    def plane_at(k):
        return (my_z + depth // 2 + ((k + 1) // 2) * (1 - 2 * (k % 2)) + depth) % depth

    def greet_plane(k, carry):
        z = plane_at(k)

        @pl.when(z > my_z)
        def _():
            for peer in peers:
                greet(z * PEERS + peer, n)

        return carry

    lax.fori_loop(0, depth - 1, greet_plane, 0)
    for peer in peers[:-1]:
        greet(my_z * PEERS + peer, n)
    greeted = PEERS * my_z + PEERS - 1 + 2
    for step in around:
        plane = (w + step + PEERS) // PEERS - 1
        greeted = greeted + jnp.where(exists(step) & (plane > my_z), 1, 0)

        @pl.when(exists(step) & (plane < my_z))
        def _(step=step):
            greet(w + step, n)

    greet(w, (n + 1) % narrow_count)
    greet(w, (n + narrow_count - 1) % narrow_count)

    for step in (-2, -1, 0, 1, 2):

        @pl.when(jnp.logical_not(bottom) & exists(step))
        def _(step=step):
            greet(w + step, narrow_count - 1)

    order = (6, 7, 5, 0, 1, 2, 3, 4, 8, 9)
    held = (head_ref, texture_ref, saturated_ref, shape_ref, capacity_ref, uptake_ref, tile_ref)
    held += (column_ref, aquifer_ref, trans_ref)
    far = (head_hbm, texture_hbm, saturated_hbm, shape_hbm, capacity_hbm, uptake_hbm, tile_hbm)
    far += (column_hbm, aquifer_hbm, trans_hbm)
    loads = [pltpu.make_async_copy(far[i], held[i], load_done.at[i]) for i in range(10)]
    for i in order:
        loads[i].start()
    for i in (6, 7, 5):
        loads[i].wait()

    made = root_slots(
        uptake_ref[...],
        tile_ref[...],
        column_ref[...],
    )
    slots[...] = made
    for z in range(depth):
        for p in range(PEERS):
            by_peer[p, z : z + 1] = slots[z * PEERS + p : z * PEERS + p + 1]

    near_tiles = sum(jnp.where(exists(step), 1, 0) for step in (-2, -1, 0, 1, 2))
    greeted = greeted + jnp.where(bottom, (narrow_count - 1) * near_tiles, 0)
    pl.semaphore_wait(barrier, greeted)

    def send_rows(tile):
        remote(
            slots.at[pl.ds(tile, 1)], rows.at[pl.ds(w, 1)], rows_sent.at[0], rows_got.at[my_z], tile, n
        ).start()

    def rows_from(count, z):
        at = rows.at[pl.ds(0, count)]
        return remote(at, at, rows_sent.at[0], rows_got.at[z], w, n)

    def send_plane(k, carry):
        z = plane_at(k)

        @pl.when(z < my_z)
        def _():
            for peer in peers:
                send_rows(z * PEERS + peer)

        return carry

    lax.fori_loop(0, depth - 1, send_plane, 0)

    plane_copies = [
        remote(
            by_peer.at[peer],
            plane_rows.at[my_peer],
            plane_sent.at[j],
            plane_got.at[j],
            my_z * PEERS + peer,
            n,
        )
        for j, peer in enumerate(peers[:-1])
    ]
    for copy in plane_copies:
        copy.start()

    def rows_to(z):
        return (by_plane.at[z], rows.at[pl.ds(my_z * PEERS, PEERS)])

    def answer_plane(z, carry):
        rows_from(PEERS, z).wait_recv()
        to = z * PEERS + my_peer
        remote(*rows_to(z), answers_sent.at[0], rows_got.at[my_z], to, n).start()
        return carry

    def await_plane(z, carry):
        rows_from(PEERS, z).wait_recv()
        return carry

    for i in (8, 9):
        loads[i].wait()
    lane4 = iota((4, 128), 1)
    for a in range(6):
        source = aquifer_ref if a < 3 else trans_ref
        first = (a % 3) * 32
        here = source[pl.ds(pl.multiple_of(first + 8 * n, 8), 8), :]
        after = source[pl.ds(pl.multiple_of(first + 8 * jnp.minimum(n + 1, 3), 8), 8), :]
        before = source[pl.ds(pl.multiple_of(first + 8 * jnp.maximum(n - 1, 0), 8), 8), :]
        after = jnp.where(n < narrow_count - 1, after[0:4], 0.0)
        before = jnp.where(n > 0, before[4:8], 0.0)
        patch[3 * a] = here[0:4]
        patch[3 * a + 1] = here[4:8]
        patch[3 * a + 2] = jnp.where(lane4 < 64, after, before)
    for a in range(18):
        patches[a, 2] = patch[a]
        patches[a, 5] = jnp.zeros((4, 128), F32)
    for t in range(3):
        drains[t, 5] = jnp.zeros((4, 128), F32)

    for i in (0, 1, 2, 3, 4):
        loads[i].wait()
    table[...] = jnp.zeros_like(table)
    table[0:1, 0:12] = saturated_ref[...]
    table[8:9, 0:12] = shape_ref[...]
    table[16:17, 0:12] = capacity_ref[...]

    def look_up(row, index):
        values = jnp.broadcast_to(table[row : row + 1, :], index.shape)
        return jnp.take_along_axis(values, index, axis=1, mode="promise_in_bounds")

    def conduct_layer(z, carry):
        here = pl.ds(pl.multiple_of(z * 32, 32), 32)
        head = head_ref[here, :]
        index = texture_ref[here, :]
        soil[0, here, :] = head
        soil[1, here, :] = look_up(0, index) * jnp.exp(look_up(8, index) * jnp.minimum(head, 0.0))
        rest[here, :] = TIME_STEP / look_up(16, index)
        return carry

    lax.fori_loop(0, 16, conduct_layer, 0, unroll=4)

    for i, first in ((0, 3), (1, 0)):
        for v in range(2):
            face_out[i, v] = soil[v, pl.ds(first, 128, stride=4), :]
    @pl.when(bottom)
    def _():
        flow = soil[1, 480:512, :] * (soil[0, 480:512, :] - aquifer_ref[0:32, :] + 1.0)
        for q in range(4):
            drain[q, 0] = flow[8 * q : 8 * q + 4]
            drain[q, 1] = flow[8 * q + 4 : 8 * q + 8]
            after = flow[8 * q + 8 : 8 * q + 12] if q < 3 else jnp.zeros((4, 128), F32)
            before = flow[8 * q - 4 : 8 * q] if q > 0 else jnp.zeros((4, 128), F32)
            drain[q, 2] = jnp.where(lane4 < 64, after, before)
        drains[:, 2] = drain[3]

    face_copies = [
        remote(face_out.at[i], face_in.at[i], face_sent.at[i], face_got.at[i], w + step, n)
        for i, step in ((0, 1), (1, -1))
    ]
    for copy, step in zip(face_copies, (1, -1)):
        pl.when(exists(step))(copy.start)
    slab_copies = [
        remote(
            soil.at[:, pl.ds(first, 32)],
            slab_in.at[i],
            slab_sent.at[i],
            slab_got.at[i],
            w,
            (n + step) % narrow_count,
        )
        for i, first, step in ((0, 480, 1), (1, 0, narrow_count - 1))
    ]
    for copy in slab_copies:
        copy.start()
    patch_copies = [
        remote(patch, patches.at[:, 2 - step], patch_sent.at[i], patch_got.at[i], w + step, n)
        for i, step in enumerate(around)
    ]
    for copy, step in zip(patch_copies, around):
        pl.when(exists(step))(copy.start)

    def drain_copy(step, q):
        return remote(
            drain.at[q],
            drains.at[:, 2 - step],
            drain_sent.at[step + 2, q],
            drain_got.at[2 - step],
            w + step,
            q,
        )

    def each_drain(act):
        for step in (0, 1, -1, 2, -2):

            @pl.when(bottom & exists(step))
            def _(step=step):
                for q in range(narrow_count - 1 if step == 0 else narrow_count):
                    act(drain_copy(step, q))

    each_drain(lambda copy: copy.start())

    def answer():
        lax.fori_loop(my_z + 1, depth, answer_plane, 0)

    def regroup():
        for copy in plane_copies:
            copy.wait_recv()
        plane_rows[my_peer] = by_peer[my_peer]
        for z in range(depth):
            for p in range(PEERS):
                by_plane[z, p : p + 1] = plane_rows[p, z : z + 1]
        rows[pl.ds(pl.multiple_of(my_z * PEERS, PEERS), PEERS), :] = by_plane[my_z]

    row = iota((32, 128), 0)
    lane = iota((32, 128), 1)
    across_open = jnp.where(row % 4 == 0, 0.0, 0.5)
    along_open = jnp.where((lane == 0) & (row < 4), 0.0, 0.5)

    def previous_column(v):
        moved = roll(v, 1, 1)
        return jnp.where(lane == 0, roll(moved, 4, 0), moved)

    def layer(z):
        at = pl.ds(pl.multiple_of(z * 32, 32), 32)
        return soil[0, at, :], soil[1, at, :]

    def sides(head, cond):
        across = across_open * (roll(cond, 1, 0) + cond) * (roll(head, 1, 0) - head)
        along = along_open * (previous_column(cond) + cond) * (previous_column(head) - head)
        moved = roll(along, -1, 1)
        along_out = jnp.where(lane == 127, roll(moved, -4, 0), moved)
        return (across - roll(across, -1, 0)) + (along - along_out)

    def balance_layer(z, vertical_in):
        head, cond = layer(z)
        head_under, cond_under = layer(z + 1)
        vertical_out = 0.5 * (cond + cond_under) * (head - head_under + 1.0)
        at = pl.ds(pl.multiple_of(z * 32, 32), 32)
        balance = (vertical_in - vertical_out) + sides(head, cond)
        part[at, :] = head + balance * rest[at, :]
        return vertical_out

    vertical_in = lax.fori_loop(0, 15, balance_layer, jnp.zeros((32, 128), F32), unroll=5)
    head, cond = layer(15)
    part[480:512, :] = head + (vertical_in + sides(head, cond)) * rest[480:512, :]

    regroup()
    pl.when(my_z >= depth // 4)(answer)

    for copy in slab_copies:
        copy.wait_recv()
    for copy, step in zip(face_copies, (1, -1)):
        pl.when(exists(-step))(copy.wait_recv)
    head_under = jnp.where(bottom, aquifer_ref[0:32, :], slab_in[1, 0])
    cond_under = jnp.where(bottom, cond, slab_in[1, 1])
    vertical_out = 0.5 * (cond + cond_under) * (head - head_under + 1.0)
    part[480:512, :] = part[480:512, :] - vertical_out * rest[480:512, :]
    head, cond = layer(0)
    top_open = jnp.where(n == 0, 0.0, 0.5)
    vertical_in = top_open * (slab_in[0, 1] + cond) * (slab_in[0, 0] - head + 1.0)
    part[0:32, :] = part[0:32, :] + vertical_in * rest[0:32, :]
    for side, first, factor, is_open in ((0, 0, 0.5, exists(-1)), (1, 3, -0.5, exists(1))):
        head, cond = face_out[1 - side, 0], face_out[1 - side, 1]
        other_head, other_cond = face_in[side, 0], face_in[side, 1]
        jump = other_head - head if side == 0 else head - other_head
        at = pl.ds(first, 128, stride=4)
        flow = jnp.where(is_open, factor * (cond + other_cond) * jump, 0.0)
        part[at, :] = part[at, :] + flow * rest[at, :]

    for copy, step in zip(patch_copies, around):
        pl.when(exists(-step))(copy.wait_recv)
    for step in (-2, -1, 0, 1, 2):
        needed = exists(-step) & jnp.logical_not(bottom) if step == 0 else exists(-step)
        pl.when(needed)(drain_copy(step, 0).wait_recv)

    lane24 = iota((24, 128), 1)
    line = iota((24, 128), 0) + 4 * w - 8
    real = (line >= 0) & (line < 4 * wide_count)
    inside = jnp.where(real, 1.0, 0.0)
    after_open = jnp.where(n < narrow_count - 1, 1.0, 0.0)
    before_open = jnp.where(n > 0, 1.0, 0.0)
    inside_halo = inside * jnp.where(lane24 < 64, after_open, before_open)

    def stacked(ref, a):
        return jnp.where(real, jnp.concatenate([ref[a, s] for s in range(6)], axis=0), 0.0)

    heads = [[stacked(patches, 3 * l + t) for t in range(3)] for l in range(3)]
    flows = [stacked(drains, t) for t in range(3)]
    for l in range(3):
        trans = [stacked(patches, 9 + 3 * l + t) for t in range(3)]
        wests, easts = ring_left(trans, lane24), ring_right(trans, lane24)
        for t in range(3):
            centre = trans[t]
            north = 0.5 * (centre + roll(centre, 1, 0))
            south = 0.5 * (centre + roll(centre, -1, 0))
            west = 0.5 * (centre + wests[t])
            east = 0.5 * (centre + easts[t])
            links = 2.0 if l == 1 else 1.0
            divisor = STORAGE + north + south + west + east + LEAKANCE * links
            inverse = (inside_halo if t == 2 else inside) / divisor
            source = STORAGE * heads[l][t]
            if l == 0:
                source = source + flows[t]
            k = 3 * l + t
            coef[0, k] = north * inverse
            coef[1, k] = south * inverse
            coef[2, k] = west * inverse
            coef[3, k] = east * inverse
            coef[4, k] = LEAKANCE * inverse
            coef[5, k] = source * inverse

    def sweep(_, flat):
        now = [flat[3 * l : 3 * l + 3] for l in range(3)]
        later = []
        for l in range(3):
            wests, easts = ring_left(now[l], lane24), ring_right(now[l], lane24)
            for t in range(3):
                k = 3 * l + t
                centre = now[l][t]
                if l == 1:
                    vertical = now[0][t] + now[2][t]
                else:
                    vertical = now[1][t]
                later.append(
                    coef[5, k]
                    + coef[0, k] * roll(centre, 1, 0)
                    + coef[1, k] * roll(centre, -1, 0)
                    + coef[2, k] * wests[t]
                    + coef[3, k] * easts[t]
                    + coef[4, k] * vertical
                )
        return tuple(later)

    flat = lax.fori_loop(0, SWEEPS, sweep, tuple(v for layer in heads for v in layer))
    for l in range(3):
        aquifer_next[8 * l : 8 * l + 8, :] = jnp.concatenate(
            [flat[3 * l][8:12], flat[3 * l + 1][8:12]], axis=0
        )

    pl.when(my_z < depth // 4)(answer)
    lax.fori_loop(0, my_z, await_plane, 0)

    for copy in slab_copies:
        copy.wait_send()
    for copy, step in zip(patch_copies + face_copies, around + (1, -1)):
        pl.when(exists(step))(copy.wait_send)
    each_drain(lambda copy: copy.wait_send())
    for copy in plane_copies:
        copy.wait_send()

    def left_plane(z, carry):
        rows_from(PEERS, 0).wait_send()
        return carry

    def left_answer(z, carry):
        remote(*rows_to(0), answers_sent.at[0], rows_got.at[0], w, n).wait_send()
        return carry

    lax.fori_loop(0, my_z, left_plane, 0)
    lax.fori_loop(my_z + 1, depth, left_answer, 0)


def finish(
    rows_in,
    part,
    rest,
    aquifer_next,
    out_hbm,
    aquifer_out_hbm,
    out,
    spread,
    slot_lines,
    done,
):
    aquifer_out = pltpu.make_async_copy(aquifer_next, aquifer_out_hbm, done.at[4])
    aquifer_out.start()
    slot_lines[...] = rows_in[...].T
    lanes = iota((128, 128), 0).astype(F32)
    rows = iota((32, 128), 0).astype(F32)
    target = jnp.concatenate(
        [
            (lanes == slot_lines[32 * k + 17 : 32 * k + 18, :]).astype(F32).astype(BF16)
            for k in range(CAP)
        ],
        axis=1,
    )
    hits = [rows == slot_lines[32 * k + 16 : 32 * k + 17, :] for k in range(CAP)]
    stores = []
    for i in range(4):
        for layer in range(4):
            for k in range(CAP):
                line = 32 * k + 4 * i + layer
                value = jnp.broadcast_to(slot_lines[line : line + 1, :], (32, 128))
                value = jnp.where(hits[k], value, 0.0)
                high = value.astype(BF16)
                low = (value - high.astype(F32)).astype(BF16)
                spread[i, 32 * layer : 32 * layer + 32, 128 * k : 128 * k + 128] = high
                spread[i, 32 * layer + 128 : 32 * layer + 160, 128 * k : 128 * k + 128] = low
        taken = lax.dot_general(spread[i], target, NT, preferred_element_type=F32)
        at = pl.ds(128 * i, 128)
        out[at, :] = part[at, :] - (taken[:128] + taken[128:]) * rest[at, :]
        stores.append(pltpu.make_async_copy(out.at[at], out_hbm.at[at], done.at[i]))
        stores[i].start()
    aquifer_out.wait()
    for store in stores:
        store.wait()


def rows_of(a):
    k = a.shape[0]
    return a.reshape(k, 4, 8, 128).transpose(0, 2, 1, 3).reshape(k * 32, 128)


def grid_of(a, k, columns):
    return a.reshape(k, columns // 128, 4, 128).transpose(0, 2, 1, 3).reshape(k, 4, columns)


def body(
    pressure_head,
    texture,
    saturated_table,
    shape_table,
    capacity_table,
    uptake,
    root_tile,
    root_column,
    aquifer_head,
    transmissivity,
):
    wide_count = lax.axis_size("wide")
    narrow_count = lax.axis_size("narrow")
    depth = wide_count // PEERS
    dma = pltpu.SemaphoreType.DMA
    hbm, vmem = pl.BlockSpec(memory_space=pltpu.HBM), pl.BlockSpec(memory_space=pltpu.VMEM)
    rows_in, part, rest, aquifer_next = pl.pallas_call(
        functools.partial(kernel, wide_count, narrow_count),
        out_shape=(
            pltpu.VMEM((wide_count, 128), F32),
            pltpu.VMEM((512, 128), F32),
            pltpu.VMEM((512, 128), F32),
            pltpu.VMEM((24, 128), F32),
        ),
        in_specs=[hbm] * 10,
        out_specs=[vmem] * 4,
        scratch_shapes=[
            pltpu.VMEM((512, 128), F32),
            pltpu.VMEM((512, 128), I32),
            pltpu.VMEM((1, 12), F32),
            pltpu.VMEM((1, 12), F32),
            pltpu.VMEM((1, 12), F32),
            pltpu.VMEM((16, 256), F32),
            pltpu.VMEM((1, 256), I32),
            pltpu.VMEM((1, 256), I32),
            pltpu.VMEM((96, 128), F32),
            pltpu.VMEM((96, 128), F32),
            pltpu.VMEM((24, 128), F32),
            pltpu.VMEM((2, 512, 128), F32),
            pltpu.VMEM((2, 2, 128, 128), F32),
            pltpu.VMEM((2, 2, 128, 128), F32),
            pltpu.VMEM((2, 2, 32, 128), F32),
            pltpu.VMEM((wide_count, 128), F32),
            pltpu.VMEM((PEERS, depth, 128), F32),
            pltpu.VMEM((PEERS, depth, 128), F32),
            pltpu.VMEM((depth, PEERS, 128), F32),
            pltpu.VMEM((18, 4, 128), F32),
            pltpu.VMEM((18, 6, 4, 128), F32),
            pltpu.VMEM((4, 3, 4, 128), F32),
            pltpu.VMEM((3, 6, 4, 128), F32),
            pltpu.VMEM((6, 9, 24, 128), F32),
            dma((10,)),
            dma((1,)),
            dma((depth,)),
            dma((1,)),
            dma((PEERS - 1,)),
            dma((PEERS - 1,)),
            dma((4,)),
            dma((4,)),
            dma((5, 4)),
            dma((5,)),
            dma((2,)),
            dma((2,)),
            dma((2,)),
            dma((2,)),
        ],
        compiler_params=pltpu.CompilerParams(
            collective_id=0, has_side_effects=True, vmem_limit_bytes=VMEM_GRANT
        ),
        name="coupled_step",
    )(
        *(
            pltpu.with_memory_space_constraint(a, pltpu.HBM)
            for a in (
                rows_of(pressure_head),
                rows_of(texture),
                saturated_table.reshape(1, -1),
                shape_table.reshape(1, -1),
                capacity_table.reshape(1, -1),
                uptake.T,
                root_tile.reshape(1, -1),
                root_column.reshape(1, -1),
                rows_of(aquifer_head),
                rows_of(transmissivity),
            )
        )
    )
    out, aquifer_out = pl.pallas_call(
        finish,
        out_shape=(
            jax.ShapeDtypeStruct((512, 128), F32),
            jax.ShapeDtypeStruct((24, 128), F32),
        ),
        in_specs=[vmem] * 4,
        out_specs=[hbm] * 2,
        scratch_shapes=[
            pltpu.VMEM((512, 128), F32),
            pltpu.VMEM((4, 256, 512), BF16),
            pltpu.VMEM((128, 128), F32),
            dma((5,)),
        ],
        compiler_params=pltpu.CompilerParams(vmem_limit_bytes=VMEM_GRANT),
        name="finish_step",
    )(rows_in, part, rest, aquifer_next)
    return grid_of(out, 16, 1024), grid_of(aquifer_out, 3, 256)


def solution(mesh):
    in_specs = (
        P("narrow", "wide", None),
        P("narrow", "wide", None),
        P(),
        P(),
        P(),
        P("wide", "narrow"),
        P("wide", None),
        P("wide"),
        P(None, "wide", None),
        P(None, "wide", None),
    )
    out_specs = (P("narrow", "wide", None), P(None, "wide", "narrow"))
    return jax.shard_map(body, mesh=mesh, in_specs=in_specs, out_specs=out_specs, check_vma=False)
```

```python
import functools

import jax
import jax.numpy as jnp
from jax import lax
from jax.experimental import pallas as pl
from jax.experimental.pallas import tpu as pltpu
from jax.sharding import PartitionSpec as P

SWEEPS = 8
TIME_STEP = 0.25
STORAGE = 0.05
LEAKANCE = 0.5
PEERS = 8
CAP = 4
VMEM_GRANT = 32 * 1024 * 1024
F32, BF16, I32 = jnp.float32, jnp.bfloat16, jnp.int32
MESH = pl.DeviceIdType.MESH
NT = (((1,), (1,)), ((), ()))


def roll(x, shift, axis):
    return pltpu.roll(x, shift % x.shape[axis], axis)


def iota(shape, axis):
    return lax.broadcasted_iota(I32, shape, axis)


def remote(src, dst, send_sem, recv_sem, wide, narrow):
    return pltpu.make_async_remote_copy(
        src_ref=src,
        dst_ref=dst,
        send_sem=send_sem,
        recv_sem=recv_sem,
        device_id=(wide, narrow),
        device_id_type=MESH,
    )


def root_slots(uptake, tile, column):
    cell_row = ((column // 128) % 8) * 4 + column // 1024
    cell_lane = column % 128
    count = tile.shape[1]
    aimed = iota((128, count), 0) == tile
    earlier = iota((count, count), 0) < iota((count, count), 1)
    rank = jnp.dot(
        aimed.astype(F32).astype(BF16),
        earlier.astype(F32).astype(BF16),
        preferred_element_type=F32,
    )
    picks = jnp.concatenate(
        [(aimed & (rank == float(k))).astype(F32).astype(BF16) for k in range(CAP)], axis=0
    )
    high = uptake.astype(BF16)
    low = (uptake - high.astype(F32)).astype(BF16)
    line = iota((16, count), 0)
    extra = jnp.where(
        line == 0,
        cell_row.astype(F32),
        jnp.where(line == 1, cell_lane.astype(F32), 0.0),
    ).astype(BF16)
    base = jnp.concatenate([high, extra, low, jnp.zeros_like(extra)], axis=0)
    spread = lax.dot_general(base, picks, NT, preferred_element_type=F32)
    rows = spread[:32] + spread[32:]
    slots = jnp.concatenate([rows[:, 128 * k : 128 * (k + 1)] for k in range(CAP)], axis=0)
    return slots.T


def ring_left(tiles, lane):
    moved = [roll(v, 1, 1) for v in tiles]
    return [jnp.where(lane == 0, moved[t - 1], moved[t]) for t in range(len(tiles))]


def ring_right(tiles, lane):
    moved = [roll(v, -1, 1) for v in tiles]
    return [
        jnp.where(lane == 127, moved[(t + 1) % len(tiles)], moved[t]) for t in range(len(tiles))
    ]


def kernel(
    wide_count,
    narrow_count,
    head_hbm,
    texture_hbm,
    saturated_hbm,
    shape_hbm,
    capacity_hbm,
    uptake_hbm,
    tile_hbm,
    column_hbm,
    aquifer_hbm,
    trans_hbm,
    out,
    aquifer_next,
    head_ref,
    texture_ref,
    saturated_ref,
    shape_ref,
    capacity_ref,
    uptake_ref,
    tile_ref,
    column_ref,
    aquifer_ref,
    trans_ref,
    table,
    soil,
    rows,
    part,
    rest,
    spread,
    slot_lines,
    face_out,
    face_in,
    slab_in,
    slots,
    by_peer,
    plane_rows,
    by_plane,
    patch,
    patches,
    drain,
    drains,
    coef,
    load_done,
    rows_sent,
    rows_got,
    answers_sent,
    plane_sent,
    plane_got,
    patch_sent,
    patch_got,
    drain_sent,
    drain_got,
    face_sent,
    face_got,
    slab_sent,
    slab_got,
):
    w = lax.axis_index("wide")
    n = lax.axis_index("narrow")
    depth = wide_count // PEERS
    my_z, my_peer = w // PEERS, w % PEERS
    bottom = n == narrow_count - 1
    around = (-2, -1, 1, 2)

    def exists(step):
        return (w + step >= 0) & (w + step < wide_count)

    barrier = pltpu.get_barrier_semaphore()

    def greet(wide, narrow):
        pl.semaphore_signal(barrier, inc=1, device_id=(wide, narrow), device_id_type=MESH)

    peers = [(my_peer + j) % PEERS for j in range(1, PEERS + 1)]

    def plane_at(k):
        return (my_z + depth // 2 + ((k + 1) // 2) * (1 - 2 * (k % 2)) + depth) % depth

    def greet_plane(k, carry):
        z = plane_at(k)

        @pl.when(z > my_z)
        def _():
            for peer in peers:
                greet(z * PEERS + peer, n)

        return carry

    for peer in peers[:-1]:
        greet(my_z * PEERS + peer, n)
    greeted = PEERS * my_z + PEERS - 1 + 2
    for step in around:
        plane = (w + step + PEERS) // PEERS - 1
        greeted = greeted + jnp.where(exists(step) & (plane > my_z), 1, 0)

        @pl.when(exists(step) & (plane < my_z))
        def _(step=step):
            greet(w + step, n)

    greet(w, (n + 1) % narrow_count)
    greet(w, (n + narrow_count - 1) % narrow_count)

    for step in (-2, -1, 0, 1, 2):

        @pl.when(jnp.logical_not(bottom) & exists(step))
        def _(step=step):
            greet(w + step, narrow_count - 1)

    lax.fori_loop(0, depth - 1, greet_plane, 0)

    order = (6, 7, 5, 0, 1, 2, 3, 4, 8, 9)
    held = (head_ref, texture_ref, saturated_ref, shape_ref, capacity_ref, uptake_ref, tile_ref)
    held += (column_ref, aquifer_ref, trans_ref)
    far = (head_hbm, texture_hbm, saturated_hbm, shape_hbm, capacity_hbm, uptake_hbm, tile_hbm)
    far += (column_hbm, aquifer_hbm, trans_hbm)
    loads = [pltpu.make_async_copy(far[i], held[i], load_done.at[i]) for i in range(10)]
    for i in order:
        loads[i].start()
    for i in (6, 7, 5):
        loads[i].wait()

    made = root_slots(
        uptake_ref[...],
        tile_ref[...],
        column_ref[...],
    )
    slots[...] = made
    for z in range(depth):
        for p in range(PEERS):
            by_peer[p, z : z + 1] = slots[z * PEERS + p : z * PEERS + p + 1]

    near_tiles = sum(jnp.where(exists(step), 1, 0) for step in (-2, -1, 0, 1, 2))
    greeted = greeted + jnp.where(bottom, (narrow_count - 1) * near_tiles, 0)
    pl.semaphore_wait(barrier, greeted)

    def send_rows(tile):
        remote(
            slots.at[pl.ds(tile, 1)], rows.at[pl.ds(w, 1)], rows_sent.at[0], rows_got.at[my_z], tile, n
        ).start()

    def rows_from(count, z):
        at = rows.at[pl.ds(0, count)]
        return remote(at, at, rows_sent.at[0], rows_got.at[z], w, n)

    def send_plane(k, carry):
        z = plane_at(k)

        @pl.when(z < my_z)
        def _():
            for peer in peers:
                send_rows(z * PEERS + peer)

        return carry

    lax.fori_loop(0, depth - 1, send_plane, 0)

    plane_copies = [
        remote(
            by_peer.at[peer],
            plane_rows.at[my_peer],
            plane_sent.at[j],
            plane_got.at[j],
            my_z * PEERS + peer,
            n,
        )
        for j, peer in enumerate(peers[:-1])
    ]
    for copy in plane_copies:
        copy.start()

    def rows_to(z):
        return (by_plane.at[z], rows.at[pl.ds(my_z * PEERS, PEERS)])

    def answer_plane(z, carry):
        rows_from(PEERS, z).wait_recv()
        to = z * PEERS + my_peer
        remote(*rows_to(z), answers_sent.at[0], rows_got.at[my_z], to, n).start()
        return carry

    def await_plane(z, carry):
        rows_from(PEERS, z).wait_recv()
        return carry

    for i in (8, 9):
        loads[i].wait()
    lane4 = iota((4, 128), 1)
    for a in range(6):
        source = aquifer_ref if a < 3 else trans_ref
        first = (a % 3) * 32
        here = source[pl.ds(pl.multiple_of(first + 8 * n, 8), 8), :]
        after = source[pl.ds(pl.multiple_of(first + 8 * jnp.minimum(n + 1, 3), 8), 8), :]
        before = source[pl.ds(pl.multiple_of(first + 8 * jnp.maximum(n - 1, 0), 8), 8), :]
        after = jnp.where(n < narrow_count - 1, after[0:4], 0.0)
        before = jnp.where(n > 0, before[4:8], 0.0)
        patch[3 * a] = here[0:4]
        patch[3 * a + 1] = here[4:8]
        patch[3 * a + 2] = jnp.where(lane4 < 64, after, before)
    for a in range(18):
        patches[a, 2] = patch[a]
        patches[a, 5] = jnp.zeros((4, 128), F32)
    for t in range(3):
        drains[t, 5] = jnp.zeros((4, 128), F32)

    for i in (0, 1, 2, 3, 4):
        loads[i].wait()
    table[...] = jnp.zeros_like(table)
    table[0:1, 0:12] = saturated_ref[...]
    table[8:9, 0:12] = shape_ref[...]
    table[16:17, 0:12] = capacity_ref[...]

    def look_up(row, index):
        values = jnp.broadcast_to(table[row : row + 1, :], index.shape)
        return jnp.take_along_axis(values, index, axis=1, mode="promise_in_bounds")

    def conduct_layer(z, carry):
        here = pl.ds(pl.multiple_of(z * 32, 32), 32)
        head = head_ref[here, :]
        index = texture_ref[here, :]
        soil[0, here, :] = head
        soil[1, here, :] = look_up(0, index) * jnp.exp(look_up(8, index) * jnp.minimum(head, 0.0))
        rest[here, :] = TIME_STEP / look_up(16, index)
        return carry

    lax.fori_loop(0, 16, conduct_layer, 0, unroll=4)

    for i, first in ((0, 3), (1, 0)):
        for v in range(2):
            face_out[i, v] = soil[v, pl.ds(first, 128, stride=4), :]
    @pl.when(bottom)
    def _():
        flow = soil[1, 480:512, :] * (soil[0, 480:512, :] - aquifer_ref[0:32, :] + 1.0)
        for q in range(4):
            drain[q, 0] = flow[8 * q : 8 * q + 4]
            drain[q, 1] = flow[8 * q + 4 : 8 * q + 8]
            after = flow[8 * q + 8 : 8 * q + 12] if q < 3 else jnp.zeros((4, 128), F32)
            before = flow[8 * q - 4 : 8 * q] if q > 0 else jnp.zeros((4, 128), F32)
            drain[q, 2] = jnp.where(lane4 < 64, after, before)
        drains[:, 2] = drain[3]

    face_copies = [
        remote(face_out.at[i], face_in.at[i], face_sent.at[i], face_got.at[i], w + step, n)
        for i, step in ((0, 1), (1, -1))
    ]
    for copy, step in zip(face_copies, (1, -1)):
        pl.when(exists(step))(copy.start)
    slab_copies = [
        remote(
            soil.at[:, pl.ds(first, 32)],
            slab_in.at[i],
            slab_sent.at[i],
            slab_got.at[i],
            w,
            (n + step) % narrow_count,
        )
        for i, first, step in ((0, 480, 1), (1, 0, narrow_count - 1))
    ]
    for copy in slab_copies:
        copy.start()
    patch_copies = [
        remote(patch, patches.at[:, 2 - step], patch_sent.at[i], patch_got.at[i], w + step, n)
        for i, step in enumerate(around)
    ]
    for copy, step in zip(patch_copies, around):
        pl.when(exists(step))(copy.start)

    def drain_copy(step, q):
        return remote(
            drain.at[q],
            drains.at[:, 2 - step],
            drain_sent.at[step + 2, q],
            drain_got.at[2 - step],
            w + step,
            q,
        )

    def each_drain(act):
        for step in (0, 1, -1, 2, -2):

            @pl.when(bottom & exists(step))
            def _(step=step):
                for q in range(narrow_count - 1 if step == 0 else narrow_count):
                    act(drain_copy(step, q))

    each_drain(lambda copy: copy.start())

    half = depth // 2

    def answer(low, high):
        lax.fori_loop(jnp.maximum(my_z + 1, low), high, answer_plane, 0)

    def regroup():
        for copy in plane_copies:
            copy.wait_recv()
        plane_rows[my_peer] = by_peer[my_peer]
        for z in range(depth):
            for p in range(PEERS):
                by_plane[z, p : p + 1] = plane_rows[p, z : z + 1]
        rows[pl.ds(pl.multiple_of(my_z * PEERS, PEERS), PEERS), :] = by_plane[my_z]

    row = iota((32, 128), 0)
    lane = iota((32, 128), 1)
    across_open = jnp.where(row % 4 == 0, 0.0, 0.5)
    along_open = jnp.where((lane == 0) & (row < 4), 0.0, 0.5)

    def previous_column(v):
        moved = roll(v, 1, 1)
        return jnp.where(lane == 0, roll(moved, 4, 0), moved)

    def layer(z):
        at = pl.ds(pl.multiple_of(z * 32, 32), 32)
        return soil[0, at, :], soil[1, at, :]

    def sides(head, cond):
        across = across_open * (roll(cond, 1, 0) + cond) * (roll(head, 1, 0) - head)
        along = along_open * (previous_column(cond) + cond) * (previous_column(head) - head)
        moved = roll(along, -1, 1)
        along_out = jnp.where(lane == 127, roll(moved, -4, 0), moved)
        return (across - roll(across, -1, 0)) + (along - along_out)

    def balance_layer(z, vertical_in):
        head, cond = layer(z)
        head_under, cond_under = layer(z + 1)
        vertical_out = 0.5 * (cond + cond_under) * (head - head_under + 1.0)
        at = pl.ds(pl.multiple_of(z * 32, 32), 32)
        balance = (vertical_in - vertical_out) + sides(head, cond)
        part[at, :] = head + balance * rest[at, :]
        return vertical_out

    vertical_in = lax.fori_loop(0, 15, balance_layer, jnp.zeros((32, 128), F32), unroll=5)
    head, cond = layer(15)
    part[480:512, :] = head + (vertical_in + sides(head, cond)) * rest[480:512, :]

    regroup()
    pl.when(my_z >= depth // 4)(lambda: answer(0, depth))

    for copy in slab_copies:
        copy.wait_recv()
    for copy, step in zip(face_copies, (1, -1)):
        pl.when(exists(-step))(copy.wait_recv)
    head_under = jnp.where(bottom, aquifer_ref[0:32, :], slab_in[1, 0])
    cond_under = jnp.where(bottom, cond, slab_in[1, 1])
    vertical_out = 0.5 * (cond + cond_under) * (head - head_under + 1.0)
    part[480:512, :] = part[480:512, :] - vertical_out * rest[480:512, :]
    head, cond = layer(0)
    top_open = jnp.where(n == 0, 0.0, 0.5)
    vertical_in = top_open * (slab_in[0, 1] + cond) * (slab_in[0, 0] - head + 1.0)
    part[0:32, :] = part[0:32, :] + vertical_in * rest[0:32, :]
    for side, first, factor, is_open in ((0, 0, 0.5, exists(-1)), (1, 3, -0.5, exists(1))):
        head, cond = face_out[1 - side, 0], face_out[1 - side, 1]
        other_head, other_cond = face_in[side, 0], face_in[side, 1]
        jump = other_head - head if side == 0 else head - other_head
        at = pl.ds(first, 128, stride=4)
        flow = jnp.where(is_open, factor * (cond + other_cond) * jump, 0.0)
        part[at, :] = part[at, :] + flow * rest[at, :]

    for copy, step in zip(patch_copies, around):
        pl.when(exists(-step))(copy.wait_recv)
    for step in (-2, -1, 0, 1, 2):
        needed = exists(-step) & jnp.logical_not(bottom) if step == 0 else exists(-step)
        pl.when(needed)(drain_copy(step, 0).wait_recv)

    lane24 = iota((24, 128), 1)
    line = iota((24, 128), 0) + 4 * w - 8
    real = (line >= 0) & (line < 4 * wide_count)
    inside = jnp.where(real, 1.0, 0.0)
    after_open = jnp.where(n < narrow_count - 1, 1.0, 0.0)
    before_open = jnp.where(n > 0, 1.0, 0.0)
    inside_halo = inside * jnp.where(lane24 < 64, after_open, before_open)

    def stacked(ref, a):
        return jnp.where(real, jnp.concatenate([ref[a, s] for s in range(6)], axis=0), 0.0)

    heads = [[stacked(patches, 3 * l + t) for t in range(3)] for l in range(3)]
    flows = [stacked(drains, t) for t in range(3)]
    for l in range(3):
        trans = [stacked(patches, 9 + 3 * l + t) for t in range(3)]
        wests, easts = ring_left(trans, lane24), ring_right(trans, lane24)
        for t in range(3):
            centre = trans[t]
            north = 0.5 * (centre + roll(centre, 1, 0))
            south = 0.5 * (centre + roll(centre, -1, 0))
            west = 0.5 * (centre + wests[t])
            east = 0.5 * (centre + easts[t])
            links = 2.0 if l == 1 else 1.0
            divisor = STORAGE + north + south + west + east + LEAKANCE * links
            inverse = (inside_halo if t == 2 else inside) / divisor
            source = STORAGE * heads[l][t]
            if l == 0:
                source = source + flows[t]
            k = 3 * l + t
            coef[0, k] = north * inverse
            coef[1, k] = south * inverse
            coef[2, k] = west * inverse
            coef[3, k] = east * inverse
            coef[4, k] = LEAKANCE * inverse
            coef[5, k] = source * inverse

    def sweep(_, flat):
        now = [flat[3 * l : 3 * l + 3] for l in range(3)]
        later = []
        for l in range(3):
            wests, easts = ring_left(now[l], lane24), ring_right(now[l], lane24)
            for t in range(3):
                k = 3 * l + t
                centre = now[l][t]
                if l == 1:
                    vertical = now[0][t] + now[2][t]
                else:
                    vertical = now[1][t]
                later.append(
                    coef[5, k]
                    + coef[0, k] * roll(centre, 1, 0)
                    + coef[1, k] * roll(centre, -1, 0)
                    + coef[2, k] * wests[t]
                    + coef[3, k] * easts[t]
                    + coef[4, k] * vertical
                )
        return tuple(later)

    flat = lax.fori_loop(0, SWEEPS, sweep, tuple(v for layer in heads for v in layer))
    for l in range(3):
        aquifer_next[8 * l : 8 * l + 8, :] = jnp.concatenate(
            [flat[3 * l][8:12], flat[3 * l + 1][8:12]], axis=0
        )

    lanes = iota((128, 128), 0).astype(F32)
    cell_rows = iota((32, 128), 0).astype(F32)

    def scatter(which, result):
        some = rows[pl.ds(pl.multiple_of(which * (wide_count // 2), 64), 64), :]
        slot_lines[...] = jnp.concatenate([some, roll(some, 64, 1)], axis=0).T
        pairs = range(CAP // 2)
        target = jnp.concatenate(
            [
                (lanes == slot_lines[32 * k + 17 : 32 * k + 18, :]).astype(F32).astype(BF16)
                for k in pairs
            ],
            axis=1,
        )
        hits = [cell_rows == slot_lines[32 * k + 16 : 32 * k + 17, :] for k in pairs]
        for i in range(4):
            for layer in range(4):
                for k in pairs:
                    line = 32 * k + 4 * i + layer
                    value = jnp.broadcast_to(slot_lines[line : line + 1, :], (32, 128))
                    value = jnp.where(hits[k], value, 0.0)
                    high = value.astype(BF16)
                    low = (value - high.astype(F32)).astype(BF16)
                    at = pl.ds(128 * k, 128)
                    spread[i, 32 * layer : 32 * layer + 32, at] = high
                    spread[i, 32 * layer + 128 : 32 * layer + 160, at] = low
            taken = lax.dot_general(spread[i], target, NT, preferred_element_type=F32)
            at = pl.ds(128 * i, 128)
            result[at, :] = part[at, :] - (taken[:128] + taken[128:]) * rest[at, :]

    mine = my_z // half
    pl.when(my_z < depth // 4)(lambda: answer(0, half))
    lax.fori_loop(mine * half, my_z, await_plane, 0)
    scatter(mine, part)
    pl.when(my_z < depth // 4)(lambda: answer(half, depth))
    lax.fori_loop(0, mine * half, await_plane, 0)
    scatter(1 - mine, out)

    for copy in slab_copies:
        copy.wait_send()
    for copy, step in zip(patch_copies + face_copies, around + (1, -1)):
        pl.when(exists(step))(copy.wait_send)
    each_drain(lambda copy: copy.wait_send())
    for copy in plane_copies:
        copy.wait_send()

    def left_plane(z, carry):
        rows_from(PEERS, 0).wait_send()
        return carry

    def left_answer(z, carry):
        remote(*rows_to(0), answers_sent.at[0], rows_got.at[0], w, n).wait_send()
        return carry

    lax.fori_loop(0, my_z, left_plane, 0)
    lax.fori_loop(my_z + 1, depth, left_answer, 0)


def store(head_next, aquifer_next, head_out, aquifer_out, done):
    copies = [pltpu.make_async_copy(aquifer_next, aquifer_out, done.at[4])]
    for i in range(4):
        at = pl.ds(128 * i, 128)
        copies.append(pltpu.make_async_copy(head_next.at[at], head_out.at[at], done.at[i]))
    for copy in copies:
        copy.start()
    for copy in copies:
        copy.wait()


def rows_of(a):
    k = a.shape[0]
    return a.reshape(k, 4, 8, 128).transpose(0, 2, 1, 3).reshape(k * 32, 128)


def grid_of(a, k, columns):
    return a.reshape(k, columns // 128, 4, 128).transpose(0, 2, 1, 3).reshape(k, 4, columns)


def body(
    pressure_head,
    texture,
    saturated_table,
    shape_table,
    capacity_table,
    uptake,
    root_tile,
    root_column,
    aquifer_head,
    transmissivity,
):
    wide_count = lax.axis_size("wide")
    narrow_count = lax.axis_size("narrow")
    depth = wide_count // PEERS
    dma = pltpu.SemaphoreType.DMA
    hbm, vmem = pl.BlockSpec(memory_space=pltpu.HBM), pl.BlockSpec(memory_space=pltpu.VMEM)
    head_next, aquifer_next = pl.pallas_call(
        functools.partial(kernel, wide_count, narrow_count),
        out_shape=(
            pltpu.VMEM((512, 128), F32),
            pltpu.VMEM((24, 128), F32),
        ),
        in_specs=[hbm] * 10,
        out_specs=[vmem] * 2,
        scratch_shapes=[
            pltpu.VMEM((512, 128), F32),
            pltpu.VMEM((512, 128), I32),
            pltpu.VMEM((1, 12), F32),
            pltpu.VMEM((1, 12), F32),
            pltpu.VMEM((1, 12), F32),
            pltpu.VMEM((16, 256), F32),
            pltpu.VMEM((1, 256), I32),
            pltpu.VMEM((1, 256), I32),
            pltpu.VMEM((96, 128), F32),
            pltpu.VMEM((96, 128), F32),
            pltpu.VMEM((24, 128), F32),
            pltpu.VMEM((2, 512, 128), F32),
            pltpu.VMEM((wide_count, 128), F32),
            pltpu.VMEM((512, 128), F32),
            pltpu.VMEM((512, 128), F32),
            pltpu.VMEM((4, 256, 256), BF16),
            pltpu.VMEM((128, 128), F32),
            pltpu.VMEM((2, 2, 128, 128), F32),
            pltpu.VMEM((2, 2, 128, 128), F32),
            pltpu.VMEM((2, 2, 32, 128), F32),
            pltpu.VMEM((wide_count, 128), F32),
            pltpu.VMEM((PEERS, depth, 128), F32),
            pltpu.VMEM((PEERS, depth, 128), F32),
            pltpu.VMEM((depth, PEERS, 128), F32),
            pltpu.VMEM((18, 4, 128), F32),
            pltpu.VMEM((18, 6, 4, 128), F32),
            pltpu.VMEM((4, 3, 4, 128), F32),
            pltpu.VMEM((3, 6, 4, 128), F32),
            pltpu.VMEM((6, 9, 24, 128), F32),
            dma((10,)),
            dma((1,)),
            dma((depth,)),
            dma((1,)),
            dma((PEERS - 1,)),
            dma((PEERS - 1,)),
            dma((4,)),
            dma((4,)),
            dma((5, 4)),
            dma((5,)),
            dma((2,)),
            dma((2,)),
            dma((2,)),
            dma((2,)),
        ],
        compiler_params=pltpu.CompilerParams(
            collective_id=0, has_side_effects=True, vmem_limit_bytes=VMEM_GRANT
        ),
        name="coupled_step",
    )(
        *(
            pltpu.with_memory_space_constraint(a, pltpu.HBM)
            for a in (
                rows_of(pressure_head),
                rows_of(texture),
                saturated_table.reshape(1, -1),
                shape_table.reshape(1, -1),
                capacity_table.reshape(1, -1),
                uptake.T,
                root_tile.reshape(1, -1),
                root_column.reshape(1, -1),
                rows_of(aquifer_head),
                rows_of(transmissivity),
            )
        )
    )
    out, aquifer_out = pl.pallas_call(
        store,
        out_shape=(
            jax.ShapeDtypeStruct((512, 128), F32),
            jax.ShapeDtypeStruct((24, 128), F32),
        ),
        in_specs=[vmem] * 2,
        out_specs=[hbm] * 2,
        scratch_shapes=[dma((5,))],
        compiler_params=pltpu.CompilerParams(vmem_limit_bytes=VMEM_GRANT),
        name="finish_step",
    )(head_next, aquifer_next)
    return grid_of(out, 16, 1024), grid_of(aquifer_out, 3, 256)


def solution(mesh):
    in_specs = (
        P("narrow", "wide", None),
        P("narrow", "wide", None),
        P(),
        P(),
        P(),
        P("wide", "narrow"),
        P("wide", None),
        P("wide"),
        P(None, "wide", None),
        P(None, "wide", None),
    )
    out_specs = (P("narrow", "wide", None), P(None, "wide", "narrow"))
    return jax.shard_map(body, mesh=mesh, in_specs=in_specs, out_specs=out_specs, check_vma=False)
```

```python
import functools

import jax
import jax.numpy as jnp
from jax import lax
from jax.experimental import pallas as pl
from jax.experimental.pallas import tpu as pltpu
from jax.sharding import PartitionSpec as P

SWEEPS = 8
TIME_STEP = 0.25
STORAGE = 0.05
LEAKANCE = 0.5
PEERS = 8
CAP = 4
VMEM_GRANT = 32 * 1024 * 1024
F32, BF16, I32 = jnp.float32, jnp.bfloat16, jnp.int32
MESH = pl.DeviceIdType.MESH
NT = (((1,), (1,)), ((), ()))


def roll(x, shift, axis):
    return pltpu.roll(x, shift % x.shape[axis], axis)


def iota(shape, axis):
    return lax.broadcasted_iota(I32, shape, axis)


def remote(src, dst, send_sem, recv_sem, wide, narrow):
    return pltpu.make_async_remote_copy(
        src_ref=src,
        dst_ref=dst,
        send_sem=send_sem,
        recv_sem=recv_sem,
        device_id=(wide, narrow),
        device_id_type=MESH,
    )


def root_slots(uptake, tile, column):
    cell_row = ((column // 128) % 8) * 4 + column // 1024
    cell_lane = column % 128
    count = tile.shape[1]
    aimed = iota((128, count), 0) == tile
    earlier = iota((count, count), 0) < iota((count, count), 1)
    rank = jnp.dot(
        aimed.astype(F32).astype(BF16),
        earlier.astype(F32).astype(BF16),
        preferred_element_type=F32,
    )
    picks = jnp.concatenate(
        [(aimed & (rank == float(k))).astype(F32).astype(BF16) for k in range(CAP)], axis=0
    )
    high = uptake.astype(BF16)
    low = (uptake - high.astype(F32)).astype(BF16)
    line = iota((16, count), 0)
    extra = jnp.where(
        line == 0,
        cell_row.astype(F32),
        jnp.where(line == 1, cell_lane.astype(F32), 0.0),
    ).astype(BF16)
    base = jnp.concatenate([high, extra, low, jnp.zeros_like(extra)], axis=0)
    spread = lax.dot_general(base, picks, NT, preferred_element_type=F32)
    rows = spread[:32] + spread[32:]
    slots = jnp.concatenate([rows[:, 128 * k : 128 * (k + 1)] for k in range(CAP)], axis=0)
    return slots.T


def ring_left(tiles, lane):
    moved = [roll(v, 1, 1) for v in tiles]
    return [jnp.where(lane == 0, moved[t - 1], moved[t]) for t in range(len(tiles))]


def ring_right(tiles, lane):
    moved = [roll(v, -1, 1) for v in tiles]
    return [
        jnp.where(lane == 127, moved[(t + 1) % len(tiles)], moved[t]) for t in range(len(tiles))
    ]


def kernel(
    wide_count,
    narrow_count,
    head_hbm,
    texture_hbm,
    saturated_hbm,
    shape_hbm,
    capacity_hbm,
    uptake_hbm,
    tile_hbm,
    column_hbm,
    aquifer_hbm,
    trans_hbm,
    out,
    aquifer_next,
    head_ref,
    texture_ref,
    saturated_ref,
    shape_ref,
    capacity_ref,
    uptake_ref,
    tile_ref,
    column_ref,
    aquifer_ref,
    trans_ref,
    table,
    soil,
    rows,
    part,
    rest,
    spread,
    slot_lines,
    face_out,
    face_in,
    slab_in,
    slots,
    by_peer,
    plane_rows,
    by_plane,
    patch,
    patches,
    drain,
    drains,
    coef,
    load_done,
    rows_sent,
    rows_got,
    answers_sent,
    plane_sent,
    plane_got,
    patch_sent,
    patch_got,
    drain_sent,
    drain_got,
    face_sent,
    face_got,
    slab_sent,
    slab_got,
):
    w = lax.axis_index("wide")
    n = lax.axis_index("narrow")
    depth = wide_count // PEERS
    my_z, my_peer = w // PEERS, w % PEERS
    bottom = n == narrow_count - 1
    around = (-2, -1, 1, 2)

    def exists(step):
        return (w + step >= 0) & (w + step < wide_count)

    barrier = pltpu.get_barrier_semaphore()

    def greet(wide, narrow):
        pl.semaphore_signal(barrier, inc=1, device_id=(wide, narrow), device_id_type=MESH)

    peers = [(my_peer + j) % PEERS for j in range(1, PEERS + 1)]

    def plane_at(k):
        return (my_z + depth // 2 + ((k + 1) // 2) * (1 - 2 * (k % 2)) + depth) % depth

    def greet_plane(k, carry):
        z = plane_at(k)

        @pl.when(z > my_z)
        def _():
            for peer in peers:
                greet(z * PEERS + peer, n)

        return carry

    for peer in peers[:-1]:
        greet(my_z * PEERS + peer, n)
    greeted = PEERS * my_z + PEERS - 1 + 2
    for step in around:
        plane = (w + step + PEERS) // PEERS - 1
        greeted = greeted + jnp.where(exists(step) & (plane > my_z), 1, 0)

        @pl.when(exists(step) & (plane < my_z))
        def _(step=step):
            greet(w + step, n)

    greet(w, (n + 1) % narrow_count)
    greet(w, (n + narrow_count - 1) % narrow_count)

    for step in (-2, -1, 0, 1, 2):

        @pl.when(jnp.logical_not(bottom) & exists(step))
        def _(step=step):
            greet(w + step, narrow_count - 1)

    lax.fori_loop(0, depth - 1, greet_plane, 0)

    order = (6, 7, 5, 0, 1, 2, 3, 4, 8, 9)
    held = (head_ref, texture_ref, saturated_ref, shape_ref, capacity_ref, uptake_ref, tile_ref)
    held += (column_ref, aquifer_ref, trans_ref)
    far = (head_hbm, texture_hbm, saturated_hbm, shape_hbm, capacity_hbm, uptake_hbm, tile_hbm)
    far += (column_hbm, aquifer_hbm, trans_hbm)
    loads = [pltpu.make_async_copy(far[i], held[i], load_done.at[i]) for i in range(10)]
    for i in order:
        loads[i].start()
    for i in (6, 7, 5):
        loads[i].wait()

    made = root_slots(
        uptake_ref[...],
        tile_ref[...],
        column_ref[...],
    )
    slots[...] = made
    for z in range(depth):
        for p in range(PEERS):
            by_peer[p, z : z + 1] = slots[z * PEERS + p : z * PEERS + p + 1]

    near_tiles = sum(jnp.where(exists(step), 1, 0) for step in (-2, -1, 0, 1, 2))
    greeted = greeted + jnp.where(bottom, (narrow_count - 1) * near_tiles, 0)
    pl.semaphore_wait(barrier, greeted)

    def send_rows(tile):
        remote(
            slots.at[pl.ds(tile, 1)], rows.at[pl.ds(w, 1)], rows_sent.at[0], rows_got.at[my_z], tile, n
        ).start()

    def rows_from(count, z):
        at = rows.at[pl.ds(0, count)]
        return remote(at, at, rows_sent.at[0], rows_got.at[z], w, n)

    def send_plane(k, carry):
        z = plane_at(k)

        @pl.when(z < my_z)
        def _():
            for core in (0, 1):
                for j in range(1, PEERS // 2 + 1):
                    send_rows(z * PEERS + (2 * (my_peer // 2) + 2 * j) % PEERS + core)

        return carry

    lax.fori_loop(0, depth - 1, send_plane, 0)

    plane_copies = [
        remote(
            by_peer.at[peer],
            plane_rows.at[my_peer],
            plane_sent.at[j],
            plane_got.at[j],
            my_z * PEERS + peer,
            n,
        )
        for j, peer in enumerate(peers[:-1])
    ]
    for copy in plane_copies:
        copy.start()

    def rows_to(z):
        return (by_plane.at[z], rows.at[pl.ds(my_z * PEERS, PEERS)])

    def answer_plane(z, carry):
        rows_from(PEERS, z).wait_recv()
        to = z * PEERS + my_peer
        remote(*rows_to(z), answers_sent.at[0], rows_got.at[my_z], to, n).start()
        return carry

    def await_plane(z, carry):
        rows_from(PEERS, z).wait_recv()
        return carry

    for i in (8, 9):
        loads[i].wait()
    lane4 = iota((4, 128), 1)
    for a in range(6):
        source = aquifer_ref if a < 3 else trans_ref
        first = (a % 3) * 32
        here = source[pl.ds(pl.multiple_of(first + 8 * n, 8), 8), :]
        after = source[pl.ds(pl.multiple_of(first + 8 * jnp.minimum(n + 1, 3), 8), 8), :]
        before = source[pl.ds(pl.multiple_of(first + 8 * jnp.maximum(n - 1, 0), 8), 8), :]
        after = jnp.where(n < narrow_count - 1, after[0:4], 0.0)
        before = jnp.where(n > 0, before[4:8], 0.0)
        patch[3 * a] = here[0:4]
        patch[3 * a + 1] = here[4:8]
        patch[3 * a + 2] = jnp.where(lane4 < 64, after, before)
    for a in range(18):
        patches[a, 2] = patch[a]
        patches[a, 5] = jnp.zeros((4, 128), F32)
    for t in range(3):
        drains[t, 5] = jnp.zeros((4, 128), F32)

    for i in (0, 1, 2, 3, 4):
        loads[i].wait()
    table[...] = jnp.zeros_like(table)
    table[0:1, 0:12] = saturated_ref[...]
    table[8:9, 0:12] = shape_ref[...]
    table[16:17, 0:12] = capacity_ref[...]

    def look_up(row, index):
        values = jnp.broadcast_to(table[row : row + 1, :], index.shape)
        return jnp.take_along_axis(values, index, axis=1, mode="promise_in_bounds")

    def conduct_layer(z, carry):
        here = pl.ds(pl.multiple_of(z * 32, 32), 32)
        head = head_ref[here, :]
        index = texture_ref[here, :]
        soil[0, here, :] = head
        soil[1, here, :] = look_up(0, index) * jnp.exp(look_up(8, index) * jnp.minimum(head, 0.0))
        rest[here, :] = TIME_STEP / look_up(16, index)
        return carry

    lax.fori_loop(0, 16, conduct_layer, 0, unroll=4)

    for i, first in ((0, 3), (1, 0)):
        for v in range(2):
            face_out[i, v] = soil[v, pl.ds(first, 128, stride=4), :]
    @pl.when(bottom)
    def _():
        flow = soil[1, 480:512, :] * (soil[0, 480:512, :] - aquifer_ref[0:32, :] + 1.0)
        for q in range(4):
            drain[q, 0] = flow[8 * q : 8 * q + 4]
            drain[q, 1] = flow[8 * q + 4 : 8 * q + 8]
            after = flow[8 * q + 8 : 8 * q + 12] if q < 3 else jnp.zeros((4, 128), F32)
            before = flow[8 * q - 4 : 8 * q] if q > 0 else jnp.zeros((4, 128), F32)
            drain[q, 2] = jnp.where(lane4 < 64, after, before)
        drains[:, 2] = drain[3]

    face_copies = [
        remote(face_out.at[i], face_in.at[i], face_sent.at[i], face_got.at[i], w + step, n)
        for i, step in ((0, 1), (1, -1))
    ]
    for copy, step in zip(face_copies, (1, -1)):
        pl.when(exists(step))(copy.start)
    slab_copies = [
        remote(
            soil.at[:, pl.ds(first, 32)],
            slab_in.at[i],
            slab_sent.at[i],
            slab_got.at[i],
            w,
            (n + step) % narrow_count,
        )
        for i, first, step in ((0, 480, 1), (1, 0, narrow_count - 1))
    ]
    for copy in slab_copies:
        copy.start()
    patch_copies = [
        remote(patch, patches.at[:, 2 - step], patch_sent.at[i], patch_got.at[i], w + step, n)
        for i, step in enumerate(around)
    ]
    for copy, step in zip(patch_copies, around):
        pl.when(exists(step))(copy.start)

    def drain_copy(step, q):
        return remote(
            drain.at[q],
            drains.at[:, 2 - step],
            drain_sent.at[step + 2, q],
            drain_got.at[2 - step],
            w + step,
            q,
        )

    def each_drain(act):
        for step in (0, 1, -1, 2, -2):

            @pl.when(bottom & exists(step))
            def _(step=step):
                for q in range(narrow_count - 1 if step == 0 else narrow_count):
                    act(drain_copy(step, q))

    each_drain(lambda copy: copy.start())

    half = depth // 2

    def answer(low, high):
        lax.fori_loop(jnp.maximum(my_z + 1, low), high, answer_plane, 0)

    def regroup():
        for copy in plane_copies:
            copy.wait_recv()
        plane_rows[my_peer] = by_peer[my_peer]
        for z in range(depth):
            for p in range(PEERS):
                by_plane[z, p : p + 1] = plane_rows[p, z : z + 1]
        rows[pl.ds(pl.multiple_of(my_z * PEERS, PEERS), PEERS), :] = by_plane[my_z]

    row = iota((32, 128), 0)
    lane = iota((32, 128), 1)
    across_open = jnp.where(row % 4 == 0, 0.0, 0.5)
    along_open = jnp.where((lane == 0) & (row < 4), 0.0, 0.5)

    def previous_column(v):
        moved = roll(v, 1, 1)
        return jnp.where(lane == 0, roll(moved, 4, 0), moved)

    def layer(z):
        at = pl.ds(pl.multiple_of(z * 32, 32), 32)
        return soil[0, at, :], soil[1, at, :]

    def sides(head, cond):
        across = across_open * (roll(cond, 1, 0) + cond) * (roll(head, 1, 0) - head)
        along = along_open * (previous_column(cond) + cond) * (previous_column(head) - head)
        moved = roll(along, -1, 1)
        along_out = jnp.where(lane == 127, roll(moved, -4, 0), moved)
        return (across - roll(across, -1, 0)) + (along - along_out)

    def balance_layer(z, vertical_in):
        head, cond = layer(z)
        head_under, cond_under = layer(z + 1)
        vertical_out = 0.5 * (cond + cond_under) * (head - head_under + 1.0)
        at = pl.ds(pl.multiple_of(z * 32, 32), 32)
        balance = (vertical_in - vertical_out) + sides(head, cond)
        part[at, :] = head + balance * rest[at, :]
        return vertical_out

    vertical_in = lax.fori_loop(0, 15, balance_layer, jnp.zeros((32, 128), F32), unroll=5)
    head, cond = layer(15)
    part[480:512, :] = head + (vertical_in + sides(head, cond)) * rest[480:512, :]

    regroup()
    pl.when(my_z >= depth // 4)(lambda: answer(0, depth))

    for copy in slab_copies:
        copy.wait_recv()
    for copy, step in zip(face_copies, (1, -1)):
        pl.when(exists(-step))(copy.wait_recv)
    head_under = jnp.where(bottom, aquifer_ref[0:32, :], slab_in[1, 0])
    cond_under = jnp.where(bottom, cond, slab_in[1, 1])
    vertical_out = 0.5 * (cond + cond_under) * (head - head_under + 1.0)
    part[480:512, :] = part[480:512, :] - vertical_out * rest[480:512, :]
    head, cond = layer(0)
    top_open = jnp.where(n == 0, 0.0, 0.5)
    vertical_in = top_open * (slab_in[0, 1] + cond) * (slab_in[0, 0] - head + 1.0)
    part[0:32, :] = part[0:32, :] + vertical_in * rest[0:32, :]
    for side, first, factor, is_open in ((0, 0, 0.5, exists(-1)), (1, 3, -0.5, exists(1))):
        head, cond = face_out[1 - side, 0], face_out[1 - side, 1]
        other_head, other_cond = face_in[side, 0], face_in[side, 1]
        jump = other_head - head if side == 0 else head - other_head
        at = pl.ds(first, 128, stride=4)
        flow = jnp.where(is_open, factor * (cond + other_cond) * jump, 0.0)
        part[at, :] = part[at, :] + flow * rest[at, :]

    for copy, step in zip(patch_copies, around):
        pl.when(exists(-step))(copy.wait_recv)
    for step in (-2, -1, 0, 1, 2):
        needed = exists(-step) & jnp.logical_not(bottom) if step == 0 else exists(-step)
        pl.when(needed)(drain_copy(step, 0).wait_recv)

    lane24 = iota((24, 128), 1)
    line = iota((24, 128), 0) + 4 * w - 8
    real = (line >= 0) & (line < 4 * wide_count)
    inside = jnp.where(real, 1.0, 0.0)
    after_open = jnp.where(n < narrow_count - 1, 1.0, 0.0)
    before_open = jnp.where(n > 0, 1.0, 0.0)
    inside_halo = inside * jnp.where(lane24 < 64, after_open, before_open)

    def stacked(ref, a):
        return jnp.where(real, jnp.concatenate([ref[a, s] for s in range(6)], axis=0), 0.0)

    heads = [[stacked(patches, 3 * l + t) for t in range(3)] for l in range(3)]
    flows = [stacked(drains, t) for t in range(3)]
    for l in range(3):
        trans = [stacked(patches, 9 + 3 * l + t) for t in range(3)]
        wests, easts = ring_left(trans, lane24), ring_right(trans, lane24)
        for t in range(3):
            centre = trans[t]
            north = 0.5 * (centre + roll(centre, 1, 0))
            south = 0.5 * (centre + roll(centre, -1, 0))
            west = 0.5 * (centre + wests[t])
            east = 0.5 * (centre + easts[t])
            links = 2.0 if l == 1 else 1.0
            divisor = STORAGE + north + south + west + east + LEAKANCE * links
            inverse = (inside_halo if t == 2 else inside) / divisor
            source = STORAGE * heads[l][t]
            if l == 0:
                source = source + flows[t]
            k = 3 * l + t
            coef[0, k] = north * inverse
            coef[1, k] = south * inverse
            coef[2, k] = west * inverse
            coef[3, k] = east * inverse
            coef[4, k] = LEAKANCE * inverse
            coef[5, k] = source * inverse

    def sweep(_, flat):
        now = [flat[3 * l : 3 * l + 3] for l in range(3)]
        later = []
        for l in range(3):
            wests, easts = ring_left(now[l], lane24), ring_right(now[l], lane24)
            for t in range(3):
                k = 3 * l + t
                centre = now[l][t]
                if l == 1:
                    vertical = now[0][t] + now[2][t]
                else:
                    vertical = now[1][t]
                later.append(
                    coef[5, k]
                    + coef[0, k] * roll(centre, 1, 0)
                    + coef[1, k] * roll(centre, -1, 0)
                    + coef[2, k] * wests[t]
                    + coef[3, k] * easts[t]
                    + coef[4, k] * vertical
                )
        return tuple(later)

    flat = lax.fori_loop(0, SWEEPS, sweep, tuple(v for layer in heads for v in layer))
    for l in range(3):
        aquifer_next[8 * l : 8 * l + 8, :] = jnp.concatenate(
            [flat[3 * l][8:12], flat[3 * l + 1][8:12]], axis=0
        )

    lanes = iota((128, 128), 0).astype(F32)
    cell_rows = iota((32, 128), 0).astype(F32)

    def scatter(which, result):
        some = rows[pl.ds(pl.multiple_of(which * (wide_count // 2), 64), 64), :]
        slot_lines[...] = jnp.concatenate([some, roll(some, 64, 1)], axis=0).T
        pairs = range(CAP // 2)
        target = jnp.concatenate(
            [
                (lanes == slot_lines[32 * k + 17 : 32 * k + 18, :]).astype(F32).astype(BF16)
                for k in pairs
            ],
            axis=1,
        )
        hits = [cell_rows == slot_lines[32 * k + 16 : 32 * k + 17, :] for k in pairs]
        for i in range(4):
            for layer in range(4):
                for k in pairs:
                    line = 32 * k + 4 * i + layer
                    value = jnp.broadcast_to(slot_lines[line : line + 1, :], (32, 128))
                    value = jnp.where(hits[k], value, 0.0)
                    high = value.astype(BF16)
                    low = (value - high.astype(F32)).astype(BF16)
                    at = pl.ds(128 * k, 128)
                    spread[i, 32 * layer : 32 * layer + 32, at] = high
                    spread[i, 32 * layer + 128 : 32 * layer + 160, at] = low
            taken = lax.dot_general(spread[i], target, NT, preferred_element_type=F32)
            at = pl.ds(128 * i, 128)
            result[at, :] = part[at, :] - (taken[:128] + taken[128:]) * rest[at, :]

    mine = my_z // half
    pl.when(my_z < depth // 4)(lambda: answer(0, half))
    lax.fori_loop(mine * half, my_z, await_plane, 0)
    scatter(mine, part)
    pl.when(my_z < depth // 4)(lambda: answer(half, depth))
    lax.fori_loop(0, mine * half, await_plane, 0)
    scatter(1 - mine, out)

    for copy in slab_copies:
        copy.wait_send()
    for copy, step in zip(patch_copies + face_copies, around + (1, -1)):
        pl.when(exists(step))(copy.wait_send)
    each_drain(lambda copy: copy.wait_send())
    for copy in plane_copies:
        copy.wait_send()

    def left_plane(z, carry):
        rows_from(PEERS, 0).wait_send()
        return carry

    def left_answer(z, carry):
        remote(*rows_to(0), answers_sent.at[0], rows_got.at[0], w, n).wait_send()
        return carry

    lax.fori_loop(0, my_z, left_plane, 0)
    lax.fori_loop(my_z + 1, depth, left_answer, 0)


def store(head_next, aquifer_next, head_out, aquifer_out, done):
    copies = [pltpu.make_async_copy(aquifer_next, aquifer_out, done.at[4])]
    for i in range(4):
        at = pl.ds(128 * i, 128)
        copies.append(pltpu.make_async_copy(head_next.at[at], head_out.at[at], done.at[i]))
    for copy in copies:
        copy.start()
    for copy in copies:
        copy.wait()


def rows_of(a):
    k = a.shape[0]
    return a.reshape(k, 4, 8, 128).transpose(0, 2, 1, 3).reshape(k * 32, 128)


def grid_of(a, k, columns):
    return a.reshape(k, columns // 128, 4, 128).transpose(0, 2, 1, 3).reshape(k, 4, columns)


def body(
    pressure_head,
    texture,
    saturated_table,
    shape_table,
    capacity_table,
    uptake,
    root_tile,
    root_column,
    aquifer_head,
    transmissivity,
):
    wide_count = lax.axis_size("wide")
    narrow_count = lax.axis_size("narrow")
    depth = wide_count // PEERS
    dma = pltpu.SemaphoreType.DMA
    hbm, vmem = pl.BlockSpec(memory_space=pltpu.HBM), pl.BlockSpec(memory_space=pltpu.VMEM)
    head_next, aquifer_next = pl.pallas_call(
        functools.partial(kernel, wide_count, narrow_count),
        out_shape=(
            pltpu.VMEM((512, 128), F32),
            pltpu.VMEM((24, 128), F32),
        ),
        in_specs=[hbm] * 10,
        out_specs=[vmem] * 2,
        scratch_shapes=[
            pltpu.VMEM((512, 128), F32),
            pltpu.VMEM((512, 128), I32),
            pltpu.VMEM((1, 12), F32),
            pltpu.VMEM((1, 12), F32),
            pltpu.VMEM((1, 12), F32),
            pltpu.VMEM((16, 256), F32),
            pltpu.VMEM((1, 256), I32),
            pltpu.VMEM((1, 256), I32),
            pltpu.VMEM((96, 128), F32),
            pltpu.VMEM((96, 128), F32),
            pltpu.VMEM((24, 128), F32),
            pltpu.VMEM((2, 512, 128), F32),
            pltpu.VMEM((wide_count, 128), F32),
            pltpu.VMEM((512, 128), F32),
            pltpu.VMEM((512, 128), F32),
            pltpu.VMEM((4, 256, 256), BF16),
            pltpu.VMEM((128, 128), F32),
            pltpu.VMEM((2, 2, 128, 128), F32),
            pltpu.VMEM((2, 2, 128, 128), F32),
            pltpu.VMEM((2, 2, 32, 128), F32),
            pltpu.VMEM((wide_count, 128), F32),
            pltpu.VMEM((PEERS, depth, 128), F32),
            pltpu.VMEM((PEERS, depth, 128), F32),
            pltpu.VMEM((depth, PEERS, 128), F32),
            pltpu.VMEM((18, 4, 128), F32),
            pltpu.VMEM((18, 6, 4, 128), F32),
            pltpu.VMEM((4, 3, 4, 128), F32),
            pltpu.VMEM((3, 6, 4, 128), F32),
            pltpu.VMEM((6, 9, 24, 128), F32),
            dma((10,)),
            dma((1,)),
            dma((depth,)),
            dma((1,)),
            dma((PEERS - 1,)),
            dma((PEERS - 1,)),
            dma((4,)),
            dma((4,)),
            dma((5, 4)),
            dma((5,)),
            dma((2,)),
            dma((2,)),
            dma((2,)),
            dma((2,)),
        ],
        compiler_params=pltpu.CompilerParams(
            collective_id=0, has_side_effects=True, vmem_limit_bytes=VMEM_GRANT
        ),
        name="coupled_step",
    )(
        *(
            pltpu.with_memory_space_constraint(a, pltpu.HBM)
            for a in (
                rows_of(pressure_head),
                rows_of(texture),
                saturated_table.reshape(1, -1),
                shape_table.reshape(1, -1),
                capacity_table.reshape(1, -1),
                uptake.T,
                root_tile.reshape(1, -1),
                root_column.reshape(1, -1),
                rows_of(aquifer_head),
                rows_of(transmissivity),
            )
        )
    )
    out, aquifer_out = pl.pallas_call(
        store,
        out_shape=(
            jax.ShapeDtypeStruct((512, 128), F32),
            jax.ShapeDtypeStruct((24, 128), F32),
        ),
        in_specs=[vmem] * 2,
        out_specs=[hbm] * 2,
        scratch_shapes=[dma((5,))],
        compiler_params=pltpu.CompilerParams(vmem_limit_bytes=VMEM_GRANT),
        name="finish_step",
    )(head_next, aquifer_next)
    return grid_of(out, 16, 1024), grid_of(aquifer_out, 3, 256)


def solution(mesh):
    in_specs = (
        P("narrow", "wide", None),
        P("narrow", "wide", None),
        P(),
        P(),
        P(),
        P("wide", "narrow"),
        P("wide", None),
        P("wide"),
        P(None, "wide", None),
        P(None, "wide", None),
    )
    out_specs = (P("narrow", "wide", None), P(None, "wide", "narrow"))
    return jax.shard_map(body, mesh=mesh, in_specs=in_specs, out_specs=out_specs, check_vma=False)
```
